32 devices in a mesh: row: 8 (over y, x, core), col: 4 (over z).
Axes of the slice: x: 2, y: 2, z: 4, core: 2. Of those that a mesh axis runs over, the one named last changes fastest.
Arguments:
- nodes: bfloat16 [128, 512], P(('row', 'col')), may hold values from -50 to 50
- coords: float32 [3, 128], P(None, ('row', 'col')), may hold values from -18 to 18
- atom_types: int32 [128], P(('row', 'col')), may hold values from 0 to 29
- segment_ids: int32 [128], P(('row', 'col')), may hold values from 0 to 1
- pair_mask: int32 [128, 128], P('row', 'col'), may hold values 0 or 1
- pair_bias: bfloat16 [64, 128, 128], P(None, 'row', 'col'), may hold values from -10 to 310
- ln_gain: float32 [512], replicated, may hold values from 0.1 to 1.9
- w_qkv: bfloat16 [512, 1536], replicated, may hold values from -0.25 to 0.25
- gauss_mul: float32 [60, 60], replicated, may hold values from 0.25 to 1.75
- gauss_add: float32 [60, 60], replicated, may hold values from -4 to 4
- gauss_mean: float32 [128], replicated, may hold values from 0 to 16
- gauss_width: float32 [128], replicated, may hold values from 0.5 to 2.5
- w_gauss: bfloat16 [128, 128], replicated, may hold values from -2 to 2
- w_heads: bfloat16 [128, 64], replicated, may hold values from -2 to 2
- w_coord1: bfloat16 [64, 64], replicated, may hold values from -0.75 to 0.75
- w_coord2: bfloat16 [64], replicated, may hold values from -0.75 to 0.75
Outputs:
- attended: bfloat16 [128, 512], P(('row', 'col'))
- moved: float32 [3, 128], P(None, ('row', 'col'))
The draws below stay inside these ranges and needn't reach their ends.
All inputs are finite; a program needn't handle non-finite values. No bound on the sum of `pair_mask` on one device may be relied on, other than what follows from the above.
Results may differ from the reference program's by a relative error of at most 0.015.
Values may be sent and summed in bfloat16 or wider, within the bound.
No kernel may reach another device: no remote copies, remote signals or barrier semaphores. Data moves between devices by JAX's collectives and lax.ppermute only.
A program may use at most 64 MiB of HBM per device.

```python
import math
import jax
import jax.numpy as jnp
from jax import lax

D = 512
HEADS = 64
GAUSS = 128
ATOM_TYPES = 30
KINDS = 60
ATOMS = 128
N_ROW = 8


def draw_nodes(key, part):
    base_key = jax.random.fold_in(key, 11)
    column_key = jax.random.fold_in(key, 12)
    row_key = jax.random.fold_in(key, 13)
    column_scale = jnp.exp(jax.random.uniform(column_key, (1, D), jnp.float32, -1.15, 1.15))
    row_scale = jnp.exp(jax.random.uniform(row_key, (ATOMS, 1), jnp.float32, -1.15, 1.15))
    values = jnp.clip(jax.random.normal(base_key, (ATOMS, D), jnp.float32), -5.0, 5.0)
    return (values * column_scale * row_scale).astype(jnp.bfloat16)


def draw_pair_bias(key, part):
    base_key = jax.random.fold_in(key, 21)
    full_shape = (HEADS, ATOMS, ATOMS)
    values = jnp.clip(jax.random.normal(base_key, full_shape, jnp.float32) * 2.0, -10.0, 10.0)
    return values.astype(jnp.bfloat16)


def plant(result, key, least, top_value):
    index_at = [jax.random.randint(jax.random.fold_in(key, axis), (), 0, length) for axis, length in enumerate(result.shape)]
    widest = result.shape.index(max(result.shape))
    neighbour = index_at[:widest] + [(index_at[widest] + 1) % result.shape[widest]] + index_at[widest + 1:]
    return result.at[tuple(index_at)].set(least).at[tuple(neighbour)].set(top_value)


def block_levels(rng, shape, pieces, least, largest):
    gain, own = 1.0, jax.random.fold_in(rng, 6)
    for axis_at, shards_of in pieces:
        draws = jnp.exp(jax.random.uniform(jax.random.fold_in(own, axis_at), (shards_of,), jnp.float32, least / len(pieces), largest / len(pieces)))
        gain = gain * jnp.repeat(draws, shape[axis_at] // shards_of).reshape([-1 if axis == axis_at else 1 for axis in range(len(shape))])
    return gain


def noise(own_key, dims, width, reach, split=(), kind=jnp.bfloat16):
    drawn = jax.random.normal(own_key, dims, jnp.float32) * width
    if len(split) > 0:
        drawn = block_levels(own_key, dims, split, -0.22, 0.18) * drawn
    return jnp.clip(drawn, min=-reach, max=reach).astype(kind)


def setup_inputs(seed: int = 0) -> dict:
    keys = jax.random.split(jax.random.key(seed), 17)
    return {
        "nodes": draw_nodes(jax.random.fold_in(keys[16], 71), 0),
        "coords": noise(keys[1], (3, ATOMS), 3.0, 18.0, ((1, 32),), jnp.float32),
        "atom_types": plant(jax.random.randint(keys[2], (ATOMS,), 0, ATOM_TYPES), jax.random.fold_in(keys[2], 1), 0, ATOM_TYPES - 1).astype(jnp.int32),
        "segment_ids": plant(jax.random.randint(keys[3], (ATOMS,), 0, 2), jax.random.fold_in(keys[3], 1), 0, 1).astype(jnp.int32),
        "pair_mask": plant((jax.random.randint(keys[4], (ATOMS, ATOMS), 0, 8) < 7).astype(jnp.int32), jax.random.fold_in(keys[4], 1), 0, 1),
        "pair_bias": draw_pair_bias(jax.random.fold_in(keys[16], 71), 0),
        "ln_gain": jnp.clip(1.0 + 0.18 * jax.random.normal(keys[6], (D,), jnp.float32), 0.1, 1.9),
        "w_qkv": noise(keys[7], (D, 3 * D), D ** -0.5, 0.25),
        "gauss_mul": jnp.clip(1.0 + 0.15 * jax.random.normal(keys[8], (KINDS, KINDS), jnp.float32), 0.25, 1.75),
        "gauss_add": noise(keys[9], (KINDS, KINDS), 1.0, 4.0, (), jnp.float32),
        "gauss_mean": jnp.clip(jax.random.uniform(keys[10], (GAUSS,), jnp.float32, 0.0, 16.0), 0.0, 16.0),
        "gauss_width": jnp.clip(jnp.exp(jax.random.uniform(keys[11], (GAUSS,), jnp.float32, math.log(0.5), math.log(2.5))), 0.5, 2.5),
        "w_gauss": noise(keys[12], (GAUSS, GAUSS), (GAUSS // 16) ** -0.5, 2.0),
        "w_heads": noise(keys[13], (GAUSS, HEADS), (GAUSS // 16) ** -0.5, 2.0),
        "w_coord1": noise(keys[14], (HEADS, HEADS), HEADS ** -0.5, 0.75),
        "w_coord2": noise(keys[15], (HEADS,), HEADS ** -0.5, 0.75),
    }


ln_epsilon = 1e-05
masked_fill = -1000000000.0
root_shift = 0.01

def widened(values):
    return lax.optimization_barrier(values).astype(jnp.float32)

def layer_normed(nodes, ln_gain):
    features = nodes.astype(jnp.float32)
    row_mean = lax.optimization_barrier(jnp.mean(features, axis=1, keepdims=True))
    centred = features - row_mean
    spread = lax.optimization_barrier(jnp.mean(centred * centred, axis=1, keepdims=True))
    return (centred * lax.rsqrt(spread + ln_epsilon) * ln_gain[None, :]).astype(jnp.bfloat16)

def gaussians(expanded, gauss_mean, gauss_width):
    scaled = (expanded[None, :, :] - gauss_mean[:, None, None]) / gauss_width[:, None, None]
    norming = math.sqrt(2.0 * math.pi) * gauss_width[:, None, None]
    return (jnp.exp(-0.5 * scaled * scaled) / norming).astype(jnp.bfloat16)

def reference(nodes, coords, atom_types, segment_ids, pair_mask, pair_bias, ln_gain, w_qkv, gauss_mul, gauss_add, gauss_mean, gauss_width, w_gauss, w_heads, w_coord1, w_coord2):
    head_dim = D // HEADS
    normed = layer_normed(nodes, ln_gain)
    projected = jnp.dot(normed, w_qkv, preferred_element_type=jnp.float32).astype(jnp.bfloat16)
    queries = widened(projected[:, :D]).reshape(ATOMS, HEADS, head_dim)
    keys_all = widened(projected[:, D:2 * D]).reshape(ATOMS, HEADS, head_dim)
    values_all = widened(projected[:, 2 * D:]).reshape(ATOMS, HEADS, head_dim)
    kinds = atom_types + ATOM_TYPES * segment_ids
    block_rows = ATOMS // N_ROW

    def one_block(block_index):
        start_row = (block_index * block_rows).astype(jnp.int32)
        query_block = lax.dynamic_slice_in_dim(queries, start_row, block_rows, 0)
        coord_block = lax.dynamic_slice_in_dim(coords, start_row, block_rows, 1)
        kind_block = lax.dynamic_slice_in_dim(kinds, start_row, block_rows, 0)
        bias_block = lax.dynamic_slice_in_dim(pair_bias, start_row, block_rows, 1)
        mask_block = lax.dynamic_slice_in_dim(pair_mask, start_row, block_rows, 0)
        offsets = coord_block[:, :, None] - coords[:, None, :]
        distance = jnp.sqrt(lax.optimization_barrier(jnp.sum(offsets * offsets, axis=0)) + root_shift)
        expanded = gauss_mul[kind_block[:, None], kinds[None, :]] * distance + gauss_add[kind_block[:, None], kinds[None, :]]
        features = gaussians(expanded, gauss_mean, gauss_width)
        hidden = jax.nn.gelu(jnp.einsum('kij,kl->lij', widened(features), w_gauss.astype(jnp.float32))).astype(jnp.bfloat16)
        geometry = jnp.einsum('kij,kh->hij', widened(hidden), w_heads.astype(jnp.float32))
        affinity = jnp.einsum('ihd,jhd->hij', query_block, keys_all) / math.sqrt(head_dim)
        logits = bias_block.astype(jnp.float32) + geometry + affinity
        pair_new = logits.astype(jnp.bfloat16)
        masked = jnp.where(mask_block[None, :, :] == 1, logits, masked_fill)
        weights = jnp.exp(masked - lax.optimization_barrier(jnp.max(masked, axis=2, keepdims=True)))
        denominator = lax.optimization_barrier(jnp.sum(weights, axis=2))
        numerator = jnp.einsum('hij,jhd->ihd', widened(weights.astype(jnp.bfloat16)), values_all)
        attended = (numerator / denominator.T[:, :, None]).reshape(block_rows, D).astype(jnp.bfloat16)
        mixed = jax.nn.gelu(jnp.einsum('hij,hg->gij', widened(pair_new), w_coord1.astype(jnp.float32))).astype(jnp.bfloat16)
        strength = jnp.einsum('gij,g->ij', widened(mixed), w_coord2.astype(jnp.float32))
        strength = jnp.where(mask_block == 1, strength, 0.0)
        row_total = lax.optimization_barrier(jnp.sum(strength, axis=1))
        pulled = jnp.dot(strength, coords.T, precision=lax.Precision.HIGHEST)
        displace = (coord_block.T * row_total[:, None] - pulled) / ATOMS
        return (attended, displace)
    attended, displace = lax.map(one_block, jnp.arange(N_ROW, dtype=jnp.int32))
    attended = attended.reshape(ATOMS, D)
    moved = coords + displace.reshape(ATOMS, 3).T
    return (attended, moved)
```

```python
import functools
import math

import jax
import jax.numpy as jnp
from jax import lax
from jax.experimental import pallas as pl
from jax.experimental.pallas import tpu as pltpu
from jax.sharding import PartitionSpec as P

ln_epsilon = 1e-05
masked_fill = -1000000000.0
masked_below = -100000000.0
root_shift = 0.01
lanes = 128
f32 = jnp.float32
bf16 = jnp.bfloat16
nt = (((1,), (1,)), ((), ()))
tn = (((0,), (0,)), ((), ()))


def split3(x):
    hi = x.astype(bf16).astype(f32)
    mid = (x - hi).astype(bf16).astype(f32)
    return hi, mid, x - hi - mid


def iota(shape, axis):
    return lax.broadcasted_iota(jnp.int32, shape, axis)


def column(row):
    n = row.shape[1]
    square = jnp.where(iota((n, n), 0) == iota((n, n), 1), jnp.broadcast_to(row, (n, n)), 0.0)
    return jnp.sum(square, axis=1, keepdims=True)


def gelu(x):
    inner = x * (0.7978845608028654 + 0.035677408136300125 * (x * x))
    return (0.5 * x) * (1.0 + jnp.tanh(inner))


def node_rows(width, own):
    return -(-(width // lanes + 1) * own // 16) * 16


def pack_kernel(dims, nodes, coords, types, segments, mask, bias, *refs):
    own, cols, width, heads, keys, kinds = dims
    outs, held = refs[:cols], refs[cols]
    queries = own * cols
    me = lax.axis_index("col")
    pieces = own * keys // lanes
    lane, row = iota((own, lanes), 1), iota((own, lanes), 0)
    table = jnp.zeros((own, lanes), f32)
    for c in range(3):
        for n, part in enumerate(split3(column(coords[c : c + 1, :]))):
            table = jnp.where(lane == 3 * n + c, part, table)
    for t in range(own):
        kind = (types[t] + kinds // 2 * segments[t]).astype(f32)
        table = jnp.where((lane == 9) & (row == t), kind, table)
    full = nodes[...].astype(f32)
    blocks = [full[:, b * lanes : (b + 1) * lanes] for b in range(width // lanes)] + [table]
    used = len(blocks) * own
    blocks.append(jnp.zeros((node_rows(width, own) - used, lanes), f32))
    packed = jnp.concatenate(blocks, axis=0).astype(bf16)
    for out in outs:
        out[pieces * heads :, :] = packed
    kept = jnp.where(mask[...][None] == 1, bias[...].astype(f32), masked_fill)
    held[:, :keys] = kept.reshape(heads * queries, keys)
    blocks_of = refs[cols + 1]
    for d in range(cols):
        rows = [held[pl.ds(d * own + i, heads, stride=queries), :][:, :keys] for i in range(own)]
        wide = jnp.concatenate(rows, axis=1).astype(bf16)
        for b in range(pieces):
            blocks_of[d, b * heads : (b + 1) * heads, :] = wide[:, b * lanes : (b + 1) * lanes]
    for k in range(cols):
        outs[k][: pieces * heads, :] = blocks_of[me ^ k]


def gather_kernel(dims, *refs):
    own, cols, width, heads, keys, kinds = dims
    start = own * keys // lanes * heads
    out = refs[cols]
    blocks = [ref[start:, :].astype(f32) for ref in refs[:cols]]
    for b in range(width // lanes + 1):
        rows = jnp.concatenate([block[b * own : (b + 1) * own] for block in blocks], axis=0)
        out[:, b * lanes : (b + 1) * lanes] = rows.astype(bf16)


def arrange_kernel(dims, *refs):
    own, cols, width, heads, keys, kinds = dims
    out = refs[cols]
    atoms = out.shape[1]
    per_row = own * cols
    r, c = lax.axis_index("row"), lax.axis_index("col")
    wide = [
        jnp.concatenate(
            [ref[b * heads : (b + 1) * heads, :].astype(f32) for b in range(own * keys // lanes)],
            axis=1,
        )
        for ref in refs[:cols]
    ]
    blocks = [
        jnp.concatenate([w[:, i * keys : (i + 1) * keys] for i in range(own)], axis=0).astype(bf16)
        for w in wide
    ]
    step = max(lanes // keys, 1)
    for s in range(0, atoms, lanes):
        slot = s + iota((1, lanes), 1)
        source = ((r ^ (slot // per_row)) * cols + (c ^ (slot % per_row // own))) * own + slot % own
        total = jnp.zeros((own * heads, lanes), f32)
        for k in range(0, cols, step):
            place = iota((step * keys, 1), 0)
            atom = (c ^ (k + place // keys)) * keys + place % keys
            chosen = (atom == source).astype(f32).astype(bf16)
            taken = jnp.concatenate([blocks[k + n] for n in range(step)], axis=1)
            total = total + jnp.dot(taken, chosen, preferred_element_type=f32)
        out[:, s : s + lanes] = total.astype(bf16)


def attend_kernel(
    dims,
    near,
    far,
    bias,
    coords,
    ln_gain,
    w_qkv,
    gauss_mul,
    gauss_add,
    gauss_mean,
    gauss_width,
    w_gauss,
    w_heads,
    w_coord1,
    w_coord2,
    attended,
    moved,
    logits,
    values,
    places,
    strengths,
):
    own, cols, width, heads, keys, kinds = dims
    atoms = bias.shape[1]
    head_dim = width // heads
    half = near.shape[0]
    gain = ln_gain[...]

    def normed(x):
        features = x.astype(f32)
        centred = features - jnp.mean(features, axis=1, keepdims=True)
        spread = jnp.mean(centred * centred, axis=1, keepdims=True)
        return (centred * lax.rsqrt(spread + ln_epsilon) * gain).astype(bf16)

    own_table = near[:16, width:].astype(f32)
    own_columns = [
        (own_table[:, c : c + 1] + own_table[:, 3 + c : 4 + c]) + own_table[:, 6 + c : 7 + c]
        for c in range(3)
    ]
    own_kind = own_table[:, 9:10].astype(jnp.int32)
    query_onehot = (own_kind == iota((16, kinds), 1)).astype(f32).astype(bf16)
    looked = []
    for table in (gauss_mul, gauss_add):
        parts = [
            jnp.dot(query_onehot, part.astype(bf16), preferred_element_type=f32)
            for part in split3(table[...])
        ]
        looked.extend(part.astype(bf16) for part in parts)
    lookup = jnp.concatenate(looked, axis=0)
    inverse = 1.0 / column(gauss_width[...])
    centre = column(gauss_mean[...])
    sharp = inverse * math.sqrt(0.5 * math.log2(math.e))
    norming = jnp.log2(inverse * (1.0 / math.sqrt(2.0 * math.pi)))
    queries = jnp.dot(normed(near[:16, :width]), w_qkv[:, :width], preferred_element_type=f32)
    head_mask = iota((heads, width), 1) // head_dim == iota((heads, width), 0)
    spread_queries = jnp.concatenate(
        [
            jnp.where(head_mask, jnp.broadcast_to(queries[i : i + 1], (heads, width)), 0.0)
            for i in range(own)
        ],
        axis=0,
    ).astype(bf16)
    select_at, select_from = iota((16, lanes), 0), iota((16, lanes), 1)
    selector = (
        ((select_from < 9) & (select_from % 3 == select_at) & (select_at < 3))
        | ((select_from == 9) & (select_at == 3))
    ).astype(f32).astype(bf16)

    for s in range(0, atoms, lanes):
        if half < lanes:
            x = jnp.concatenate([near[...], far[...]], axis=0)
        elif s < half:
            x = near[s : s + lanes, :]
        else:
            x = far[s - half : s - half + lanes, :]
        block = normed(x[:, :width])
        both = jnp.dot(block, w_qkv[:, width:], preferred_element_type=f32).astype(bf16)
        values[s : s + lanes, :] = both[:, width:]
        table = lax.dot_general(selector, x[:, width:], nt, preferred_element_type=f32)
        places[:, s : s + lanes] = jnp.where(iota((16, lanes), 0) == 3, 1.0, table)
        offsets = [own_columns[c] - table[c : c + 1] for c in range(3)]
        squares = offsets[0] * offsets[0] + offsets[1] * offsets[1] + offsets[2] * offsets[2]
        distance = jnp.sqrt(squares + root_shift)
        key_onehot = (table[3:4].astype(jnp.int32) == iota((kinds, lanes), 0)).astype(f32).astype(bf16)
        found = jnp.dot(lookup, key_onehot, preferred_element_type=f32)
        scale = found[0:16] + found[16:32] + found[32:48]
        shift = found[48:64] + found[64:80] + found[80:96]
        expanded = scale * distance + shift
        features = []
        for i in range(own):
            scaled = (expanded[i : i + 1] - centre) * sharp
            features.append(jnp.exp2(norming - scaled * scaled).astype(bf16))
        hidden = lax.dot_general(
            w_gauss[...], jnp.concatenate(features, axis=1), tn, preferred_element_type=f32
        )
        geometry = lax.dot_general(
            w_heads[...], gelu(hidden).astype(bf16), tn, preferred_element_type=f32
        )
        affinity = lax.dot_general(spread_queries, both[:, :width], nt, preferred_element_type=f32)
        here = bias[:, s : s + lanes].astype(f32)
        rows = []
        for i in range(own):
            at = slice(i * heads, (i + 1) * heads)
            row = here[at] + geometry[:, i * lanes : (i + 1) * lanes]
            row = row + affinity[at] * (1.0 / math.sqrt(head_dim))
            logits[at, s : s + lanes] = jnp.where(here[at] < masked_below, masked_fill, row)
            rows.append(row.astype(bf16))
        mixed = lax.dot_general(
            w_coord1[...], jnp.concatenate(rows, axis=1), tn, preferred_element_type=f32
        )
        strength = jnp.dot(w_coord2[...], gelu(mixed).astype(bf16), preferred_element_type=f32)
        strengths[:, s : s + lanes] = jnp.concatenate(
            [
                jnp.where(
                    here[i * heads : i * heads + 1] < masked_below,
                    0.0,
                    strength[:, i * lanes : (i + 1) * lanes],
                )
                for i in range(own)
            ],
            axis=0,
        )

    masked = logits[...]
    weights = jnp.exp(masked - jnp.max(masked, axis=1, keepdims=True))
    share = 1.0 / jnp.sum(weights, axis=1, keepdims=True)
    taken = jnp.dot(weights.astype(bf16), values[...], preferred_element_type=f32) * share
    attended[...] = jnp.concatenate(
        [
            jnp.sum(
                jnp.where(head_mask, taken[i * heads : (i + 1) * heads], 0.0), axis=0, keepdims=True
            )
            for i in range(own)
        ],
        axis=0,
    ).astype(bf16)
    pulled = lax.dot_general(
        places[...],
        strengths[...],
        nt,
        precision=lax.Precision.HIGHEST,
        preferred_element_type=f32,
    )
    here = coords[...]
    moved[...] = here + (here * pulled[3:4] - pulled[0:3]) * (1.0 / atoms)


def shards(
    nodes,
    coords,
    atom_types,
    segment_ids,
    pair_mask,
    pair_bias,
    ln_gain,
    w_qkv,
    gauss_mul,
    gauss_add,
    gauss_mean,
    gauss_width,
    w_gauss,
    w_heads,
    w_coord1,
    w_coord2,
):
    cols, rows = lax.axis_size("col"), lax.axis_size("row")
    own, width = nodes.shape
    heads, queries, keys = pair_bias.shape
    kinds = gauss_mul.shape[0]
    atoms = own * rows * cols
    dims = (own, cols, width, heads, keys, kinds)
    payload = jax.ShapeDtypeStruct((own * keys // lanes * heads + node_rows(width, own), lanes), bf16)
    params = pltpu.CompilerParams(vmem_limit_bytes=(16 if atoms <= 128 else 56) * 2**20)
    vmem, smem = pl.BlockSpec(memory_space=pltpu.VMEM), pl.BlockSpec(memory_space=pltpu.SMEM)
    packed = pl.pallas_call(
        functools.partial(pack_kernel, dims),
        out_shape=[payload] * cols,
        in_specs=[vmem, vmem, smem, smem, vmem, vmem],
        out_specs=[vmem] * cols,
        scratch_shapes=[
            pltpu.VMEM((heads * queries, lanes), f32),
            pltpu.VMEM((cols, own * keys // lanes * heads, lanes), bf16),
        ],
        compiler_params=params,
        name="pack",
    )(nodes, coords, atom_types, segment_ids, pair_mask, pair_bias)
    arrived = [packed[0]] + [
        lax.ppermute(packed[k], "col", [(i, i ^ k) for i in range(cols)]) for k in range(1, cols)
    ]
    near = pl.pallas_call(
        functools.partial(gather_kernel, dims),
        out_shape=jax.ShapeDtypeStruct((own * cols, width + lanes), bf16),
        in_specs=[vmem] * cols,
        out_specs=vmem,
        compiler_params=params,
        name="gather",
    )(*arrived)
    bias = pl.pallas_call(
        functools.partial(arrange_kernel, dims),
        out_shape=jax.ShapeDtypeStruct((own * heads, atoms), bf16),
        in_specs=[vmem] * cols,
        out_specs=vmem,
        compiler_params=params,
        name="arrange",
    )(*arrived)
    step = 1
    while True:
        far = lax.ppermute(near, "row", [(i, i ^ step) for i in range(rows)])
        step *= 2
        if step == rows:
            break
        near = jnp.concatenate([near, far], axis=0)
    attended, moved = pl.pallas_call(
        functools.partial(attend_kernel, dims),
        out_shape=[
            jax.ShapeDtypeStruct((own, width), bf16),
            jax.ShapeDtypeStruct((3, own), f32),
        ],
        in_specs=[vmem] * 14,
        out_specs=[vmem] * 2,
        scratch_shapes=[
            pltpu.VMEM((own * heads, atoms), f32),
            pltpu.VMEM((atoms, width), bf16),
            pltpu.VMEM((16, atoms), f32),
            pltpu.VMEM((own, atoms), f32),
        ],
        compiler_params=params,
        name="attend",
    )(
        near,
        far,
        bias,
        coords,
        ln_gain[None, :],
        w_qkv,
        gauss_mul,
        gauss_add,
        gauss_mean[None, :],
        gauss_width[None, :],
        w_gauss,
        w_heads,
        w_coord1,
        w_coord2[None, :],
    )
    return attended, moved


def solution(mesh):
    own, tile, whole = P(("row", "col")), P("row", "col"), P()
    in_specs = (
        P(("row", "col"), None),
        P(None, ("row", "col")),
        own,
        own,
        tile,
        P(None, "row", "col"),
    ) + (whole,) * 10
    out_specs = (P(("row", "col"), None), P(None, ("row", "col")))
    return jax.shard_map(shards, mesh=mesh, in_specs=in_specs, out_specs=out_specs, check_vma=False)
```

```python
import functools
import math

import jax
import jax.numpy as jnp
from jax import lax
from jax.experimental import pallas as pl
from jax.experimental.pallas import tpu as pltpu
from jax.sharding import PartitionSpec as P

ln_epsilon = 1e-05
masked_fill = -1000000000.0
masked_below = -100000000.0
root_shift = 0.01
lanes = 128
f32 = jnp.float32
bf16 = jnp.bfloat16
nt = (((1,), (1,)), ((), ()))
tn = (((0,), (0,)), ((), ()))


def split3(x):
    hi = x.astype(bf16).astype(f32)
    mid = (x - hi).astype(bf16).astype(f32)
    return hi, mid, x - hi - mid


def iota(shape, axis):
    return lax.broadcasted_iota(jnp.int32, shape, axis)


def column(row):
    n = row.shape[1]
    square = jnp.where(iota((n, n), 0) == iota((n, n), 1), jnp.broadcast_to(row, (n, n)), 0.0)
    return jnp.sum(square, axis=1, keepdims=True)


def gelu(x):
    inner = x * (0.7978845608028654 + 0.035677408136300125 * (x * x))
    return (0.5 * x) * (1.0 + jnp.tanh(inner))


def node_rows(width, own):
    return width // lanes * own + own


def payload_rows(dims):
    own, cols, width, heads, keys, kinds = dims
    pairs = own * keys
    used = pairs * heads // lanes + node_rows(width, own) + pairs // lanes
    return -(-used // 16) * 16


def in_hbm(x):
    return pltpu.with_memory_space_constraint(x, pltpu.HBM)


def fetch(sources, targets, semaphores):
    copies = [
        pltpu.make_async_copy(source, target, semaphores.at[n])
        for n, (source, target) in enumerate(zip(sources, targets, strict=True))
    ]
    for copy in copies:
        copy.start()
    return copies


def pack_kernel(dims, *refs):
    own, cols, width, heads, keys, kinds = dims
    sources, outs, held = refs[:6], refs[6 : 6 + cols], refs[6 + cols : 12 + cols]
    masks, semaphores = refs[12 + cols :]
    copies = fetch(sources, held, semaphores)
    nodes, coords, types, segments, mask, bias = held
    me = lax.axis_index("col")
    pairs, fold = own * keys, lanes // heads
    bias_rows = pairs // fold
    for copy in copies[:4]:
        copy.wait()
    lane = iota((own, lanes), 1)
    table = jnp.zeros((own, lanes), f32)
    for c in range(3):
        for n, part in enumerate(split3(column(coords[c : c + 1, :]))):
            table = jnp.where(lane == 3 * n + c, part, table)
    kind = (types[...] + kinds // 2 * segments[...]).astype(f32)
    table = jnp.where(lane == 9, column(kind), table)
    full = nodes[...].astype(f32)
    blocks = [full[:, b * lanes : (b + 1) * lanes] for b in range(width // lanes)] + [table]
    copies[4].wait()
    wide_mask = mask[...].astype(f32)
    for d in range(cols):
        row = jnp.concatenate([wide_mask[d * own + i : d * own + i + 1] for i in range(own)], axis=1)
        for n in range(pairs // lanes):
            masks[d, n : n + 1, :] = row[:, n * lanes : (n + 1) * lanes]
    rest = payload_rows(dims) - bias_rows - node_rows(width, own) - pairs // lanes
    if rest:
        filler = [jnp.zeros((rest, lanes), f32)]
    else:
        filler = []
    copies[5].wait()
    for k in range(cols):
        target = me ^ k
        tail = jnp.concatenate(blocks + [masks[target]] + filler, axis=0)
        outs[k][bias_rows:, :] = tail.astype(bf16)
        tile = bias[pl.ds(target * own, own)].astype(f32).reshape(pairs, heads)
        wide = [tile[n * bias_rows : (n + 1) * bias_rows] for n in range(fold)]
        outs[k][:bias_rows, :] = jnp.concatenate(wide, axis=1).astype(bf16)


def gather_kernel(dims, *refs):
    own, cols, width, heads, keys, kinds = dims
    start = own * keys * heads // lanes
    out = refs[cols]
    blocks = [ref[start:, :].astype(f32) for ref in refs[:cols]]
    for b in range(width // lanes + 1):
        rows = jnp.concatenate([block[b * own : (b + 1) * own] for block in blocks], axis=0)
        out[:, b * lanes : (b + 1) * lanes] = rows.astype(bf16)


def arrange_kernel(dims, steps, *refs):
    own, cols, width, heads, keys, kinds = dims
    out = refs[cols]
    atoms = out.shape[1]
    pairs, fold = own * keys, lanes // heads
    bias_rows, each = pairs // fold, own // fold
    mask_at = bias_rows + node_rows(width, own)
    per_row = own * cols
    r, c = lax.axis_index("row"), lax.axis_index("col")
    blocks = [
        jnp.concatenate([ref[b * keys : (b + 1) * keys, :] for ref in refs[:cols]], axis=0)
        for b in range(each)
    ]
    mask_rows = []
    for i in range(own):
        parts = []
        for ref in refs[:cols]:
            tail = ref[bias_rows:, :].astype(f32)
            first = mask_at - bias_rows + i * keys // lanes
            parts.append(tail[first : first + 1, i * keys % lanes : i * keys % lanes + keys])
        mask_rows.append(jnp.concatenate(parts, axis=1))
    mask_rows = jnp.concatenate(mask_rows + [jnp.zeros((16 - own, atoms), f32)], axis=0).astype(bf16)
    place = iota((atoms, 1), 0)
    atom = (c ^ (place // keys)) * keys + place % keys
    for s in range(0, atoms, lanes):
        slot = s + iota((1, lanes), 1)
        bits = slot // per_row
        row = r
        for n, step in enumerate(steps):
            row = row ^ (((bits >> n) & 1) * step)
        source = (row * cols + (c ^ (slot % per_row // own))) * own + slot % own
        chosen = (atom == source).astype(f32).astype(bf16)
        valid = jnp.dot(mask_rows, chosen, preferred_element_type=f32)
        for b in range(each):
            moved = lax.dot_general(blocks[b], chosen, tn, preferred_element_type=f32)
            for a in range(fold):
                i = a * each + b
                kept = jnp.where(valid[i : i + 1] > 0.5, moved[a * heads : (a + 1) * heads], masked_fill)
                out[i * heads : (i + 1) * heads, s : s + lanes] = kept.astype(bf16)


def normed(x, gain):
    features = x.astype(f32)
    centred = features - jnp.mean(features, axis=1, keepdims=True)
    spread = jnp.mean(centred * centred, axis=1, keepdims=True)
    return (centred * lax.rsqrt(spread + ln_epsilon) * gain).astype(bf16)


def prepare_kernel(dims, near, *refs):
    own, cols, width, heads, keys, kinds = dims
    sources = refs[:11]
    w_qkv, w_heads, ln_gain, w_coord2, coords = refs[11:16]
    w_gauss, w_coord1, spread_queries, lookup, own_columns, kernels = refs[16:22]
    mul_held, add_held, mean_held, width_held, gauss_held, coord1_held, semaphores = refs[22:]
    copies = fetch(
        sources,
        (w_qkv, w_heads, ln_gain, w_coord2, coords)
        + (mul_held, add_held, mean_held, width_held, gauss_held, coord1_held),
        semaphores,
    )
    x = near[:16, :]
    own_table = x[:, width:].astype(f32)
    for c in range(3):
        parts = (own_table[:, c : c + 1] + own_table[:, 3 + c : 4 + c]) + own_table[:, 6 + c : 7 + c]
        own_columns[c * 8 : c * 8 + 8, :] = jnp.broadcast_to(parts[:8], (8, lanes))
    own_kind = own_table[:, 9:10].astype(jnp.int32)
    query_onehot = (own_kind == iota((16, kinds), 1)).astype(f32).astype(bf16)
    for copy in copies[5:]:
        copy.wait()
    inverse = 1.0 / column(width_held[...])
    gauss = inverse.shape[0]
    kernels[0] = jnp.broadcast_to(column(mean_held[...]), (gauss, lanes))
    kernels[1] = jnp.broadcast_to(inverse * math.sqrt(0.5 * math.log2(math.e)), (gauss, lanes))
    kernels[2] = jnp.broadcast_to(jnp.log2(inverse * (1.0 / math.sqrt(2.0 * math.pi))), (gauss, lanes))
    at = 0
    for table in (mul_held, add_held):
        for part in split3(table[...]):
            found = jnp.dot(query_onehot, part.astype(bf16), preferred_element_type=f32)
            lookup[at : at + 16, :] = found.astype(bf16)
            at += 16
    w_gauss[...] = gauss_held[...].astype(f32).T.astype(bf16)
    w_coord1[...] = coord1_held[...].astype(f32).T.astype(bf16)
    for copy in copies[:5]:
        copy.wait()
    queries = jnp.dot(
        normed(x[:, :width], ln_gain[...]), w_qkv[:, :width], preferred_element_type=f32
    )
    head_mask = iota((heads, width), 1) // (width // heads) == iota((heads, width), 0)
    for i in range(own):
        spread = jnp.where(head_mask, jnp.broadcast_to(queries[i : i + 1], (heads, width)), 0.0)
        spread_queries[i * heads : (i + 1) * heads, :] = spread.astype(bf16)


def attend_kernel(
    dims,
    near,
    far,
    bias,
    w_qkv,
    w_heads,
    ln_gain,
    w_coord2,
    coords,
    w_gauss,
    w_coord1,
    spread_queries,
    lookup,
    own_columns,
    kernels,
    attended,
    moved,
    logits,
    values,
    places,
    strengths,
):
    own, cols, width, heads, keys, kinds = dims
    atoms = bias.shape[1]
    head_dim = width // heads
    half = near.shape[0]
    gain = ln_gain[...]
    select_at, select_from = iota((16, lanes), 0), iota((16, lanes), 1)
    selector = (
        ((select_from < 9) & (select_from % 3 == select_at) & (select_at < 3))
        | ((select_from == 9) & (select_at == 3))
    ).astype(f32).astype(bf16)
    centre, sharp, norming = kernels[0], kernels[1], kernels[2]

    for s in range(0, atoms, lanes):
        if half < lanes:
            x = jnp.concatenate([near[...], far[...]], axis=0)
        elif s < half:
            x = near[s : s + lanes, :]
        else:
            x = far[s - half : s - half + lanes, :]
        table = lax.dot_general(selector, x[:, width:], nt, preferred_element_type=f32)
        places[:, s : s + lanes] = jnp.where(iota((16, lanes), 0) == 3, 1.0, table)
        offsets = [own_columns[c * 8 : c * 8 + own, :] - table[c : c + 1] for c in range(3)]
        squares = offsets[0] * offsets[0] + offsets[1] * offsets[1] + offsets[2] * offsets[2]
        distance = jnp.sqrt(squares + root_shift)
        key_onehot = (table[3:4].astype(jnp.int32) == iota((kinds, lanes), 0)).astype(f32).astype(bf16)
        found = jnp.dot(lookup[...], key_onehot, preferred_element_type=f32)
        scale = found[0:16] + found[16:32] + found[32:48]
        shift = found[48:64] + found[64:80] + found[80:96]
        expanded = scale[:own] * distance + shift[:own]
        features = []
        for i in range(own):
            scaled = (expanded[i : i + 1] - centre) * sharp
            features.append(jnp.exp2(norming - scaled * scaled).astype(bf16))
        hidden = jnp.dot(w_gauss[...], jnp.concatenate(features, axis=1), preferred_element_type=f32)
        geometry = jnp.dot(w_heads[...], gelu(hidden).astype(bf16), preferred_element_type=f32)
        block = normed(x[:, :width], gain)
        both = jnp.dot(block, w_qkv[:, width:], preferred_element_type=f32).astype(bf16)
        values[s : s + lanes, :] = both[:, width:]
        affinity = lax.dot_general(
            spread_queries[...], both[:, :width], nt, preferred_element_type=f32
        )
        here = bias[:, s : s + lanes].astype(f32)
        rows = []
        for i in range(own):
            at = slice(i * heads, (i + 1) * heads)
            row = here[at] + geometry[:, i * lanes : (i + 1) * lanes]
            row = row + affinity[at] * (1.0 / math.sqrt(head_dim))
            logits[at, s : s + lanes] = jnp.where(here[at] < masked_below, masked_fill, row)
            rows.append(row.astype(bf16))
        mixed = jnp.dot(w_coord1[...], jnp.concatenate(rows, axis=1), preferred_element_type=f32)
        strength = jnp.dot(w_coord2[...], gelu(mixed).astype(bf16), preferred_element_type=f32)
        strengths[:, s : s + lanes] = jnp.concatenate(
            [
                jnp.where(
                    here[i * heads : i * heads + 1] < masked_below,
                    0.0,
                    strength[:, i * lanes : (i + 1) * lanes],
                )
                for i in range(own)
            ],
            axis=0,
        )

    masked = logits[...]
    weights = jnp.exp(masked - jnp.max(masked, axis=1, keepdims=True))
    share = 1.0 / jnp.sum(weights, axis=1, keepdims=True)
    taken = jnp.dot(weights.astype(bf16), values[...], preferred_element_type=f32) * share
    head_mask = iota((heads, width), 1) // head_dim == iota((heads, width), 0)
    attended[...] = jnp.concatenate(
        [
            jnp.sum(
                jnp.where(head_mask, taken[i * heads : (i + 1) * heads], 0.0), axis=0, keepdims=True
            )
            for i in range(own)
        ],
        axis=0,
    ).astype(bf16)
    pulled = lax.dot_general(
        places[...],
        strengths[...],
        nt,
        precision=lax.Precision.HIGHEST,
        preferred_element_type=f32,
    )
    here = coords[...]
    moved[...] = here + (here * pulled[3:4] - pulled[0:3]) * (1.0 / atoms)


def shards(
    nodes,
    coords,
    atom_types,
    segment_ids,
    pair_mask,
    pair_bias,
    ln_gain,
    w_qkv,
    gauss_mul,
    gauss_add,
    gauss_mean,
    gauss_width,
    w_gauss,
    w_heads,
    w_coord1,
    w_coord2,
):
    cols, rows = lax.axis_size("col"), lax.axis_size("row")
    own, width = nodes.shape
    heads, queries, keys = pair_bias.shape
    kinds, gauss = gauss_mul.shape[0], gauss_mean.shape[0]
    atoms = own * rows * cols
    dims = (own, cols, width, heads, keys, kinds)
    shape = jax.ShapeDtypeStruct
    params = pltpu.CompilerParams(vmem_limit_bytes=(16 if atoms <= 128 else 56) * 2**20)
    vmem, anywhere = pl.BlockSpec(memory_space=pltpu.VMEM), pl.BlockSpec(memory_space=pl.ANY)
    sources = (
        nodes,
        coords,
        atom_types[None, :],
        segment_ids[None, :],
        pair_mask,
        pair_bias.transpose(1, 2, 0),
    )
    packed = pl.pallas_call(
        functools.partial(pack_kernel, dims),
        out_shape=[shape((payload_rows(dims), lanes), bf16)] * cols,
        in_specs=[anywhere] * 6,
        out_specs=[vmem] * cols,
        scratch_shapes=[pltpu.VMEM(x.shape, x.dtype) for x in sources]
        + [pltpu.VMEM((cols, own * keys // lanes, lanes), f32), pltpu.SemaphoreType.DMA((6,))],
        compiler_params=params,
        name="pack",
    )(*map(in_hbm, sources))
    arrived = [packed[0]] + [
        lax.ppermute(packed[k], "col", [(i, i ^ k) for i in range(cols)]) for k in range(1, cols)
    ]
    near = pl.pallas_call(
        functools.partial(gather_kernel, dims),
        out_shape=shape((own * cols, width + lanes), bf16),
        in_specs=[vmem] * cols,
        out_specs=vmem,
        compiler_params=params,
        name="gather",
    )(*arrived)
    steps = [2**n for n in range(1, rows.bit_length() - 1)] + [1]
    bias = pl.pallas_call(
        functools.partial(arrange_kernel, dims, steps),
        out_shape=shape((own * heads, atoms), bf16),
        in_specs=[vmem] * cols,
        out_specs=vmem,
        compiler_params=params,
        name="arrange",
    )(*arrived)
    weights = (w_qkv, w_heads.T, ln_gain[None, :], w_coord2[None, :], coords)
    tables = (gauss_mul, gauss_add, gauss_mean[None, :], gauss_width[None, :], w_gauss, w_coord1)
    prepared = pl.pallas_call(
        functools.partial(prepare_kernel, dims),
        out_shape=[shape(x.shape, x.dtype) for x in weights]
        + [
            shape((gauss, gauss), bf16),
            shape(w_coord1.shape, bf16),
            shape((own * heads, width), bf16),
            shape((96, kinds), bf16),
            shape((24, lanes), f32),
            shape((3, gauss, lanes), f32),
        ],
        in_specs=[vmem] + [anywhere] * 11,
        out_specs=[vmem] * 11,
        scratch_shapes=[pltpu.VMEM(x.shape, x.dtype) for x in tables]
        + [pltpu.SemaphoreType.DMA((11,))],
        compiler_params=params,
        name="prepare",
    )(near, *map(in_hbm, weights + tables))
    for n, step in enumerate(steps):
        far = lax.ppermute(near, "row", [(i, i ^ step) for i in range(rows)])
        if n < len(steps) - 1:
            near = jnp.concatenate([near, far], axis=0)
    attended, moved = pl.pallas_call(
        functools.partial(attend_kernel, dims),
        out_shape=[shape((own, width), bf16), shape((3, own), f32)],
        in_specs=[vmem] * 14,
        out_specs=[vmem] * 2,
        scratch_shapes=[
            pltpu.VMEM((own * heads, atoms), f32),
            pltpu.VMEM((atoms, width), bf16),
            pltpu.VMEM((16, atoms), f32),
            pltpu.VMEM((own, atoms), f32),
        ],
        compiler_params=params,
        name="attend",
    )(near, far, bias, *prepared)
    return attended, moved


def solution(mesh):
    own, tile, whole = P(("row", "col")), P("row", "col"), P()
    in_specs = (
        P(("row", "col"), None),
        P(None, ("row", "col")),
        own,
        own,
        tile,
        P(None, "row", "col"),
    ) + (whole,) * 10
    out_specs = (P(("row", "col"), None), P(None, ("row", "col")))
    return jax.shard_map(shards, mesh=mesh, in_specs=in_specs, out_specs=out_specs, check_vma=False)
```

```python
import functools
import math

import jax
import jax.numpy as jnp
from jax import lax
from jax.experimental import pallas as pl
from jax.experimental.pallas import tpu as pltpu
from jax.sharding import PartitionSpec as P

ln_epsilon = 1e-05
masked_fill = -1000000000.0
masked_below = -100000000.0
root_shift = 0.01
lanes = 128
f32 = jnp.float32
bf16 = jnp.bfloat16
nt = (((1,), (1,)), ((), ()))
tn = (((0,), (0,)), ((), ()))


def split3(x):
    hi = x.astype(bf16).astype(f32)
    mid = (x - hi).astype(bf16).astype(f32)
    return hi, mid, x - hi - mid


def iota(shape, axis):
    return lax.broadcasted_iota(jnp.int32, shape, axis)


def column(row):
    n = row.shape[1]
    square = jnp.where(iota((n, n), 0) == iota((n, n), 1), jnp.broadcast_to(row, (n, n)), 0.0)
    return jnp.sum(square, axis=1, keepdims=True)


def gelu(x):
    inner = x * (0.7978845608028654 + 0.035677408136300125 * (x * x))
    return (0.5 * x) * (1.0 + jnp.tanh(inner))


def node_rows(width, own):
    return (width // lanes + 1) * own


def sizes(dims):
    own, cols, width, heads, keys, kinds = dims
    bias_rows, mask_rows = own * keys * heads // lanes, own * keys // lanes
    first = node_rows(width, own) + (cols - 1) * (bias_rows + mask_rows)
    second = bias_rows + 2 * node_rows(width, own) + mask_rows
    return bias_rows, mask_rows, -(-first // 16) * 16, -(-second // 16) * 16


def in_hbm(x):
    return pltpu.with_memory_space_constraint(x, pltpu.HBM)


def fetch(sources, targets, semaphores):
    copies = [
        pltpu.make_async_copy(source, target, semaphores.at[n])
        for n, (source, target) in enumerate(zip(sources, targets, strict=True))
    ]
    for copy in copies:
        copy.start()
    return copies


def filled(blocks, rows):
    rest = rows - sum(block.shape[0] for block in blocks)
    return jnp.concatenate(blocks + ([jnp.zeros((rest, lanes), f32)] if rest else []), axis=0)


def pack_kernel(dims, *refs):
    own, cols, width, heads, keys, kinds = dims
    bias_rows, mask_rows, first_rows, second_rows = sizes(dims)
    sources, first, kept, held, masks, semaphores = refs[:6], refs[6], refs[7], refs[8:14], refs[14], refs[15]
    copies = fetch(sources, held, semaphores)
    nodes, coords, types, segments, mask, bias = held
    me = lax.axis_index("col")
    pairs, fold = own * keys, lanes // heads
    for copy in copies[:4]:
        copy.wait()
    lane = iota((own, lanes), 1)
    table = jnp.zeros((own, lanes), f32)
    for c in range(3):
        for n, part in enumerate(split3(column(coords[c : c + 1, :]))):
            table = jnp.where(lane == 3 * n + c, part, table)
    kind = (types[...] + kinds // 2 * segments[...]).astype(f32)
    table = jnp.where(lane == 9, column(kind), table)
    full = nodes[...].astype(f32)
    blocks = [full[:, b * lanes : (b + 1) * lanes] for b in range(width // lanes)] + [table]
    copies[4].wait()
    wide_mask = mask[...].astype(f32)
    for d in range(cols):
        row = jnp.concatenate([wide_mask[d * own + i : d * own + i + 1] for i in range(own)], axis=1)
        for n in range(mask_rows):
            masks[d, n : n + 1, :] = row[:, n * lanes : (n + 1) * lanes]
    start = (cols - 1) * bias_rows
    tail = filled(blocks + [masks[me ^ k] for k in range(1, cols)], first_rows - start)
    first[start:, :] = tail.astype(bf16)
    kept[bias_rows:, :] = filled([masks[me]], kept.shape[0] - bias_rows).astype(bf16)
    copies[5].wait()
    for k in range(cols):
        tile = bias[pl.ds((me ^ k) * own, own)].astype(f32).reshape(pairs, heads)
        wide = [tile[n * bias_rows : (n + 1) * bias_rows] for n in range(fold)]
        block = jnp.concatenate(wide, axis=1).astype(bf16)
        if k:
            first[(k - 1) * bias_rows : k * bias_rows, :] = block
        else:
            kept[:bias_rows, :] = block


def regroup_kernel(dims, order, mine, other, *outs):
    own, cols, width, heads, keys, kinds = dims
    bias_rows, mask_rows, first_rows, second_rows = sizes(dims)
    start, rows = (cols - 1) * bias_rows, node_rows(width, own)
    here, there = mine[start:, :].astype(f32), other[start:, :].astype(f32)
    for n, k in enumerate(order):
        outs[n][:bias_rows, :] = other[(k - 1) * bias_rows : k * bias_rows, :]
        at = rows + (k - 1) * mask_rows
        tail = filled([here[:rows], there[:rows], there[at : at + mask_rows]], second_rows - bias_rows)
        outs[n][bias_rows:, :] = tail.astype(bf16)


def gather_kernel(dims, order, mine, other, *refs):
    own, cols, width, heads, keys, kinds = dims
    bias_rows, mask_rows, first_rows, second_rows = sizes(dims)
    start, rows = (cols - 1) * bias_rows, node_rows(width, own)
    out = refs[cols - 1]
    blocks = [mine[start:, :].astype(f32)[:rows], other[start:, :].astype(f32)[:rows]]
    for k in range(1, cols):
        tail = refs[order.index(k)][bias_rows:, :].astype(f32)
        blocks += [tail[rows : 2 * rows], tail[:rows]]
    for b in range(width // lanes + 1):
        taken = jnp.concatenate([block[b * own : (b + 1) * own] for block in blocks], axis=0)
        out[:, b * lanes : (b + 1) * lanes] = taken.astype(bf16)


def arrange_kernel(dims, order, steps, kept, *refs):
    own, cols, width, heads, keys, kinds = dims
    bias_rows, mask_rows, first_rows, second_rows = sizes(dims)
    received = [refs[order.index(k)] for k in range(1, cols)]
    spread_queries, w_qkv, out, keyed = refs[cols - 1 :]
    keyed[...] = lax.dot_general(
        spread_queries[...], w_qkv[:, width : 2 * width], nt, preferred_element_type=f32
    ).astype(bf16)
    atoms = out.shape[1]
    fold = lanes // heads
    each = own // fold
    mask_at = 2 * node_rows(width, own)
    per_row = 2 * own * cols
    r, c = lax.axis_index("row"), lax.axis_index("col")
    blocks = [
        jnp.concatenate([ref[b * keys : (b + 1) * keys, :] for ref in [kept] + received], axis=0)
        for b in range(each)
    ]
    tails = [kept[bias_rows:, :].astype(f32)[:mask_rows]]
    tails += [ref[bias_rows:, :].astype(f32)[mask_at : mask_at + mask_rows] for ref in received]
    masks = []
    for i in range(own):
        n, lane = i * keys // lanes, i * keys % lanes
        masks.append(jnp.concatenate([tail[n : n + 1, lane : lane + keys] for tail in tails], axis=1))
    masks = jnp.concatenate(masks + [jnp.zeros((16 - own, atoms), f32)], axis=0).astype(bf16)
    place = iota((atoms, 1), 0)
    atom = (c ^ (place // keys)) * keys + place % keys
    for s in range(0, atoms, lanes):
        slot = s + iota((1, lanes), 1)
        piece, inner = slot // per_row, slot % per_row
        step = jnp.zeros((1, lanes), jnp.int32)
        for n, value in enumerate(steps):
            step = jnp.where(piece == n, value, step)
        row = r ^ step ^ (inner // own % 2)
        source = (row * cols + (c ^ (inner // (2 * own)))) * own + inner % own
        chosen = (atom == source).astype(f32).astype(bf16)
        valid = jnp.dot(masks, chosen, preferred_element_type=f32)
        for b in range(each):
            moved = lax.dot_general(blocks[b], chosen, tn, preferred_element_type=f32)
            for a in range(fold):
                i = a * each + b
                taken = jnp.where(valid[i : i + 1] > 0.5, moved[a * heads : (a + 1) * heads], masked_fill)
                out[i * heads : (i + 1) * heads, s : s + lanes] = taken.astype(bf16)


def normed(x, gain):
    features = x.astype(f32)
    centred = features - jnp.mean(features, axis=1, keepdims=True)
    spread = jnp.mean(centred * centred, axis=1, keepdims=True)
    return (centred * lax.rsqrt(spread + ln_epsilon) * gain).astype(bf16)


def prepare_kernel(dims, mine, *refs):
    own, cols, width, heads, keys, kinds = dims
    bias_rows, mask_rows, first_rows, second_rows = sizes(dims)
    sources = refs[:11]
    w_qkv, w_heads, ln_gain, w_coord2, coords = refs[11:16]
    w_gauss, w_coord1, spread_queries, lookup, own_columns, kernels = refs[16:22]
    mul_held, add_held, mean_held, width_held, gauss_held, coord1_held, semaphores = refs[22:]
    copies = fetch(
        sources,
        (w_qkv, w_heads, ln_gain, w_coord2, coords)
        + (mul_held, add_held, mean_held, width_held, gauss_held, coord1_held),
        semaphores,
    )
    rows = mine[(cols - 1) * bias_rows :, :].astype(f32)[: node_rows(width, own)]
    filler = jnp.zeros((16 - own, lanes), f32)
    x = [
        jnp.concatenate([rows[b * own : (b + 1) * own], filler], axis=0)
        for b in range(width // lanes + 1)
    ]
    own_table = x[width // lanes]
    for c in range(3):
        parts = (own_table[:, c : c + 1] + own_table[:, 3 + c : 4 + c]) + own_table[:, 6 + c : 7 + c]
        own_columns[c * 8 : c * 8 + 8, :] = jnp.broadcast_to(parts[:8], (8, lanes))
    own_kind = own_table[:, 9:10].astype(jnp.int32)
    query_onehot = (own_kind == iota((16, kinds), 1)).astype(f32).astype(bf16)
    for copy in copies[5:]:
        copy.wait()
    inverse = 1.0 / column(width_held[...])
    gauss = inverse.shape[0]
    kernels[0] = jnp.broadcast_to(column(mean_held[...]), (gauss, lanes))
    kernels[1] = jnp.broadcast_to(inverse * math.sqrt(0.5 * math.log2(math.e)), (gauss, lanes))
    kernels[2] = jnp.broadcast_to(jnp.log2(inverse * (1.0 / math.sqrt(2.0 * math.pi))), (gauss, lanes))
    at = 0
    for table in (mul_held, add_held):
        for part in split3(table[...]):
            found = jnp.dot(query_onehot, part.astype(bf16), preferred_element_type=f32)
            lookup[at : at + 16, :] = found.astype(bf16)
            at += 16
    w_gauss[...] = gauss_held[...].astype(f32).T.astype(bf16)
    w_coord1[...] = coord1_held[...].astype(f32).T.astype(bf16)
    for copy in copies[:5]:
        copy.wait()
    queries = jnp.dot(
        normed(jnp.concatenate(x[:-1], axis=1), ln_gain[...]),
        w_qkv[:, :width],
        preferred_element_type=f32,
    )
    head_mask = iota((heads, width), 1) // (width // heads) == iota((heads, width), 0)
    for i in range(own):
        spread = jnp.where(head_mask, jnp.broadcast_to(queries[i : i + 1], (heads, width)), 0.0)
        spread_queries[i * heads : (i + 1) * heads, :] = spread.astype(bf16)


def attend_kernel(dims, count, *refs):
    own, cols, width, heads, keys, kinds = dims
    pieces = refs[:count]
    bias, keyed, w_qkv, w_heads, ln_gain, w_coord2, coords = refs[count : count + 7]
    w_gauss, w_coord1, lookup, own_columns, kernels, attended, moved = refs[count + 7 : count + 14]
    logits, values, places, strengths = refs[count + 14 :]
    atoms = bias.shape[1]
    head_dim = width // heads
    each = lanes // pieces[0].shape[0]
    gain = ln_gain[...]
    select_at, select_from = iota((16, lanes), 0), iota((16, lanes), 1)
    selector = (
        ((select_from < 9) & (select_from % 3 == select_at) & (select_at < 3))
        | ((select_from == 9) & (select_at == 3))
    ).astype(f32).astype(bf16)
    centre, sharp, norming = kernels[0], kernels[1], kernels[2]

    for s in range(0, atoms, lanes):
        if each:
            first = s // lanes * each
            x = jnp.concatenate([ref[...] for ref in pieces[first : first + each]], axis=0)
        else:
            rows = pieces[0].shape[0]
            x = pieces[s // rows][s % rows : s % rows + lanes, :]
        table = lax.dot_general(selector, x[:, width:], nt, preferred_element_type=f32)
        places[:, s : s + lanes] = jnp.where(iota((16, lanes), 0) == 3, 1.0, table)
        offsets = [own_columns[c * 8 : c * 8 + own, :] - table[c : c + 1] for c in range(3)]
        squares = offsets[0] * offsets[0] + offsets[1] * offsets[1] + offsets[2] * offsets[2]
        distance = jnp.sqrt(squares + root_shift)
        key_onehot = (table[3:4].astype(jnp.int32) == iota((kinds, lanes), 0)).astype(f32).astype(bf16)
        found = jnp.dot(lookup[...], key_onehot, preferred_element_type=f32)
        scale = found[0:16] + found[16:32] + found[32:48]
        shift = found[48:64] + found[64:80] + found[80:96]
        expanded = scale[:own] * distance + shift[:own]
        features = []
        for i in range(own):
            scaled = (expanded[i : i + 1] - centre) * sharp
            features.append(jnp.exp2(norming - scaled * scaled).astype(bf16))
        hidden = jnp.dot(w_gauss[...], jnp.concatenate(features, axis=1), preferred_element_type=f32)
        geometry = jnp.dot(w_heads[...], gelu(hidden).astype(bf16), preferred_element_type=f32)
        block = normed(x[:, :width], gain)
        values[s : s + lanes, :] = jnp.dot(
            block, w_qkv[:, 2 * width :], preferred_element_type=f32
        ).astype(bf16)
        affinity = lax.dot_general(keyed[...], block, nt, preferred_element_type=f32)
        here = bias[:, s : s + lanes].astype(f32)
        rows = []
        for i in range(own):
            at = slice(i * heads, (i + 1) * heads)
            row = here[at] + geometry[:, i * lanes : (i + 1) * lanes]
            row = row + affinity[at] * (1.0 / math.sqrt(head_dim))
            logits[at, s : s + lanes] = jnp.where(here[at] < masked_below, masked_fill, row)
            rows.append(row.astype(bf16))
        mixed = jnp.dot(w_coord1[...], jnp.concatenate(rows, axis=1), preferred_element_type=f32)
        strength = jnp.dot(w_coord2[...], gelu(mixed).astype(bf16), preferred_element_type=f32)
        strengths[:, s : s + lanes] = jnp.concatenate(
            [
                jnp.where(
                    here[i * heads : i * heads + 1] < masked_below,
                    0.0,
                    strength[:, i * lanes : (i + 1) * lanes],
                )
                for i in range(own)
            ],
            axis=0,
        )

    masked = logits[...]
    weights = jnp.exp(masked - jnp.max(masked, axis=1, keepdims=True))
    share = 1.0 / jnp.sum(weights, axis=1, keepdims=True)
    taken = jnp.dot(weights.astype(bf16), values[...], preferred_element_type=f32) * share
    head_mask = iota((heads, width), 1) // head_dim == iota((heads, width), 0)
    attended[...] = jnp.concatenate(
        [
            jnp.sum(
                jnp.where(head_mask, taken[i * heads : (i + 1) * heads], 0.0), axis=0, keepdims=True
            )
            for i in range(own)
        ],
        axis=0,
    ).astype(bf16)
    pulled = lax.dot_general(
        places[...],
        strengths[...],
        nt,
        precision=lax.Precision.HIGHEST,
        preferred_element_type=f32,
    )
    here = coords[...]
    moved[...] = here + (here * pulled[3:4] - pulled[0:3]) * (1.0 / atoms)


def exchange(x, step, distance):
    rows, cols = lax.axis_size("row"), lax.axis_size("col")
    pairs = [
        (r * cols + c, (r ^ step) * cols + (c ^ distance)) for r in range(rows) for c in range(cols)
    ]
    return lax.ppermute(x, ("row", "col"), pairs)


def shards(
    nodes,
    coords,
    atom_types,
    segment_ids,
    pair_mask,
    pair_bias,
    ln_gain,
    w_qkv,
    gauss_mul,
    gauss_add,
    gauss_mean,
    gauss_width,
    w_gauss,
    w_heads,
    w_coord1,
    w_coord2,
):
    cols, rows = lax.axis_size("col"), lax.axis_size("row")
    own, width = nodes.shape
    heads, queries, keys = pair_bias.shape
    kinds, gauss = gauss_mul.shape[0], gauss_mean.shape[0]
    atoms = own * rows * cols
    dims = (own, cols, width, heads, keys, kinds)
    bias_rows, mask_rows, first_rows, second_rows = sizes(dims)
    shape = jax.ShapeDtypeStruct
    params = pltpu.CompilerParams(vmem_limit_bytes=(16 if atoms <= 128 else 56) * 2**20)
    vmem, anywhere = pl.BlockSpec(memory_space=pltpu.VMEM), pl.BlockSpec(memory_space=pl.ANY)

    def call(kernel, name, out_shape, inputs, remote=(), scratch=()):
        single = not isinstance(out_shape, list)
        return pl.pallas_call(
            kernel,
            out_shape=out_shape,
            in_specs=[vmem] * len(inputs) + [anywhere] * len(remote),
            out_specs=vmem if single else [vmem] * len(out_shape),
            scratch_shapes=list(scratch),
            compiler_params=params,
            name=name,
        )(*inputs, *map(in_hbm, remote))

    sources = (
        nodes,
        coords,
        atom_types[None, :],
        segment_ids[None, :],
        pair_mask,
        pair_bias.transpose(1, 2, 0),
    )
    mine, kept = call(
        functools.partial(pack_kernel, dims),
        "pack",
        [
            shape((first_rows, lanes), bf16),
            shape((-(-(bias_rows + mask_rows) // 16) * 16, lanes), bf16),
        ],
        (),
        sources,
        [pltpu.VMEM(x.shape, x.dtype) for x in sources]
        + [pltpu.VMEM((cols, mask_rows, lanes), f32), pltpu.SemaphoreType.DMA((6,))],
    )
    order = (cols - 1, *range(1, cols - 1))
    other = exchange(mine, 1, 0)
    grouped = call(
        functools.partial(regroup_kernel, dims, order),
        "regroup",
        [shape((second_rows, lanes), bf16)] * (cols - 1),
        (mine, other),
    )
    received = [exchange(x, 1, k) for x, k in zip(grouped, order, strict=True)]
    near = call(
        functools.partial(gather_kernel, dims, order),
        "gather",
        shape((2 * own * cols, width + lanes), bf16),
        (mine, other, *received),
    )
    weights = (w_qkv, w_heads.T, ln_gain[None, :], w_coord2[None, :], coords)
    tables = (gauss_mul, gauss_add, gauss_mean[None, :], gauss_width[None, :], w_gauss, w_coord1)
    prepared = call(
        functools.partial(prepare_kernel, dims),
        "prepare",
        [shape(x.shape, x.dtype) for x in weights]
        + [
            shape((gauss, gauss), bf16),
            shape(w_coord1.shape, bf16),
            shape((own * heads, width), bf16),
            shape((96, kinds), bf16),
            shape((24, lanes), f32),
            shape((3, gauss, lanes), f32),
        ],
        (lax.optimization_barrier((mine, other))[0],),
        weights + tables,
        [pltpu.VMEM(x.shape, x.dtype) for x in tables] + [pltpu.SemaphoreType.DMA((11,))],
    )
    near, prepared = lax.optimization_barrier((near, prepared))
    w_qkv, w_heads, ln_gain, w_coord2, coords, w_gauss, w_coord1, spread_queries, lookup = prepared[:9]
    own_columns, kernels = prepared[9:]
    steps = [0] + [step + 1 for step in range(2, rows, 2)]
    pieces = [near] + [exchange(near, step, 0) for step in steps[1:]]
    bias, keyed = call(
        functools.partial(arrange_kernel, dims, order, steps),
        "arrange",
        [shape((own * heads, atoms), bf16), shape((own * heads, width), bf16)],
        (kept, *received, spread_queries, w_qkv),
    )
    attended, moved = call(
        functools.partial(attend_kernel, dims, len(pieces)),
        "attend",
        [shape((own, width), bf16), shape((3, own), f32)],
        (*pieces, bias, keyed, w_qkv, w_heads, ln_gain, w_coord2, coords)
        + (w_gauss, w_coord1, lookup, own_columns, kernels),
        (),
        [
            pltpu.VMEM((own * heads, atoms), f32),
            pltpu.VMEM((atoms, width), bf16),
            pltpu.VMEM((16, atoms), f32),
            pltpu.VMEM((own, atoms), f32),
        ],
    )
    return attended, moved


def solution(mesh):
    own, tile, whole = P(("row", "col")), P("row", "col"), P()
    in_specs = (
        P(("row", "col"), None),
        P(None, ("row", "col")),
        own,
        own,
        tile,
        P(None, "row", "col"),
    ) + (whole,) * 10
    out_specs = (P(("row", "col"), None), P(None, ("row", "col")))
    return jax.shard_map(shards, mesh=mesh, in_specs=in_specs, out_specs=out_specs, check_vma=False)
```

```python
import functools
import math

import jax
import jax.numpy as jnp
from jax import lax
from jax.experimental import pallas as pl
from jax.experimental.pallas import tpu as pltpu
from jax.sharding import PartitionSpec as P

ln_epsilon = 1e-05
masked_fill = -1000000000.0
masked_below = -100000000.0
root_shift = 0.01
lanes = 128
f32 = jnp.float32
bf16 = jnp.bfloat16
nt = (((1,), (1,)), ((), ()))
tn = (((0,), (0,)), ((), ()))


def split3(x):
    hi = x.astype(bf16).astype(f32)
    mid = (x - hi).astype(bf16).astype(f32)
    return hi, mid, x - hi - mid


def iota(shape, axis):
    return lax.broadcasted_iota(jnp.int32, shape, axis)


def column(row):
    n = row.shape[1]
    square = jnp.where(iota((n, n), 0) == iota((n, n), 1), jnp.broadcast_to(row, (n, n)), 0.0)
    return jnp.sum(square, axis=1, keepdims=True)


def gelu(x):
    inner = x * (0.7978845608028654 + 0.035677408136300125 * (x * x))
    return (0.5 * x) * (1.0 + jnp.tanh(inner))


table_rows = 16


def node_rows(width, own):
    return width // lanes * own


def sizes(dims):
    own, cols, width, heads, keys, kinds = dims
    bias_rows, mask_rows = own * keys * heads // lanes, own * keys // lanes
    first = table_rows + node_rows(width, own) + (cols - 1) * (bias_rows + mask_rows)
    second = bias_rows + table_rows + 2 * node_rows(width, own) + mask_rows
    return bias_rows, mask_rows, -(-first // 16) * 16, -(-second // 16) * 16


def in_hbm(x):
    return pltpu.with_memory_space_constraint(x, pltpu.HBM)


def fetch(sources, targets, semaphores):
    copies = [
        pltpu.make_async_copy(source, target, semaphores.at[n])
        for n, (source, target) in enumerate(zip(sources, targets, strict=True))
    ]
    for copy in copies:
        copy.start()
    return copies


def filled(blocks, rows):
    rest = rows - sum(block.shape[0] for block in blocks)
    return jnp.concatenate(blocks + ([jnp.zeros((rest, lanes), f32)] if rest else []), axis=0)


def pack_kernel(dims, *refs):
    own, cols, width, heads, keys, kinds = dims
    bias_rows, mask_rows, first_rows, second_rows = sizes(dims)
    sources, first, kept, held, masks, semaphores = refs[:6], refs[6], refs[7], refs[8:14], refs[14], refs[15]
    copies = fetch(sources, held, semaphores)
    nodes, coords, types, segments, mask, bias = held
    me = lax.axis_index("col")
    pairs, fold = own * keys, lanes // heads
    for copy in copies[:4]:
        copy.wait()
    high, middle, low = split3(coords[...])
    kind = (types[...] + kinds // 2 * segments[...]).astype(f32)
    blank = jnp.zeros((1, own), f32)
    table = jnp.concatenate([high, kind, low, blank, middle] + [blank] * 5, axis=0)
    table = jnp.concatenate([table, jnp.zeros((table_rows, lanes - own), f32)], axis=1)
    full = nodes[...].astype(f32)
    blocks = [table] + [full[:, b * lanes : (b + 1) * lanes] for b in range(width // lanes)]
    copies[4].wait()
    wide_mask = mask[...].astype(f32)
    for d in range(cols):
        row = jnp.concatenate([wide_mask[d * own + i : d * own + i + 1] for i in range(own)], axis=1)
        for n in range(mask_rows):
            masks[d, n : n + 1, :] = row[:, n * lanes : (n + 1) * lanes]
    start = (cols - 1) * bias_rows
    tail = filled(blocks + [masks[me ^ k] for k in range(1, cols)], first_rows - start)
    first[start:, :] = tail.astype(bf16)
    kept[bias_rows:, :] = filled([masks[me]], kept.shape[0] - bias_rows).astype(bf16)
    copies[5].wait()
    for k in range(cols):
        tile = bias[pl.ds((me ^ k) * own, own)].astype(f32).reshape(pairs, heads)
        wide = [tile[n * bias_rows : (n + 1) * bias_rows] for n in range(fold)]
        block = jnp.concatenate(wide, axis=1).astype(bf16)
        if k:
            first[(k - 1) * bias_rows : k * bias_rows, :] = block
        else:
            kept[:bias_rows, :] = block


def regroup_kernel(dims, order, mine, other, *outs):
    own, cols, width, heads, keys, kinds = dims
    bias_rows, mask_rows, first_rows, second_rows = sizes(dims)
    start, rows = (cols - 1) * bias_rows, table_rows + node_rows(width, own)
    here, there = mine[start:, :].astype(f32), other[start:, :].astype(f32)
    table = here[:table_rows] + pltpu.roll(there[:table_rows], own, 1)
    for n, k in enumerate(order):
        outs[n][:bias_rows, :] = other[(k - 1) * bias_rows : k * bias_rows, :]
        at = rows + (k - 1) * mask_rows
        tail = [table, here[table_rows:rows], there[table_rows:rows], there[at : at + mask_rows]]
        tail = filled(tail, second_rows - bias_rows)
        outs[n][bias_rows:, :] = tail.astype(bf16)


def gather_kernel(dims, order, mine, other, *refs):
    own, cols, width, heads, keys, kinds = dims
    bias_rows, mask_rows, first_rows, second_rows = sizes(dims)
    start, rows = (cols - 1) * bias_rows, node_rows(width, own)
    out = refs[cols - 1]
    here, there = mine[start:, :].astype(f32), other[start:, :].astype(f32)
    tails = [refs[order.index(k)][bias_rows:, :].astype(f32) for k in range(1, cols)]
    table = here[:table_rows] + pltpu.roll(there[:table_rows], own, 1)
    for k, tail in enumerate(tails, 1):
        table = table + pltpu.roll(tail[:table_rows], 2 * own * k, 1)
    out[:table_rows, :] = table.astype(bf16)
    blocks = [here[table_rows:], there[table_rows:]]
    for tail in tails:
        blocks += [tail[table_rows : table_rows + rows], tail[table_rows + rows :]]
    each = 2 * own * cols
    for b in range(width // lanes):
        taken = jnp.concatenate([block[b * own : (b + 1) * own] for block in blocks], axis=0)
        out[table_rows + b * each : table_rows + (b + 1) * each, :] = taken.astype(bf16)


def arrange_kernel(dims, order, steps, kept, *refs):
    own, cols, width, heads, keys, kinds = dims
    bias_rows, mask_rows, first_rows, second_rows = sizes(dims)
    received = [refs[order.index(k)] for k in range(1, cols)]
    spread_queries, w_qkv, out, keyed = refs[cols - 1 :]
    through_keys = lax.dot_general(
        spread_queries[...], w_qkv[:, width : 2 * width], nt, preferred_element_type=f32
    )
    keyed[...] = (through_keys * (1.0 / math.sqrt(width // heads))).astype(bf16)
    atoms = out.shape[1]
    fold = lanes // heads
    each = own // fold
    mask_at = table_rows + 2 * node_rows(width, own)
    per_row = 2 * own * cols
    r, c = lax.axis_index("row"), lax.axis_index("col")
    blocks = [
        jnp.concatenate([ref[b * keys : (b + 1) * keys, :] for ref in [kept] + received], axis=0)
        for b in range(each)
    ]
    tails = [kept[bias_rows:, :].astype(f32)[:mask_rows]]
    tails += [ref[bias_rows:, :].astype(f32)[mask_at : mask_at + mask_rows] for ref in received]
    masks = []
    for i in range(own):
        n, lane = i * keys // lanes, i * keys % lanes
        masks.append(jnp.concatenate([tail[n : n + 1, lane : lane + keys] for tail in tails], axis=1))
    masks = jnp.concatenate(masks + [jnp.zeros((16 - own, atoms), f32)], axis=0).astype(bf16)
    place = iota((atoms, 1), 0)
    atom = (c ^ (place // keys)) * keys + place % keys
    for s in range(0, atoms, lanes):
        slot = s + iota((1, lanes), 1)
        piece, inner = slot // per_row, slot % per_row
        step = jnp.zeros((1, lanes), jnp.int32)
        for n, value in enumerate(steps):
            step = jnp.where(piece == n, value, step)
        distance = inner // (2 * own)
        row = r ^ step ^ (inner // own % 2) ^ (distance > 0).astype(jnp.int32)
        source = (row * cols + (c ^ distance)) * own + inner % own
        chosen = (atom == source).astype(f32).astype(bf16)
        valid = jnp.dot(masks, chosen, preferred_element_type=f32)
        for b in range(each):
            moved = lax.dot_general(blocks[b], chosen, tn, preferred_element_type=f32)
            for a in range(fold):
                i = a * each + b
                taken = jnp.where(valid[i : i + 1] > 0.5, moved[a * heads : (a + 1) * heads], masked_fill)
                out[i * heads : (i + 1) * heads, s : s + lanes] = taken.astype(bf16)


def normed(x, gain):
    features = x.astype(f32)
    centred = features - jnp.mean(features, axis=1, keepdims=True)
    spread = jnp.mean(centred * centred, axis=1, keepdims=True)
    return (centred * lax.rsqrt(spread + ln_epsilon) * gain).astype(bf16)


def prepare_kernel(dims, mine, *refs):
    own, cols, width, heads, keys, kinds = dims
    bias_rows, mask_rows, first_rows, second_rows = sizes(dims)
    sources = refs[:11]
    w_qkv, w_heads, ln_gain, coords, w_gauss, w_coord1, w_coord2, spread_queries = refs[11:19]
    lookup, own_columns, kernels = refs[19:22]
    mul_held, add_held, mean_held, width_held, gauss_held, coord1_held, coord2_held = refs[22:29]
    semaphores = refs[29]
    copies = fetch(
        sources,
        (w_qkv, w_heads, ln_gain, coords, mul_held, add_held, mean_held, width_held)
        + (gauss_held, coord1_held, coord2_held),
        semaphores,
    )
    tail = mine[(cols - 1) * bias_rows :, :].astype(f32)
    table, rows = tail[:table_rows], tail[table_rows : table_rows + node_rows(width, own)]
    places = (table[0:3] + table[8:11]) + table[4:7]
    for c in range(3):
        own_columns[c * 8 : c * 8 + own, :] = jnp.broadcast_to(
            column(places[c : c + 1, :own]), (own, lanes)
        )
    own_kind = column(table[3:4, :own]).astype(jnp.int32)
    own_kind = jnp.concatenate([own_kind, jnp.zeros((16 - own, 1), jnp.int32)], axis=0)
    query_onehot = (own_kind == iota((16, kinds), 1)).astype(f32).astype(bf16)
    for copy in copies[4:]:
        copy.wait()
    inverse = 1.0 / column(width_held[...])
    gauss = inverse.shape[0]
    kernels[0] = jnp.broadcast_to(column(mean_held[...]), (gauss, lanes))
    kernels[1] = jnp.broadcast_to(inverse * math.sqrt(0.5 * math.log2(math.e)), (gauss, lanes))
    kernels[2] = jnp.broadcast_to(jnp.log2(inverse * (1.0 / math.sqrt(2.0 * math.pi))), (gauss, lanes))
    found = []
    for table in (mul_held, add_held):
        parts = [
            jnp.dot(query_onehot, part.astype(bf16), preferred_element_type=f32)
            for part in split3(table[...])
        ]
        found.append((parts[0] + parts[1] + parts[2])[:own])
    found = jnp.concatenate(found, axis=0)
    lookup[...] = jnp.concatenate([found, jnp.zeros((2 * own, lanes - kinds), f32)], axis=1)
    w_gauss[...] = gauss_held[...].astype(f32).T.astype(bf16)
    w_coord1[...] = coord1_held[...].astype(f32).T.astype(bf16)
    w_coord2[...] = jnp.broadcast_to(column(coord2_held[...].astype(f32)), (heads, lanes))
    for copy in copies[:4]:
        copy.wait()
    x = jnp.concatenate([rows[b * own : (b + 1) * own] for b in range(width // lanes)], axis=1)
    x = jnp.concatenate([x, jnp.zeros((16 - own, width), f32)], axis=0)
    queries = jnp.dot(normed(x, ln_gain[...]), w_qkv[:, :width], preferred_element_type=f32)
    head_mask = iota((heads, width), 1) // (width // heads) == iota((heads, width), 0)
    for i in range(own):
        spread = jnp.where(head_mask, jnp.broadcast_to(queries[i : i + 1], (heads, width)), 0.0)
        spread_queries[i * heads : (i + 1) * heads, :] = spread.astype(bf16)


def attend_kernel(dims, count, *refs):
    own, cols, width, heads, keys, kinds = dims
    pieces = refs[:count]
    bias, keyed, w_qkv, w_heads, ln_gain, coords = refs[count : count + 6]
    w_gauss, w_coord1, w_coord2, lookup, own_columns, kernels = refs[count + 6 : count + 12]
    attended, moved, logits, values, places, strengths = refs[count + 12 :]
    atoms = bias.shape[1]
    each = 2 * own * cols
    gain = ln_gain[...]
    centre, sharp, norming = kernels[0], kernels[1], kernels[2]
    found = lookup[...]

    for s in range(0, atoms, lanes):
        taken = pieces[s // each : (s + lanes) // each]
        table = jnp.concatenate([ref[:table_rows, :].astype(f32)[:, :each] for ref in taken], axis=1)
        place = (table[0:3] + table[8:11]) + table[4:7]
        places[0:3, s : s + lanes] = place
        offsets = [own_columns[c * 8 : c * 8 + own, :] - place[c : c + 1] for c in range(3)]
        squares = offsets[0] * offsets[0] + offsets[1] * offsets[1] + offsets[2] * offsets[2]
        distance = jnp.sqrt(squares + root_shift)
        kind = jnp.broadcast_to(table[3:4].astype(jnp.int32), (2 * own, lanes))
        pair = jnp.take_along_axis(found, kind, axis=1)
        expanded = pair[:own] * distance + pair[own:]
        features = []
        for i in range(own):
            scaled = (expanded[i : i + 1] - centre) * sharp
            features.append(jnp.exp2(norming - scaled * scaled).astype(bf16))
        hidden = jnp.dot(w_gauss[...], jnp.concatenate(features, axis=1), preferred_element_type=f32)
        geometry = jnp.dot(w_heads[...], gelu(hidden).astype(bf16), preferred_element_type=f32)
        x = [
            jnp.concatenate(
                [
                    ref[table_rows + b * each : table_rows + (b + 1) * each, :]
                    for b in range(width // lanes)
                ],
                axis=1,
            )
            for ref in taken
        ]
        block = normed(jnp.concatenate(x, axis=0), gain)
        values[s : s + lanes, :] = jnp.dot(
            block, w_qkv[:, 2 * width :], preferred_element_type=f32
        ).astype(bf16)
        affinity = lax.dot_general(keyed[...], block, nt, preferred_element_type=f32)
        here = bias[:, s : s + lanes].astype(f32)
        rows = []
        for i in range(own):
            at = slice(i * heads, (i + 1) * heads)
            row = (here[at] + affinity[at]) + geometry[:, i * lanes : (i + 1) * lanes]
            logits[at, s : s + lanes] = jnp.where(here[at] < masked_below, masked_fill, row)
            rows.append(row.astype(bf16))
        mixed = jnp.dot(w_coord1[...], jnp.concatenate(rows, axis=1), preferred_element_type=f32)
        mixed = gelu(mixed)
        for i in range(own):
            strength = jnp.sum(
                mixed[:, i * lanes : (i + 1) * lanes] * w_coord2[...], axis=0, keepdims=True
            )
            masked = here[i * heads : i * heads + 1] < masked_below
            strengths[i : i + 1, s : s + lanes] = jnp.where(masked, 0.0, strength)

    masked = logits[...]
    weights = jnp.exp(masked - jnp.max(masked, axis=1, keepdims=True))
    share = 1.0 / jnp.sum(weights, axis=1, keepdims=True)
    taken = jnp.dot(weights.astype(bf16), values[...], preferred_element_type=f32) * share
    head_mask = iota((heads, width), 1) // (width // heads) == iota((heads, width), 0)
    attended[...] = jnp.concatenate(
        [
            jnp.sum(
                jnp.where(head_mask, taken[i * heads : (i + 1) * heads], 0.0), axis=0, keepdims=True
            )
            for i in range(own)
        ],
        axis=0,
    ).astype(bf16)
    here = coords[...]
    shift = jnp.zeros((3, own), f32)
    for i in range(own):
        pulls = (here[:, i : i + 1] - places[0:3, :]) * strengths[i : i + 1, :]
        shift = jnp.where(iota((3, own), 1) == i, jnp.sum(pulls, axis=1, keepdims=True), shift)
    moved[...] = here + shift * (1.0 / atoms)


def exchange(x, step, distance):
    rows, cols = lax.axis_size("row"), lax.axis_size("col")
    pairs = [
        (r * cols + c, (r ^ step) * cols + (c ^ distance)) for r in range(rows) for c in range(cols)
    ]
    return lax.ppermute(x, ("row", "col"), pairs)


def shards(
    nodes,
    coords,
    atom_types,
    segment_ids,
    pair_mask,
    pair_bias,
    ln_gain,
    w_qkv,
    gauss_mul,
    gauss_add,
    gauss_mean,
    gauss_width,
    w_gauss,
    w_heads,
    w_coord1,
    w_coord2,
):
    cols, rows = lax.axis_size("col"), lax.axis_size("row")
    own, width = nodes.shape
    heads, queries, keys = pair_bias.shape
    kinds, gauss = gauss_mul.shape[0], gauss_mean.shape[0]
    atoms = own * rows * cols
    dims = (own, cols, width, heads, keys, kinds)
    bias_rows, mask_rows, first_rows, second_rows = sizes(dims)
    shape = jax.ShapeDtypeStruct
    params = pltpu.CompilerParams(vmem_limit_bytes=(16 if atoms <= 128 else 56) * 2**20)
    vmem, anywhere = pl.BlockSpec(memory_space=pltpu.VMEM), pl.BlockSpec(memory_space=pl.ANY)

    def call(kernel, name, out_shape, inputs, remote=(), scratch=()):
        single = not isinstance(out_shape, list)
        return pl.pallas_call(
            kernel,
            out_shape=out_shape,
            in_specs=[vmem] * len(inputs) + [anywhere] * len(remote),
            out_specs=vmem if single else [vmem] * len(out_shape),
            scratch_shapes=list(scratch),
            compiler_params=params,
            name=name,
        )(*inputs, *map(in_hbm, remote))

    sources = (
        nodes,
        coords,
        atom_types[None, :],
        segment_ids[None, :],
        pair_mask,
        pair_bias.transpose(1, 2, 0),
    )
    mine, kept = call(
        functools.partial(pack_kernel, dims),
        "pack",
        [
            shape((first_rows, lanes), bf16),
            shape((-(-(bias_rows + mask_rows) // 16) * 16, lanes), bf16),
        ],
        (),
        sources,
        [pltpu.VMEM(x.shape, x.dtype) for x in sources]
        + [pltpu.VMEM((cols, mask_rows, lanes), f32), pltpu.SemaphoreType.DMA((6,))],
    )
    order = (cols - 1, *range(1, cols - 1))
    other = exchange(mine, 1, 0)
    grouped = call(
        functools.partial(regroup_kernel, dims, order),
        "regroup",
        [shape((second_rows, lanes), bf16)] * (cols - 1),
        (mine, other),
    )
    received = [exchange(x, 1, k) for x, k in zip(grouped, order, strict=True)]
    near = call(
        functools.partial(gather_kernel, dims, order),
        "gather",
        shape((table_rows + 2 * node_rows(width, own) * cols, lanes), bf16),
        (mine, other, *received),
    )
    weights = (w_qkv, w_heads.T, ln_gain[None, :], coords)
    tables = (gauss_mul, gauss_add, gauss_mean[None, :], gauss_width[None, :], w_gauss, w_coord1)
    tables += (w_coord2[None, :],)
    prepared = call(
        functools.partial(prepare_kernel, dims),
        "prepare",
        [shape(x.shape, x.dtype) for x in weights]
        + [
            shape((gauss, gauss), bf16),
            shape(w_coord1.shape, bf16),
            shape((heads, lanes), f32),
            shape((own * heads, width), bf16),
            shape((2 * own, lanes), f32),
            shape((24, lanes), f32),
            shape((3, gauss, lanes), f32),
        ],
        (lax.optimization_barrier((mine, other))[0],),
        weights + tables,
        [pltpu.VMEM(x.shape, x.dtype) for x in tables] + [pltpu.SemaphoreType.DMA((11,))],
    )
    near, prepared = lax.optimization_barrier((near, prepared))
    w_qkv, w_heads, ln_gain, coords, w_gauss, w_coord1, w_coord2, spread_queries = prepared[:8]
    lookup, own_columns, kernels = prepared[8:]
    steps = [0] + [step + 1 for step in range(2, rows, 2)]
    pieces = [near] + [exchange(near, step, 0) for step in steps[1:]]
    bias, keyed = call(
        functools.partial(arrange_kernel, dims, order, steps),
        "arrange",
        [shape((own * heads, atoms), bf16), shape((own * heads, width), bf16)],
        (kept, *received, spread_queries, w_qkv),
    )
    attended, moved = call(
        functools.partial(attend_kernel, dims, len(pieces)),
        "attend",
        [shape((own, width), bf16), shape((3, own), f32)],
        (*pieces, bias, keyed, w_qkv, w_heads, ln_gain, coords)
        + (w_gauss, w_coord1, w_coord2, lookup, own_columns, kernels),
        (),
        [
            pltpu.VMEM((own * heads, atoms), f32),
            pltpu.VMEM((atoms, width), bf16),
            pltpu.VMEM((8, atoms), f32),
            pltpu.VMEM((8, atoms), f32),
        ],
    )
    return attended, moved


def solution(mesh):
    own, tile, whole = P(("row", "col")), P("row", "col"), P()
    in_specs = (
        P(("row", "col"), None),
        P(None, ("row", "col")),
        own,
        own,
        tile,
        P(None, "row", "col"),
    ) + (whole,) * 10
    out_specs = (P(("row", "col"), None), P(None, ("row", "col")))
    return jax.shard_map(shards, mesh=mesh, in_specs=in_specs, out_specs=out_specs, check_vma=False)
```

```python
import functools
import math

import jax
import jax.numpy as jnp
from jax import lax
from jax.experimental import pallas as pl
from jax.experimental.pallas import tpu as pltpu
from jax.sharding import PartitionSpec as P

ln_epsilon = 1e-05
masked_fill = -1000000000.0
masked_below = -100000000.0
root_shift = 0.01
lanes = 128
f32 = jnp.float32
bf16 = jnp.bfloat16
nt = (((1,), (1,)), ((), ()))
tn = (((0,), (0,)), ((), ()))


def split3(x):
    hi = x.astype(bf16).astype(f32)
    mid = (x - hi).astype(bf16).astype(f32)
    return hi, mid, x - hi - mid


def iota(shape, axis):
    return lax.broadcasted_iota(jnp.int32, shape, axis)


def column(row):
    n = row.shape[1]
    square = jnp.where(iota((n, n), 0) == iota((n, n), 1), jnp.broadcast_to(row, (n, n)), 0.0)
    return jnp.sum(square, axis=1, keepdims=True)


def gelu(x):
    inner = x * (0.7978845608028654 + 0.035677408136300125 * (x * x))
    return (0.5 * x) * (1.0 + jnp.tanh(inner))


table_rows, table_used = 16, 11


def node_rows(width, own):
    return width // lanes * own


def sizes(dims):
    own, cols, width, heads, keys, kinds = dims
    bias_rows, mask_rows = own * keys * heads // lanes, own * keys // lanes
    first = table_rows + node_rows(width, own) + (cols - 1) * (bias_rows + mask_rows)
    wide_table = -(-(table_used + 2 * mask_rows) // 16) * 16
    second = 2 * bias_rows + wide_table + 2 * node_rows(width, own)
    return bias_rows, mask_rows, -(-first // 16) * 16, wide_table, second


def paired(steps):
    return [(steps[n + 1], steps[n]) for n in range(0, len(steps) - 1, 2)] + [(steps[-1], steps[-1])]


def sources(transfers):
    direct = [(odd, even, 1) for even, odd in transfers]
    return [(0, 0, 0)] + direct + [(even, odd, 0) for even, odd in transfers[:-1]]


def in_hbm(x):
    return pltpu.with_memory_space_constraint(x, pltpu.HBM)


def fetch(sources, targets, semaphores):
    copies = [
        pltpu.make_async_copy(source, target, semaphores.at[n])
        for n, (source, target) in enumerate(zip(sources, targets, strict=True))
    ]
    for copy in copies:
        copy.start()
    return copies


def filled(blocks, rows):
    rest = rows - sum(block.shape[0] for block in blocks)
    return jnp.concatenate(blocks + ([jnp.zeros((rest, lanes), f32)] if rest else []), axis=0)


def pack_kernel(dims, *refs):
    own, cols, width, heads, keys, kinds = dims
    bias_rows, mask_rows, first_rows, wide_table, second_rows = sizes(dims)
    first, kept, held, masks, semaphores = refs[6], refs[7], refs[8:14], refs[14], refs[15]
    copies = fetch(refs[:6], held, semaphores)
    nodes, coords, types, segments, mask, bias = held
    me = lax.axis_index("col")
    pairs, fold = own * keys, lanes // heads
    for copy in copies[:4]:
        copy.wait()
    high, middle, low = split3(coords[...])
    kind = (types[...] + kinds // 2 * segments[...]).astype(f32)
    blank = jnp.zeros((1, own), f32)
    table = jnp.concatenate([high, kind, low, blank, middle] + [blank] * 5, axis=0)
    table = jnp.concatenate([table, jnp.zeros((table_rows, lanes - own), f32)], axis=1)
    full = nodes[...].astype(f32)
    blocks = [table] + [full[:, b * lanes : (b + 1) * lanes] for b in range(width // lanes)]
    copies[4].wait()
    wide_mask = mask[...].astype(f32)
    for d in range(cols):
        row = jnp.concatenate([wide_mask[d * own + i : d * own + i + 1] for i in range(own)], axis=1)
        for n in range(mask_rows):
            masks[d, n : n + 1, :] = row[:, n * lanes : (n + 1) * lanes]
    start = (cols - 1) * bias_rows
    tail = filled(blocks + [masks[(me + k) % cols] for k in range(1, cols)], first_rows - start)
    first[start:, :] = tail.astype(bf16)
    kept[bias_rows:, :] = filled([masks[me]], kept.shape[0] - bias_rows).astype(bf16)
    copies[5].wait()
    for k in range(cols):
        tile = bias[pl.ds((me + k) % cols * own, own)].astype(f32).reshape(pairs, heads)
        wide = [tile[n * bias_rows : (n + 1) * bias_rows] for n in range(fold)]
        block = jnp.concatenate(wide, axis=1).astype(bf16)
        if k:
            first[(k - 1) * bias_rows : k * bias_rows, :] = block
        else:
            kept[:bias_rows, :] = block


def regroup_kernel(dims, transfers, mine, other, *outs):
    own, cols, width, heads, keys, kinds = dims
    bias_rows, mask_rows, first_rows, wide_table, second_rows = sizes(dims)
    odd = lax.axis_index("row") % 2 == 1
    start, rows = (cols - 1) * bias_rows, table_rows + node_rows(width, own)
    here, there = mine[start:, :].astype(f32), other[start:, :].astype(f32)
    table = (here[:table_rows] + pltpu.roll(there[:table_rows], own, 1))[:table_used]
    nodes = [here[table_rows:rows], there[table_rows:rows]]
    for out, (for_even, for_odd) in zip(outs, transfers, strict=True):

        def chosen(x, first, count):
            even_block = x[first + (for_even - 1) * count : first + for_even * count]
            if for_even == for_odd:
                return even_block
            return jnp.where(odd, x[first + (for_odd - 1) * count : first + for_odd * count], even_block)

        for n, ref in enumerate((mine, other)):
            out[n * bias_rows : (n + 1) * bias_rows, :] = chosen(ref, 0, bias_rows)
        masks = [chosen(x, rows, mask_rows) for x in (here, there)]
        tail = filled([table] + masks, wide_table)
        out[2 * bias_rows :, :] = jnp.concatenate([tail] + nodes, axis=0).astype(bf16)


def gather_kernel(dims, mine, other, *refs):
    own, cols, width, heads, keys, kinds = dims
    bias_rows, mask_rows, first_rows, wide_table, second_rows = sizes(dims)
    start, rows = (cols - 1) * bias_rows, node_rows(width, own)
    out = refs[cols - 1]
    here, there = mine[start:, :].astype(f32), other[start:, :].astype(f32)
    tails = [ref[2 * bias_rows :, :].astype(f32) for ref in refs[: cols - 1]]
    table = here[:table_rows] + pltpu.roll(there[:table_rows], own, 1)
    for k, tail in enumerate(tails, 1):
        part = jnp.where(iota((table_rows, lanes), 0) < table_used, tail[:table_rows], 0.0)
        table = table + pltpu.roll(part, 2 * own * k, 1)
    out[:table_rows, :] = table.astype(bf16)
    blocks = [here[table_rows:], there[table_rows:]]
    for tail in tails:
        blocks += [tail[wide_table : wide_table + rows], tail[wide_table + rows :]]
    each = 2 * own * cols
    for b in range(width // lanes):
        taken = jnp.concatenate([block[b * own : (b + 1) * own] for block in blocks], axis=0)
        out[table_rows + b * each : table_rows + (b + 1) * each, :] = taken.astype(bf16)


def normed(x, gain):
    features = x.astype(f32)
    centred = features - jnp.mean(features, axis=1, keepdims=True)
    spread = jnp.mean(centred * centred, axis=1, keepdims=True)
    return (centred * lax.rsqrt(spread + ln_epsilon) * gain).astype(bf16)


def arrange_kernel(dims, column_parts, row_parts, mine, kept, *refs):
    own, cols, width, heads, keys, kinds = dims
    bias_rows, mask_rows, first_rows, wide_table, second_rows = sizes(dims)
    received = refs[: cols - 1]
    ln_gain, w_source, out, keyed, w_qkv, semaphores = refs[cols - 1 :]
    copies = fetch((w_source,), (w_qkv,), semaphores)
    atoms = out.shape[1]
    fold = lanes // heads
    each = own // fold
    per_row = 2 * own * cols
    r, c = lax.axis_index("row"), lax.axis_index("col")

    def by_core(odd, part):
        return jnp.where(odd, part[1], part[0])

    blocks, masks = [], []
    for b in range(each):
        rows = [kept[b * keys : (b + 1) * keys, :]]
        for ref, part in zip(received, column_parts[1:], strict=True):
            first = part[2] * bias_rows + b * keys
            rows.append(ref[first : first + keys, :])
        blocks.append(jnp.concatenate(rows, axis=0))
    tails = [kept[bias_rows:, :].astype(f32)[:mask_rows]]
    for ref, part in zip(received, column_parts[1:], strict=True):
        first = table_used + part[2] * mask_rows
        tails.append(ref[2 * bias_rows : 2 * bias_rows + wide_table, :].astype(f32)[first : first + mask_rows])
    for i in range(own):
        n, lane = i * keys // lanes, i * keys % lanes
        masks.append(jnp.concatenate([tail[n : n + 1, lane : lane + keys] for tail in tails], axis=1))
    masks = jnp.concatenate(masks + [jnp.zeros((16 - own, atoms), f32)], axis=0).astype(bf16)
    place = iota((atoms, 1), 0)
    step = jnp.zeros((atoms, 1), jnp.int32)
    for n, part in enumerate(column_parts):
        step = jnp.where(place // keys == n, by_core(r % 2 == 1, part), step)
    atom = (c + cols - step) % cols * keys + place % keys
    for s in range(0, atoms, lanes):
        slot = s + iota((1, lanes), 1)
        piece, inner = slot // per_row, slot % per_row
        row = jnp.zeros((1, lanes), jnp.int32) + r
        for n, part in enumerate(row_parts):
            row = jnp.where(piece == n, r ^ by_core(r % 2 == 1, part), row)
        step, flip = jnp.zeros((1, lanes), jnp.int32), jnp.zeros((1, lanes), jnp.int32)
        for n, part in enumerate(column_parts):
            here = inner // (2 * own) == n
            step = jnp.where(here, by_core(row % 2 == 1, part), step)
            flip = jnp.where(here, part[2], flip)
        row = row ^ flip ^ (inner // own % 2)
        source = (row * cols + (c + cols - step) % cols) * own + inner % own
        chosen = (atom == source).astype(f32).astype(bf16)
        valid = jnp.dot(masks, chosen, preferred_element_type=f32)
        for b in range(each):
            moved = lax.dot_general(blocks[b], chosen, tn, preferred_element_type=f32)
            for a in range(fold):
                i = a * each + b
                taken = jnp.where(valid[i : i + 1] > 0.5, moved[a * heads : (a + 1) * heads], masked_fill)
                out[i * heads : (i + 1) * heads, s : s + lanes] = taken.astype(bf16)
    rows = mine[(cols - 1) * bias_rows :, :].astype(f32)[table_rows : table_rows + node_rows(width, own)]
    x = jnp.concatenate([rows[b * own : (b + 1) * own] for b in range(width // lanes)], axis=1)
    x = normed(jnp.concatenate([x, jnp.zeros((16 - own, width), f32)], axis=0), ln_gain[...])
    copies[0].wait()
    queries = jnp.dot(x, w_qkv[:, :width], preferred_element_type=f32)
    head_mask = iota((heads, width), 1) // (width // heads) == iota((heads, width), 0)
    spread = [
        jnp.where(head_mask, jnp.broadcast_to(queries[i : i + 1], (heads, width)), 0.0)
        for i in range(own)
    ]
    spread = jnp.concatenate(spread, axis=0).astype(bf16)
    through_keys = lax.dot_general(
        spread, w_qkv[:, width : 2 * width], nt, preferred_element_type=f32
    )
    keyed[...] = (through_keys * (1.0 / math.sqrt(width // heads))).astype(bf16)


def prepare_kernel(dims, mine, *refs):
    own, cols, width, heads, keys, kinds = dims
    bias_rows, mask_rows, first_rows, wide_table, second_rows = sizes(dims)
    w_heads, ln_gain, coords, w_gauss, w_coord1, w_coord2 = refs[10:16]
    lookup, own_columns, kernels = refs[16:19]
    mul_held, add_held, mean_held, width_held, gauss_held, coord1_held, coord2_held = refs[19:26]
    copies = fetch(
        refs[:10],
        (w_heads, ln_gain, coords, mul_held, add_held, mean_held, width_held)
        + (gauss_held, coord1_held, coord2_held),
        refs[26],
    )
    table = mine[(cols - 1) * bias_rows :, :].astype(f32)[:table_rows]
    places = (table[0:3] + table[8:11]) + table[4:7]
    for c in range(3):
        own_columns[c * 8 : c * 8 + own, :] = jnp.broadcast_to(
            column(places[c : c + 1, :own]), (own, lanes)
        )
    own_kind = column(table[3:4, :own]).astype(jnp.int32)
    own_kind = jnp.concatenate([own_kind, jnp.zeros((16 - own, 1), jnp.int32)], axis=0)
    query_onehot = (own_kind == iota((16, kinds), 1)).astype(f32).astype(bf16)
    for copy in copies:
        copy.wait()
    inverse = 1.0 / column(width_held[...])
    gauss = inverse.shape[0]
    kernels[0] = jnp.broadcast_to(column(mean_held[...]), (gauss, lanes))
    kernels[1] = jnp.broadcast_to(inverse * math.sqrt(0.5 * math.log2(math.e)), (gauss, lanes))
    kernels[2] = jnp.broadcast_to(jnp.log2(inverse * (1.0 / math.sqrt(2.0 * math.pi))), (gauss, lanes))
    found = []
    for table in (mul_held, add_held):
        parts = [
            jnp.dot(query_onehot, part.astype(bf16), preferred_element_type=f32)
            for part in split3(table[...])
        ]
        found.append((parts[0] + parts[1] + parts[2])[:own])
    found = jnp.concatenate(found, axis=0)
    lookup[...] = jnp.concatenate([found, jnp.zeros((2 * own, lanes - kinds), f32)], axis=1)
    w_gauss[...] = gauss_held[...].astype(f32).T.astype(bf16)
    w_coord1[...] = coord1_held[...].astype(f32).T.astype(bf16)
    w_coord2[...] = jnp.broadcast_to(column(coord2_held[...].astype(f32)), (heads, lanes))


def attend_kernel(dims, count, *refs):
    own, cols, width, heads, keys, kinds = dims
    pieces = refs[:count]
    bias, keyed, w_qkv, w_heads, ln_gain, coords = refs[count : count + 6]
    w_gauss, w_coord1, w_coord2, lookup, own_columns, kernels = refs[count + 6 : count + 12]
    attended, moved, logits, values, places, strengths = refs[count + 12 :]
    atoms = bias.shape[1]
    each = 2 * own * cols
    gain = ln_gain[...]
    centre, sharp, norming = kernels[0], kernels[1], kernels[2]
    found = lookup[...]

    for s in range(0, atoms, lanes):
        taken = pieces[s // each : (s + lanes) // each]
        table = jnp.concatenate([ref[:table_rows, :].astype(f32)[:, :each] for ref in taken], axis=1)
        place = (table[0:3] + table[8:11]) + table[4:7]
        places[0:3, s : s + lanes] = place
        offsets = [own_columns[c * 8 : c * 8 + own, :] - place[c : c + 1] for c in range(3)]
        squares = offsets[0] * offsets[0] + offsets[1] * offsets[1] + offsets[2] * offsets[2]
        distance = jnp.sqrt(squares + root_shift)
        kind = jnp.broadcast_to(table[3:4].astype(jnp.int32), (2 * own, lanes))
        pair = jnp.take_along_axis(found, kind, axis=1)
        expanded = pair[:own] * distance + pair[own:]
        features = []
        for i in range(own):
            scaled = (expanded[i : i + 1] - centre) * sharp
            features.append(jnp.exp2(norming - scaled * scaled).astype(bf16))
        hidden = jnp.dot(w_gauss[...], jnp.concatenate(features, axis=1), preferred_element_type=f32)
        geometry = jnp.dot(w_heads[...], gelu(hidden).astype(bf16), preferred_element_type=f32)
        x = [
            jnp.concatenate(
                [
                    ref[table_rows + b * each : table_rows + (b + 1) * each, :]
                    for b in range(width // lanes)
                ],
                axis=1,
            )
            for ref in taken
        ]
        block = normed(jnp.concatenate(x, axis=0), gain)
        values[s : s + lanes, :] = jnp.dot(
            block, w_qkv[:, 2 * width :], preferred_element_type=f32
        ).astype(bf16)
        affinity = lax.dot_general(keyed[...], block, nt, preferred_element_type=f32)
        here = bias[:, s : s + lanes].astype(f32)
        rows = []
        for i in range(own):
            at = slice(i * heads, (i + 1) * heads)
            row = (here[at] + affinity[at]) + geometry[:, i * lanes : (i + 1) * lanes]
            logits[at, s : s + lanes] = jnp.where(here[at] < masked_below, masked_fill, row)
            rows.append(row.astype(bf16))
        mixed = jnp.dot(w_coord1[...], jnp.concatenate(rows, axis=1), preferred_element_type=f32)
        mixed = gelu(mixed)
        for i in range(own):
            strength = jnp.sum(
                mixed[:, i * lanes : (i + 1) * lanes] * w_coord2[...], axis=0, keepdims=True
            )
            masked = here[i * heads : i * heads + 1] < masked_below
            strengths[i : i + 1, s : s + lanes] = jnp.where(masked, 0.0, strength)

    masked = logits[...]
    weights = jnp.exp(masked - jnp.max(masked, axis=1, keepdims=True))
    share = 1.0 / jnp.sum(weights, axis=1, keepdims=True)
    taken = jnp.dot(weights.astype(bf16), values[...], preferred_element_type=f32) * share
    head_mask = iota((heads, width), 1) // (width // heads) == iota((heads, width), 0)
    attended[...] = jnp.concatenate(
        [
            jnp.sum(
                jnp.where(head_mask, taken[i * heads : (i + 1) * heads], 0.0), axis=0, keepdims=True
            )
            for i in range(own)
        ],
        axis=0,
    ).astype(bf16)
    here = coords[...]
    shift = jnp.zeros((3, own), f32)
    for i in range(own):
        pulls = (here[:, i : i + 1] - places[0:3, :]) * strengths[i : i + 1, :]
        shift = jnp.where(iota((3, own), 1) == i, jnp.sum(pulls, axis=1, keepdims=True), shift)
    moved[...] = here + shift * (1.0 / atoms)


def exchange(x, steps, distances):
    rows, cols = lax.axis_size("row"), lax.axis_size("col")
    pairs = [
        (r * cols + c, (r ^ steps[r % 2]) * cols + (c + distances[r % 2]) % cols)
        for r in range(rows)
        for c in range(cols)
    ]
    return lax.ppermute(x, ("row", "col"), pairs)


def shards(
    nodes,
    coords,
    atom_types,
    segment_ids,
    pair_mask,
    pair_bias,
    ln_gain,
    w_qkv,
    gauss_mul,
    gauss_add,
    gauss_mean,
    gauss_width,
    w_gauss,
    w_heads,
    w_coord1,
    w_coord2,
):
    cols, rows = lax.axis_size("col"), lax.axis_size("row")
    own, width = nodes.shape
    heads, queries, keys = pair_bias.shape
    kinds, gauss = gauss_mul.shape[0], gauss_mean.shape[0]
    atoms = own * rows * cols
    dims = (own, cols, width, heads, keys, kinds)
    bias_rows, mask_rows, first_rows, wide_table, second_rows = sizes(dims)
    near_step, still = (1, 1), (0, 0)
    along_col = paired(list(range(1, cols)))
    along_row = [(even, odd) for odd, even in paired(list(range(3, rows, 2)))]
    column_parts, row_parts = sources(along_col), sources(along_row)
    row_parts = [(even ^ (1 - other), odd ^ (1 - other), other) if n else (0, 0, 0) for n, (even, odd, other) in enumerate(row_parts)]
    shape = jax.ShapeDtypeStruct
    params = pltpu.CompilerParams(vmem_limit_bytes=(16 if atoms <= 128 else 56) * 2**20)
    vmem, anywhere = pl.BlockSpec(memory_space=pltpu.VMEM), pl.BlockSpec(memory_space=pl.ANY)

    def call(kernel, name, out_shape, inputs, remote=(), scratch=()):
        single = not isinstance(out_shape, list)
        return pl.pallas_call(
            kernel,
            out_shape=out_shape,
            in_specs=[vmem] * len(inputs) + [anywhere] * len(remote),
            out_specs=vmem if single else [vmem] * len(out_shape),
            scratch_shapes=list(scratch),
            compiler_params=params,
            name=name,
        )(*inputs, *map(in_hbm, remote))

    own_arrays = (
        nodes,
        coords,
        atom_types[None, :],
        segment_ids[None, :],
        pair_mask,
        pair_bias.transpose(1, 2, 0),
    )
    mine, kept = call(
        functools.partial(pack_kernel, dims),
        "pack",
        [
            shape((first_rows, lanes), bf16),
            shape((-(-(bias_rows + mask_rows) // 16) * 16, lanes), bf16),
        ],
        (),
        own_arrays,
        [pltpu.VMEM(x.shape, x.dtype) for x in own_arrays]
        + [pltpu.VMEM((cols, mask_rows, lanes), f32), pltpu.SemaphoreType.DMA((6,))],
    )
    other = exchange(mine, near_step, still)
    grouped = call(
        functools.partial(regroup_kernel, dims, along_col),
        "regroup",
        [shape((second_rows, lanes), bf16)] * len(along_col),
        (mine, other),
    )
    received = [exchange(x, near_step, shift) for x, shift in zip(grouped, along_col, strict=True)]
    small = (w_heads.T, ln_gain[None, :], coords)
    tables = (gauss_mul, gauss_add, gauss_mean[None, :], gauss_width[None, :], w_gauss, w_coord1)
    tables += (w_coord2[None, :],)
    prepared = call(
        functools.partial(prepare_kernel, dims),
        "prepare",
        [shape(x.shape, x.dtype) for x in small]
        + [
            shape((gauss, gauss), bf16),
            shape(w_coord1.shape, bf16),
            shape((heads, lanes), f32),
            shape((2 * own, lanes), f32),
            shape((24, lanes), f32),
            shape((3, gauss, lanes), f32),
        ],
        (lax.optimization_barrier((mine, grouped[0]))[0],),
        small + tables,
        [pltpu.VMEM(x.shape, x.dtype) for x in tables] + [pltpu.SemaphoreType.DMA((10,))],
    )
    received[0], prepared = lax.optimization_barrier((received[0], prepared))
    received += [exchange(x, near_step, still) for x in received[:-1]]
    w_heads, ln_gain, coords, w_gauss, w_coord1, w_coord2, lookup, own_columns, kernels = prepared
    near = call(
        functools.partial(gather_kernel, dims),
        "gather",
        shape((table_rows + 2 * node_rows(width, own) * cols, lanes), bf16),
        (mine, other, *received),
    )
    pieces = [near] + [exchange(near, step, still) for step in along_row]
    pieces += [exchange(x, near_step, still) for x in pieces[1 : len(along_row)]]
    bias, keyed, w_qkv = call(
        functools.partial(arrange_kernel, dims, column_parts, row_parts),
        "arrange",
        [
            shape((own * heads, atoms), bf16),
            shape((own * heads, width), bf16),
            shape(w_qkv.shape, bf16),
        ],
        (lax.optimization_barrier((mine, pieces[1]))[0], kept, *received, ln_gain),
        (w_qkv,),
        [pltpu.SemaphoreType.DMA((1,))],
    )
    attended, moved = call(
        functools.partial(attend_kernel, dims, len(pieces)),
        "attend",
        [shape((own, width), bf16), shape((3, own), f32)],
        (*pieces, bias, keyed, w_qkv, w_heads, ln_gain, coords)
        + (w_gauss, w_coord1, w_coord2, lookup, own_columns, kernels),
        (),
        [
            pltpu.VMEM((own * heads, atoms), f32),
            pltpu.VMEM((atoms, width), bf16),
            pltpu.VMEM((8, atoms), f32),
            pltpu.VMEM((8, atoms), f32),
        ],
    )
    return attended, moved


def solution(mesh):
    own, tile, whole = P(("row", "col")), P("row", "col"), P()
    in_specs = (
        P(("row", "col"), None),
        P(None, ("row", "col")),
        own,
        own,
        tile,
        P(None, "row", "col"),
    ) + (whole,) * 10
    out_specs = (P(("row", "col"), None), P(None, ("row", "col")))
    return jax.shard_map(shards, mesh=mesh, in_specs=in_specs, out_specs=out_specs, check_vma=False)
```

```python
import functools
import math

import jax
import jax.numpy as jnp
from jax import lax
from jax.experimental import pallas as pl
from jax.experimental.pallas import tpu as pltpu
from jax.sharding import PartitionSpec as P

ln_epsilon = 1e-05
masked_fill = -1000000000.0
masked_below = -100000000.0
root_shift = 0.01
lanes = 128
f32 = jnp.float32
bf16 = jnp.bfloat16
nt = (((1,), (1,)), ((), ()))
tn = (((0,), (0,)), ((), ()))


def split3(x):
    hi = x.astype(bf16).astype(f32)
    mid = (x - hi).astype(bf16).astype(f32)
    return hi, mid, x - hi - mid


def iota(shape, axis):
    return lax.broadcasted_iota(jnp.int32, shape, axis)


def column(row):
    n = row.shape[1]
    square = jnp.where(iota((n, n), 0) == iota((n, n), 1), jnp.broadcast_to(row, (n, n)), 0.0)
    return jnp.sum(square, axis=1, keepdims=True)


def gelu(x):
    inner = x * (0.7978845608028654 + 0.035677408136300125 * (x * x))
    return (0.5 * x) * (1.0 + jnp.tanh(inner))


table_rows, table_used = 16, 11


def node_rows(width, own):
    return width // lanes * own


def sizes(dims):
    own, cols, width, heads, keys, kinds = dims
    bias_rows, mask_rows = own * keys * heads // lanes, own * keys // lanes
    first = table_rows + node_rows(width, own) + (cols - 1) * (bias_rows + mask_rows)
    wide_table = -(-(table_used + 2 * mask_rows) // 16) * 16
    second = 2 * bias_rows + wide_table + 2 * node_rows(width, own)
    return bias_rows, mask_rows, -(-first // 16) * 16, wide_table, second


def paired(steps):
    return [(steps[n + 1], steps[n]) for n in range(0, len(steps) - 1, 2)] + [(steps[-1], steps[-1])]


def sources(transfers):
    direct = [(odd, even, 1) for even, odd in transfers]
    return [(0, 0, 0)] + direct + [(even, odd, 0) for even, odd in transfers[:-1]]


def in_hbm(x):
    return pltpu.with_memory_space_constraint(x, pltpu.HBM)


def fetch(sources, targets, semaphores):
    copies = [
        pltpu.make_async_copy(source, target, semaphores.at[n])
        for n, (source, target) in enumerate(zip(sources, targets, strict=True))
    ]
    for copy in copies:
        copy.start()
    return copies


def filled(blocks, rows):
    rest = rows - sum(block.shape[0] for block in blocks)
    return jnp.concatenate(blocks + ([jnp.zeros((rest, lanes), f32)] if rest else []), axis=0)


def normed(x, gain):
    features = x.astype(f32)
    centred = features - jnp.mean(features, axis=1, keepdims=True)
    spread = jnp.mean(centred * centred, axis=1, keepdims=True)
    return (centred * lax.rsqrt(spread + ln_epsilon) * gain).astype(bf16)


def pack_kernel(dims, *refs):
    own, cols, width, heads, keys, kinds = dims
    bias_rows, mask_rows, first_rows, wide_table, second_rows = sizes(dims)
    first, kept, held, masks, semaphores = refs[7], refs[8], refs[9:16], refs[16], refs[17]
    copies = fetch(refs[:7], held, semaphores)
    nodes, coords, types, segments, ln_gain, mask, bias = held
    me = lax.axis_index("col")
    pairs, fold = own * keys, lanes // heads
    for copy in copies[:5]:
        copy.wait()
    high, middle, low = split3(coords[...])
    kind = (types[...] + kinds // 2 * segments[...]).astype(f32)
    blank = jnp.zeros((1, own), f32)
    table = jnp.concatenate([high, kind, low, blank, middle] + [blank] * 5, axis=0)
    table = jnp.concatenate([table, jnp.zeros((table_rows, lanes - own), f32)], axis=1)
    full = normed(nodes[...], ln_gain[...]).astype(f32)
    blocks = [table] + [full[:, b * lanes : (b + 1) * lanes] for b in range(width // lanes)]
    copies[5].wait()
    wide_mask = mask[...].astype(f32)
    for d in range(cols):
        row = jnp.concatenate([wide_mask[d * own + i : d * own + i + 1] for i in range(own)], axis=1)
        for n in range(mask_rows):
            masks[d, n : n + 1, :] = row[:, n * lanes : (n + 1) * lanes]
    start = (cols - 1) * bias_rows
    tail = filled(blocks + [masks[(me + k) % cols] for k in range(1, cols)], first_rows - start)
    first[start:, :] = tail.astype(bf16)
    kept[bias_rows:, :] = filled([masks[me]], kept.shape[0] - bias_rows).astype(bf16)
    copies[6].wait()
    for k in range(cols):
        tile = bias[pl.ds((me + k) % cols * own, own)].astype(f32).reshape(pairs, heads)
        wide = [tile[n * bias_rows : (n + 1) * bias_rows] for n in range(fold)]
        block = jnp.concatenate(wide, axis=1).astype(bf16)
        if k:
            first[(k - 1) * bias_rows : k * bias_rows, :] = block
        else:
            kept[:bias_rows, :] = block


def regroup_kernel(dims, transfers, mine, other, *outs):
    own, cols, width, heads, keys, kinds = dims
    bias_rows, mask_rows, first_rows, wide_table, second_rows = sizes(dims)
    odd = lax.axis_index("row") % 2 == 1
    start, rows = (cols - 1) * bias_rows, table_rows + node_rows(width, own)
    here, there = mine[start:, :].astype(f32), other[start:, :].astype(f32)
    table = (here[:table_rows] + pltpu.roll(there[:table_rows], own, 1))[:table_used]
    nodes = [here[table_rows:rows], there[table_rows:rows]]
    for out, (for_even, for_odd) in zip(outs, transfers, strict=True):

        def chosen(x, first, count):
            even_block = x[first + (for_even - 1) * count : first + for_even * count]
            if for_even == for_odd:
                return even_block
            return jnp.where(odd, x[first + (for_odd - 1) * count : first + for_odd * count], even_block)

        for n, ref in enumerate((mine, other)):
            out[n * bias_rows : (n + 1) * bias_rows, :] = chosen(ref, 0, bias_rows)
        masks = [chosen(x, rows, mask_rows) for x in (here, there)]
        tail = filled([table] + masks, wide_table)
        out[2 * bias_rows :, :] = jnp.concatenate([tail] + nodes, axis=0).astype(bf16)


def gather_kernel(dims, mine, other, *refs):
    own, cols, width, heads, keys, kinds = dims
    bias_rows, mask_rows, first_rows, wide_table, second_rows = sizes(dims)
    start, rows = (cols - 1) * bias_rows, node_rows(width, own)
    out = refs[cols - 1]
    here, there = mine[start:, :].astype(f32), other[start:, :].astype(f32)
    tails = [ref[2 * bias_rows :, :].astype(f32) for ref in refs[: cols - 1]]
    table = here[:table_rows] + pltpu.roll(there[:table_rows], own, 1)
    for k, tail in enumerate(tails, 1):
        part = jnp.where(iota((table_rows, lanes), 0) < table_used, tail[:table_rows], 0.0)
        table = table + pltpu.roll(part, 2 * own * k, 1)
    out[:table_rows, :] = table.astype(bf16)
    blocks = [here[table_rows:], there[table_rows:]]
    for tail in tails:
        blocks += [tail[wide_table : wide_table + rows], tail[wide_table + rows :]]
    each = 2 * own * cols
    for b in range(width // lanes):
        taken = jnp.concatenate([block[b * own : (b + 1) * own] for block in blocks], axis=0)
        out[table_rows + b * each : table_rows + (b + 1) * each, :] = taken.astype(bf16)


def arrange_kernel(dims, column_parts, row_parts, mine, kept, *refs):
    own, cols, width, heads, keys, kinds = dims
    bias_rows, mask_rows, first_rows, wide_table, second_rows = sizes(dims)
    received = refs[: cols - 1]
    w_source, out, spread_queries, w_qkv, semaphores = refs[cols - 1 :]
    copies = fetch((w_source,), (w_qkv,), semaphores)
    atoms = out.shape[1]
    fold = lanes // heads
    each = own // fold
    per_row = 2 * own * cols
    r, c = lax.axis_index("row"), lax.axis_index("col")

    def by_core(odd, part):
        return jnp.where(odd, part[1], part[0])

    blocks, masks = [], []
    for b in range(each):
        rows = [kept[b * keys : (b + 1) * keys, :]]
        for ref, part in zip(received, column_parts[1:], strict=True):
            first = part[2] * bias_rows + b * keys
            rows.append(ref[first : first + keys, :])
        blocks.append(jnp.concatenate(rows, axis=0))
    tails = [kept[bias_rows:, :].astype(f32)[:mask_rows]]
    for ref, part in zip(received, column_parts[1:], strict=True):
        first = table_used + part[2] * mask_rows
        tails.append(ref[2 * bias_rows : 2 * bias_rows + wide_table, :].astype(f32)[first : first + mask_rows])
    for i in range(own):
        n, lane = i * keys // lanes, i * keys % lanes
        masks.append(jnp.concatenate([tail[n : n + 1, lane : lane + keys] for tail in tails], axis=1))
    masks = jnp.concatenate(masks + [jnp.zeros((16 - own, atoms), f32)], axis=0).astype(bf16)
    place = iota((atoms, 1), 0)
    step = jnp.zeros((atoms, 1), jnp.int32)
    for n, part in enumerate(column_parts):
        step = jnp.where(place // keys == n, by_core(r % 2 == 1, part), step)
    atom = (c + cols - step) % cols * keys + place % keys
    for s in range(0, atoms, lanes):
        slot = s + iota((1, lanes), 1)
        piece, inner = slot // per_row, slot % per_row
        row = jnp.zeros((1, lanes), jnp.int32) + r
        for n, part in enumerate(row_parts):
            row = jnp.where(piece == n, r ^ by_core(r % 2 == 1, part), row)
        step, flip = jnp.zeros((1, lanes), jnp.int32), jnp.zeros((1, lanes), jnp.int32)
        for n, part in enumerate(column_parts):
            here = inner // (2 * own) == n
            step = jnp.where(here, by_core(row % 2 == 1, part), step)
            flip = jnp.where(here, part[2], flip)
        row = row ^ flip ^ (inner // own % 2)
        source = (row * cols + (c + cols - step) % cols) * own + inner % own
        chosen = (atom == source).astype(f32).astype(bf16)
        valid = jnp.dot(masks, chosen, preferred_element_type=f32)
        for b in range(each):
            moved = lax.dot_general(blocks[b], chosen, tn, preferred_element_type=f32)
            for a in range(fold):
                i = a * each + b
                taken = jnp.where(valid[i : i + 1] > 0.5, moved[a * heads : (a + 1) * heads], masked_fill)
                out[i * heads : (i + 1) * heads, s : s + lanes] = taken.astype(bf16)
    rows = mine[(cols - 1) * bias_rows :, :].astype(f32)[table_rows : table_rows + node_rows(width, own)]
    x = jnp.concatenate([rows[b * own : (b + 1) * own] for b in range(width // lanes)], axis=1)
    x = jnp.concatenate([x, jnp.zeros((16 - own, width), f32)], axis=0).astype(bf16)
    copies[0].wait()
    queries = jnp.dot(x, w_qkv[:, :width], preferred_element_type=f32)
    head_mask = iota((heads, width), 1) // (width // heads) == iota((heads, width), 0)
    for i in range(own):
        spread = jnp.where(head_mask, jnp.broadcast_to(queries[i : i + 1], (heads, width)), 0.0)
        spread_queries[i * heads : (i + 1) * heads, :] = spread.astype(bf16)


def prepare_kernel(dims, mine, *refs):
    own, cols, width, heads, keys, kinds = dims
    bias_rows, mask_rows, first_rows, wide_table, second_rows = sizes(dims)
    w_heads, coords, w_gauss, w_coord1, w_coord2 = refs[9:14]
    lookup, own_columns, kernels = refs[14:17]
    mul_held, add_held, mean_held, width_held, gauss_held, coord1_held, coord2_held = refs[17:24]
    copies = fetch(
        refs[:9],
        (w_heads, coords, mul_held, add_held, mean_held, width_held)
        + (gauss_held, coord1_held, coord2_held),
        refs[24],
    )
    table = mine[(cols - 1) * bias_rows :, :].astype(f32)[:table_rows]
    places = (table[0:3] + table[8:11]) + table[4:7]
    for c in range(3):
        own_columns[c * 8 : c * 8 + own, :] = jnp.broadcast_to(
            column(places[c : c + 1, :own]), (own, lanes)
        )
    own_kind = column(table[3:4, :own]).astype(jnp.int32)
    own_kind = jnp.concatenate([own_kind, jnp.zeros((16 - own, 1), jnp.int32)], axis=0)
    query_onehot = (own_kind == iota((16, kinds), 1)).astype(f32).astype(bf16)
    for copy in copies:
        copy.wait()
    inverse = 1.0 / column(width_held[...])
    gauss = inverse.shape[0]
    kernels[0] = jnp.broadcast_to(column(mean_held[...]), (gauss, lanes))
    kernels[1] = jnp.broadcast_to(inverse * math.sqrt(0.5 * math.log2(math.e)), (gauss, lanes))
    kernels[2] = jnp.broadcast_to(jnp.log2(inverse * (1.0 / math.sqrt(2.0 * math.pi))), (gauss, lanes))
    found = []
    for table in (mul_held, add_held):
        parts = [
            jnp.dot(query_onehot, part.astype(bf16), preferred_element_type=f32)
            for part in split3(table[...])
        ]
        found.append((parts[0] + parts[1] + parts[2])[:own])
    found = jnp.concatenate(found, axis=0)
    lookup[...] = jnp.concatenate([found, jnp.zeros((2 * own, lanes - kinds), f32)], axis=1)
    w_gauss[...] = gauss_held[...].astype(f32).T.astype(bf16)
    w_coord1[...] = coord1_held[...].astype(f32).T.astype(bf16)
    w_coord2[...] = jnp.broadcast_to(column(coord2_held[...].astype(f32)), (heads, lanes))


def attend_kernel(dims, count, *refs):
    own, cols, width, heads, keys, kinds = dims
    pieces = refs[:count]
    bias, spread_queries, w_qkv, w_heads, coords = refs[count : count + 5]
    w_gauss, w_coord1, w_coord2, lookup, own_columns, kernels = refs[count + 5 : count + 11]
    attended, moved, logits, values, places, strengths = refs[count + 11 :]
    atoms = bias.shape[1]
    each = 2 * own * cols
    centre, sharp, norming = kernels[0], kernels[1], kernels[2]
    found = lookup[...]

    for s in range(0, atoms, lanes):
        taken = pieces[s // each : (s + lanes) // each]
        table = jnp.concatenate([ref[:table_rows, :].astype(f32)[:, :each] for ref in taken], axis=1)
        place = (table[0:3] + table[8:11]) + table[4:7]
        places[0:3, s : s + lanes] = place
        offsets = [own_columns[c * 8 : c * 8 + own, :] - place[c : c + 1] for c in range(3)]
        squares = offsets[0] * offsets[0] + offsets[1] * offsets[1] + offsets[2] * offsets[2]
        distance = jnp.sqrt(squares + root_shift)
        kind = jnp.broadcast_to(table[3:4].astype(jnp.int32), (2 * own, lanes))
        pair = jnp.take_along_axis(found, kind, axis=1)
        expanded = pair[:own] * distance + pair[own:]
        features = []
        for i in range(own):
            scaled = (expanded[i : i + 1] - centre) * sharp
            features.append(jnp.exp2(norming - scaled * scaled).astype(bf16))
        hidden = jnp.dot(w_gauss[...], jnp.concatenate(features, axis=1), preferred_element_type=f32)
        geometry = jnp.dot(w_heads[...], gelu(hidden).astype(bf16), preferred_element_type=f32)
        x = [
            jnp.concatenate(
                [
                    ref[table_rows + b * each : table_rows + (b + 1) * each, :]
                    for b in range(width // lanes)
                ],
                axis=1,
            )
            for ref in taken
        ]
        block = jnp.concatenate(x, axis=0)
        keys_here = jnp.dot(block, w_qkv[:, width : 2 * width], preferred_element_type=f32)
        affinity = lax.dot_general(
            spread_queries[...], keys_here.astype(bf16), nt, preferred_element_type=f32
        )
        values[s : s + lanes, :] = jnp.dot(
            block, w_qkv[:, 2 * width :], preferred_element_type=f32
        ).astype(bf16)
        here = bias[:, s : s + lanes].astype(f32)
        rows = []
        for i in range(own):
            at = slice(i * heads, (i + 1) * heads)
            row = here[at] + affinity[at] * (1.0 / math.sqrt(width // heads))
            row = row + geometry[:, i * lanes : (i + 1) * lanes]
            logits[at, s : s + lanes] = jnp.where(here[at] < masked_below, masked_fill, row)
            rows.append(row.astype(bf16))
        mixed = jnp.dot(w_coord1[...], jnp.concatenate(rows, axis=1), preferred_element_type=f32)
        mixed = gelu(mixed)
        for i in range(own):
            strength = jnp.sum(
                mixed[:, i * lanes : (i + 1) * lanes] * w_coord2[...], axis=0, keepdims=True
            )
            masked = here[i * heads : i * heads + 1] < masked_below
            strengths[i : i + 1, s : s + lanes] = jnp.where(masked, 0.0, strength)

    masked = logits[...]
    weights = jnp.exp(masked - jnp.max(masked, axis=1, keepdims=True))
    share = 1.0 / jnp.sum(weights, axis=1, keepdims=True)
    taken = jnp.dot(weights.astype(bf16), values[...], preferred_element_type=f32) * share
    head_mask = iota((heads, width), 1) // (width // heads) == iota((heads, width), 0)
    attended[...] = jnp.concatenate(
        [
            jnp.sum(
                jnp.where(head_mask, taken[i * heads : (i + 1) * heads], 0.0), axis=0, keepdims=True
            )
            for i in range(own)
        ],
        axis=0,
    ).astype(bf16)
    here = coords[...]
    shift = jnp.zeros((3, own), f32)
    for i in range(own):
        pulls = (here[:, i : i + 1] - places[0:3, :]) * strengths[i : i + 1, :]
        shift = jnp.where(iota((3, own), 1) == i, jnp.sum(pulls, axis=1, keepdims=True), shift)
    moved[...] = here + shift * (1.0 / atoms)


def exchange(x, steps, distances):
    rows, cols = lax.axis_size("row"), lax.axis_size("col")
    pairs = [
        (r * cols + c, (r ^ steps[r % 2]) * cols + (c + distances[r % 2]) % cols)
        for r in range(rows)
        for c in range(cols)
    ]
    return lax.ppermute(x, ("row", "col"), pairs)


def shards(
    nodes,
    coords,
    atom_types,
    segment_ids,
    pair_mask,
    pair_bias,
    ln_gain,
    w_qkv,
    gauss_mul,
    gauss_add,
    gauss_mean,
    gauss_width,
    w_gauss,
    w_heads,
    w_coord1,
    w_coord2,
):
    cols, rows = lax.axis_size("col"), lax.axis_size("row")
    own, width = nodes.shape
    heads, queries, keys = pair_bias.shape
    kinds, gauss = gauss_mul.shape[0], gauss_mean.shape[0]
    atoms = own * rows * cols
    dims = (own, cols, width, heads, keys, kinds)
    bias_rows, mask_rows, first_rows, wide_table, second_rows = sizes(dims)
    near_step, still = (1, 1), (0, 0)
    along_col = paired(list(range(1, cols)))
    along_row = [(even, odd) for odd, even in paired(list(range(3, rows, 2)))]
    column_parts, row_parts = sources(along_col), sources(along_row)
    row_parts = [(even ^ (1 - other), odd ^ (1 - other), other) if n else (0, 0, 0) for n, (even, odd, other) in enumerate(row_parts)]
    shape = jax.ShapeDtypeStruct
    params = pltpu.CompilerParams(vmem_limit_bytes=(16 if atoms <= 128 else 56) * 2**20)
    vmem, anywhere = pl.BlockSpec(memory_space=pltpu.VMEM), pl.BlockSpec(memory_space=pl.ANY)

    def call(kernel, name, out_shape, inputs, remote=(), scratch=()):
        single = not isinstance(out_shape, list)
        return pl.pallas_call(
            kernel,
            out_shape=out_shape,
            in_specs=[vmem] * len(inputs) + [anywhere] * len(remote),
            out_specs=vmem if single else [vmem] * len(out_shape),
            scratch_shapes=list(scratch),
            compiler_params=params,
            name=name,
        )(*inputs, *map(in_hbm, remote))

    own_arrays = (
        nodes,
        coords,
        atom_types[None, :],
        segment_ids[None, :],
        ln_gain[None, :],
        pair_mask,
        pair_bias.transpose(1, 2, 0),
    )
    mine, kept = call(
        functools.partial(pack_kernel, dims),
        "pack",
        [
            shape((first_rows, lanes), bf16),
            shape((-(-(bias_rows + mask_rows) // 16) * 16, lanes), bf16),
        ],
        (),
        own_arrays,
        [pltpu.VMEM(x.shape, x.dtype) for x in own_arrays]
        + [pltpu.VMEM((cols, mask_rows, lanes), f32), pltpu.SemaphoreType.DMA((7,))],
    )
    other = exchange(mine, near_step, still)
    grouped = call(
        functools.partial(regroup_kernel, dims, along_col),
        "regroup",
        [shape((second_rows, lanes), bf16)] * len(along_col),
        (mine, other),
    )
    received = [exchange(x, near_step, shift) for x, shift in zip(grouped, along_col, strict=True)]
    small = (w_heads.T, coords)
    tables = (gauss_mul, gauss_add, gauss_mean[None, :], gauss_width[None, :], w_gauss, w_coord1)
    tables += (w_coord2[None, :],)
    prepared = call(
        functools.partial(prepare_kernel, dims),
        "prepare",
        [shape(x.shape, x.dtype) for x in small]
        + [
            shape((gauss, gauss), bf16),
            shape(w_coord1.shape, bf16),
            shape((heads, lanes), f32),
            shape((2 * own, lanes), f32),
            shape((24, lanes), f32),
            shape((3, gauss, lanes), f32),
        ],
        (lax.optimization_barrier((mine, grouped[0]))[0],),
        small + tables,
        [pltpu.VMEM(x.shape, x.dtype) for x in tables] + [pltpu.SemaphoreType.DMA((9,))],
    )
    received[0], prepared = lax.optimization_barrier((received[0], prepared))
    received += [exchange(x, near_step, still) for x in received[:-1]]
    w_heads, coords, w_gauss, w_coord1, w_coord2, lookup, own_columns, kernels = prepared
    near = call(
        functools.partial(gather_kernel, dims),
        "gather",
        shape((table_rows + 2 * node_rows(width, own) * cols, lanes), bf16),
        (mine, other, *received),
    )
    pieces = [near] + [exchange(near, step, still) for step in along_row]
    pieces += [exchange(x, near_step, still) for x in pieces[1 : len(along_row)]]
    bias, spread_queries, w_qkv = call(
        functools.partial(arrange_kernel, dims, column_parts, row_parts),
        "arrange",
        [
            shape((own * heads, atoms), bf16),
            shape((own * heads, width), bf16),
            shape(w_qkv.shape, bf16),
        ],
        (lax.optimization_barrier((mine, pieces[1]))[0], kept, *received),
        (w_qkv,),
        [pltpu.SemaphoreType.DMA((1,))],
    )
    attended, moved = call(
        functools.partial(attend_kernel, dims, len(pieces)),
        "attend",
        [shape((own, width), bf16), shape((3, own), f32)],
        (*pieces, bias, spread_queries, w_qkv, w_heads, coords)
        + (w_gauss, w_coord1, w_coord2, lookup, own_columns, kernels),
        (),
        [
            pltpu.VMEM((own * heads, atoms), f32),
            pltpu.VMEM((atoms, width), bf16),
            pltpu.VMEM((8, atoms), f32),
            pltpu.VMEM((8, atoms), f32),
        ],
    )
    return attended, moved


def solution(mesh):
    own, tile, whole = P(("row", "col")), P("row", "col"), P()
    in_specs = (
        P(("row", "col"), None),
        P(None, ("row", "col")),
        own,
        own,
        tile,
        P(None, "row", "col"),
    ) + (whole,) * 10
    out_specs = (P(("row", "col"), None), P(None, ("row", "col")))
    return jax.shard_map(shards, mesh=mesh, in_specs=in_specs, out_specs=out_specs, check_vma=False)
```

```python
import functools
import math

import jax
import jax.numpy as jnp
from jax import lax
from jax.experimental import pallas as pl
from jax.experimental.pallas import tpu as pltpu
from jax.sharding import PartitionSpec as P

ln_epsilon = 1e-05
masked_fill = -1000000000.0
masked_below = -100000000.0
root_shift = 0.01
lanes = 128
f32 = jnp.float32
bf16 = jnp.bfloat16
nt = (((1,), (1,)), ((), ()))
tn = (((0,), (0,)), ((), ()))


def split3(x):
    hi = x.astype(bf16).astype(f32)
    mid = (x - hi).astype(bf16).astype(f32)
    return hi, mid, x - hi - mid


def iota(shape, axis):
    return lax.broadcasted_iota(jnp.int32, shape, axis)


def column(row):
    n = row.shape[1]
    square = jnp.where(iota((n, n), 0) == iota((n, n), 1), jnp.broadcast_to(row, (n, n)), 0.0)
    return jnp.sum(square, axis=1, keepdims=True)


def gelu(x):
    inner = x * (0.7978845608028654 + 0.035677408136300125 * (x * x))
    return (0.5 * x) * (1.0 + jnp.tanh(inner))


table_rows, table_used = 16, 11


def node_rows(width, own):
    return width // lanes * own


def sizes(dims):
    own, cols, width, heads, keys, kinds = dims
    bias_rows, mask_rows = own * keys * heads // lanes, own * keys // lanes
    first = table_rows + node_rows(width, own) + (cols - 1) * (bias_rows + mask_rows)
    wide_table = -(-(table_used + 2 * mask_rows) // 16) * 16
    second = 2 * bias_rows + wide_table + 2 * node_rows(width, own)
    return bias_rows, mask_rows, -(-first // 16) * 16, wide_table, second


def paired(steps):
    return [(steps[n + 1], steps[n]) for n in range(0, len(steps) - 1, 2)] + [(steps[-1], steps[-1])]


def sources(transfers):
    direct = [(odd, even, 1) for even, odd in transfers]
    return [(0, 0, 0)] + direct + [(even, odd, 0) for even, odd in transfers[:-1]]


def in_hbm(x):
    return pltpu.with_memory_space_constraint(x, pltpu.HBM)


def fetch(sources, targets, semaphores):
    copies = [
        pltpu.make_async_copy(source, target, semaphores.at[n])
        for n, (source, target) in enumerate(zip(sources, targets, strict=True))
    ]
    for copy in copies:
        copy.start()
    return copies


def filled(blocks, rows):
    rest = rows - sum(block.shape[0] for block in blocks)
    return jnp.concatenate(blocks + ([jnp.zeros((rest, lanes), f32)] if rest else []), axis=0)


def normed(x, gain):
    features = x.astype(f32)
    centred = features - jnp.mean(features, axis=1, keepdims=True)
    spread = jnp.mean(centred * centred, axis=1, keepdims=True)
    return (centred * lax.rsqrt(spread + ln_epsilon) * gain).astype(bf16)


def pack_kernel(dims, *refs):
    own, cols, width, heads, keys, kinds = dims
    bias_rows, mask_rows, first_rows, wide_table, second_rows = sizes(dims)
    first, kept, held, masks, semaphores = refs[7], refs[8], refs[9:16], refs[16], refs[17]
    copies = fetch(refs[:7], held, semaphores)
    nodes, coords, types, segments, ln_gain, mask, bias = held
    me = lax.axis_index("col")
    pairs, fold = own * keys, lanes // heads
    for copy in copies[:5]:
        copy.wait()
    high, middle, low = split3(coords[...])
    kind = (types[...] + kinds // 2 * segments[...]).astype(f32)
    blank = jnp.zeros((1, own), f32)
    table = jnp.concatenate([high, kind, low, blank, middle] + [blank] * 5, axis=0)
    table = jnp.concatenate([table, jnp.zeros((table_rows, lanes - own), f32)], axis=1)
    full = normed(nodes[...], ln_gain[...]).astype(f32)
    blocks = [table] + [full[:, b * lanes : (b + 1) * lanes] for b in range(width // lanes)]
    copies[5].wait()
    wide_mask = mask[...].astype(f32)
    for d in range(cols):
        row = jnp.concatenate([wide_mask[d * own + i : d * own + i + 1] for i in range(own)], axis=1)
        for n in range(mask_rows):
            masks[d, n : n + 1, :] = row[:, n * lanes : (n + 1) * lanes]
    start = (cols - 1) * bias_rows
    tail = filled(blocks + [masks[(me + k) % cols] for k in range(1, cols)], first_rows - start)
    first[start:, :] = tail.astype(bf16)
    kept[bias_rows:, :] = filled([masks[me]], kept.shape[0] - bias_rows).astype(bf16)
    copies[6].wait()
    for k in range(cols):
        tile = bias[pl.ds((me + k) % cols * own, own)].astype(f32).reshape(pairs, heads)
        wide = [tile[n * bias_rows : (n + 1) * bias_rows] for n in range(fold)]
        block = jnp.concatenate(wide, axis=1).astype(bf16)
        if k:
            first[(k - 1) * bias_rows : k * bias_rows, :] = block
        else:
            kept[:bias_rows, :] = block


def regroup_kernel(dims, transfers, mine, other, *outs):
    own, cols, width, heads, keys, kinds = dims
    bias_rows, mask_rows, first_rows, wide_table, second_rows = sizes(dims)
    odd = lax.axis_index("row") % 2 == 1
    start, rows = (cols - 1) * bias_rows, table_rows + node_rows(width, own)
    here, there = mine[start:, :].astype(f32), other[start:, :].astype(f32)
    table = (here[:table_rows] + pltpu.roll(there[:table_rows], own, 1))[:table_used]
    nodes = [here[table_rows:rows], there[table_rows:rows]]
    for out, (for_even, for_odd) in zip(outs, transfers, strict=True):

        def chosen(x, first, count):
            even_block = x[first + (for_even - 1) * count : first + for_even * count]
            if for_even == for_odd:
                return even_block
            return jnp.where(odd, x[first + (for_odd - 1) * count : first + for_odd * count], even_block)

        for n, ref in enumerate((mine, other)):
            out[n * bias_rows : (n + 1) * bias_rows, :] = chosen(ref, 0, bias_rows)
        masks = [chosen(x, rows, mask_rows) for x in (here, there)]
        tail = filled([table] + masks, wide_table)
        out[2 * bias_rows :, :] = jnp.concatenate([tail] + nodes, axis=0).astype(bf16)


def gather_kernel(dims, mine, other, *refs):
    own, cols, width, heads, keys, kinds = dims
    bias_rows, mask_rows, first_rows, wide_table, second_rows = sizes(dims)
    start, rows = (cols - 1) * bias_rows, node_rows(width, own)
    out = refs[cols - 1]
    here, there = mine[start:, :].astype(f32), other[start:, :].astype(f32)
    tails = [ref[2 * bias_rows :, :].astype(f32) for ref in refs[: cols - 1]]
    table = here[:table_rows] + pltpu.roll(there[:table_rows], own, 1)
    for k, tail in enumerate(tails, 1):
        part = jnp.where(iota((table_rows, lanes), 0) < table_used, tail[:table_rows], 0.0)
        table = table + pltpu.roll(part, 2 * own * k, 1)
    out[:table_rows, :] = table.astype(bf16)
    blocks = [here[table_rows:], there[table_rows:]]
    for tail in tails:
        blocks += [tail[wide_table : wide_table + rows], tail[wide_table + rows :]]
    each = 2 * own * cols
    for b in range(width // lanes):
        taken = jnp.concatenate([block[b * own : (b + 1) * own] for block in blocks], axis=0)
        out[table_rows + b * each : table_rows + (b + 1) * each, :] = taken.astype(bf16)


def arrange_kernel(dims, column_parts, row_parts, mine, kept, *refs):
    own, cols, width, heads, keys, kinds = dims
    bias_rows, mask_rows, first_rows, wide_table, second_rows = sizes(dims)
    received = refs[: cols - 1]
    w_source, out, spread_queries, w_qkv, semaphores = refs[cols - 1 :]
    copies = fetch((w_source,), (w_qkv,), semaphores)
    atoms = out.shape[1]
    fold = lanes // heads
    each = own // fold
    per_row = 2 * own * cols
    r, c = lax.axis_index("row"), lax.axis_index("col")

    def by_core(odd, part):
        return jnp.where(odd, part[1], part[0])

    blocks, masks = [], []
    for b in range(each):
        rows = [kept[b * keys : (b + 1) * keys, :]]
        for ref, part in zip(received, column_parts[1:], strict=True):
            first = part[2] * bias_rows + b * keys
            rows.append(ref[first : first + keys, :])
        blocks.append(jnp.concatenate(rows, axis=0))
    tails = [kept[bias_rows:, :].astype(f32)[:mask_rows]]
    for ref, part in zip(received, column_parts[1:], strict=True):
        first = table_used + part[2] * mask_rows
        tails.append(ref[2 * bias_rows : 2 * bias_rows + wide_table, :].astype(f32)[first : first + mask_rows])
    for i in range(own):
        n, lane = i * keys // lanes, i * keys % lanes
        masks.append(jnp.concatenate([tail[n : n + 1, lane : lane + keys] for tail in tails], axis=1))
    masks = jnp.concatenate(masks + [jnp.zeros((16 - own, atoms), f32)], axis=0).astype(bf16)
    place = iota((atoms, 1), 0)
    step = jnp.zeros((atoms, 1), jnp.int32)
    for n, part in enumerate(column_parts):
        step = jnp.where(place // keys == n, by_core(r % 2 == 1, part), step)
    atom = (c + cols - step) % cols * keys + place % keys
    for s in range(0, atoms, lanes):
        slot = s + iota((1, lanes), 1)
        piece, inner = slot // per_row, slot % per_row
        row = jnp.zeros((1, lanes), jnp.int32) + r
        for n, part in enumerate(row_parts):
            row = jnp.where(piece == n, r ^ by_core(r % 2 == 1, part), row)
        step, flip = jnp.zeros((1, lanes), jnp.int32), jnp.zeros((1, lanes), jnp.int32)
        for n, part in enumerate(column_parts):
            here = inner // (2 * own) == n
            step = jnp.where(here, by_core(row % 2 == 1, part), step)
            flip = jnp.where(here, part[2], flip)
        row = row ^ flip ^ (inner // own % 2)
        source = (row * cols + (c + cols - step) % cols) * own + inner % own
        chosen = (atom == source).astype(f32).astype(bf16)
        valid = jnp.dot(masks, chosen, preferred_element_type=f32)
        for b in range(each):
            moved = lax.dot_general(blocks[b], chosen, tn, preferred_element_type=f32)
            for a in range(fold):
                i = a * each + b
                taken = jnp.where(valid[i : i + 1] > 0.5, moved[a * heads : (a + 1) * heads], masked_fill)
                out[i * heads : (i + 1) * heads, s : s + lanes] = taken.astype(bf16)
    rows = mine[(cols - 1) * bias_rows :, :].astype(f32)[table_rows : table_rows + node_rows(width, own)]
    x = jnp.concatenate([rows[b * own : (b + 1) * own] for b in range(width // lanes)], axis=1)
    x = jnp.concatenate([x, jnp.zeros((16 - own, width), f32)], axis=0).astype(bf16)
    copies[0].wait()
    queries = jnp.dot(x, w_qkv[:, :width], preferred_element_type=f32)
    head_mask = iota((heads, width), 1) // (width // heads) == iota((heads, width), 0)
    for i in range(own):
        spread = jnp.where(head_mask, jnp.broadcast_to(queries[i : i + 1], (heads, width)), 0.0)
        spread_queries[i * heads : (i + 1) * heads, :] = spread.astype(bf16)


def prepare_kernel(dims, mine, *refs):
    own, cols, width, heads, keys, kinds = dims
    bias_rows, mask_rows, first_rows, wide_table, second_rows = sizes(dims)
    w_heads, coords, w_gauss, w_coord1, w_coord2 = refs[9:14]
    lookup, own_columns, kernels = refs[14:17]
    mul_held, add_held, mean_held, width_held, gauss_held, coord1_held, coord2_held = refs[17:24]
    copies = fetch(
        refs[:9],
        (w_heads, coords, mul_held, add_held, mean_held, width_held)
        + (gauss_held, coord1_held, coord2_held),
        refs[24],
    )
    table = mine[(cols - 1) * bias_rows :, :].astype(f32)[:table_rows]
    places = (table[0:3] + table[8:11]) + table[4:7]
    for c in range(3):
        own_columns[c * 8 : c * 8 + own, :] = jnp.broadcast_to(
            column(places[c : c + 1, :own]), (own, lanes)
        )
    own_kind = column(table[3:4, :own]).astype(jnp.int32)
    own_kind = jnp.concatenate([own_kind, jnp.zeros((16 - own, 1), jnp.int32)], axis=0)
    query_onehot = (own_kind == iota((16, kinds), 1)).astype(f32).astype(bf16)
    for copy in copies:
        copy.wait()
    inverse = 1.0 / column(width_held[...])
    gauss = inverse.shape[0]
    kernels[0] = jnp.broadcast_to(column(mean_held[...]), (gauss, lanes))
    kernels[1] = jnp.broadcast_to(inverse * math.sqrt(0.5 * math.log2(math.e)), (gauss, lanes))
    kernels[2] = jnp.broadcast_to(jnp.log2(inverse * (1.0 / math.sqrt(2.0 * math.pi))), (gauss, lanes))
    found = []
    for table in (mul_held, add_held):
        parts = [
            jnp.dot(query_onehot, part.astype(bf16), preferred_element_type=f32)
            for part in split3(table[...])
        ]
        found.append((parts[0] + parts[1] + parts[2])[:own])
    found = jnp.concatenate(found, axis=0)
    lookup[...] = jnp.concatenate([found, jnp.zeros((2 * own, lanes - kinds), f32)], axis=1)
    w_gauss[...] = gauss_held[...].astype(f32).T.astype(bf16)
    w_coord1[...] = coord1_held[...].astype(f32).T.astype(bf16)
    w_coord2[...] = jnp.broadcast_to(column(coord2_held[...].astype(f32)), (heads, lanes))


def attend_kernel(dims, count, *refs):
    own, cols, width, heads, keys, kinds = dims
    pieces = refs[:count]
    bias, spread_queries, w_qkv, w_heads, coords = refs[count : count + 5]
    w_gauss, w_coord1, w_coord2, lookup, own_columns, kernels = refs[count + 5 : count + 11]
    attended, moved, logits, values, places, strengths = refs[count + 11 :]
    atoms = bias.shape[1]
    each = 2 * own * cols
    centre, sharp, norming = kernels[0], kernels[1], kernels[2]
    found = lookup[...]

    for s in range(0, atoms, lanes):
        taken = pieces[s // each : (s + lanes) // each]
        x = [
            jnp.concatenate(
                [
                    ref[table_rows + b * each : table_rows + (b + 1) * each, :]
                    for b in range(width // lanes)
                ],
                axis=1,
            )
            for ref in taken
        ]
        block = jnp.concatenate(x, axis=0)
        table = jnp.concatenate([ref[:table_rows, :].astype(f32)[:, :each] for ref in taken], axis=1)
        place = (table[0:3] + table[8:11]) + table[4:7]
        places[0:3, s : s + lanes] = place
        offsets = [own_columns[c * 8 : c * 8 + own, :] - place[c : c + 1] for c in range(3)]
        squares = offsets[0] * offsets[0] + offsets[1] * offsets[1] + offsets[2] * offsets[2]
        distance = jnp.sqrt(squares + root_shift)
        kind = jnp.broadcast_to(table[3:4].astype(jnp.int32), (2 * own, lanes))
        pair = jnp.take_along_axis(found, kind, axis=1)
        expanded = pair[:own] * distance + pair[own:]
        features = []
        for i in range(own):
            scaled = (expanded[i : i + 1] - centre) * sharp
            features.append(jnp.exp2(norming - scaled * scaled).astype(bf16))
        keys_here = jnp.dot(block, w_qkv[:, width : 2 * width], preferred_element_type=f32)
        values[s : s + lanes, :] = jnp.dot(
            block, w_qkv[:, 2 * width :], preferred_element_type=f32
        ).astype(bf16)
        affinity = lax.dot_general(
            spread_queries[...], keys_here.astype(bf16), nt, preferred_element_type=f32
        )
        hidden = jnp.dot(w_gauss[...], jnp.concatenate(features, axis=1), preferred_element_type=f32)
        geometry = jnp.dot(w_heads[...], gelu(hidden).astype(bf16), preferred_element_type=f32)
        here = bias[:, s : s + lanes].astype(f32)
        rows = []
        for i in range(own):
            at = slice(i * heads, (i + 1) * heads)
            row = here[at] + affinity[at] * (1.0 / math.sqrt(width // heads))
            row = row + geometry[:, i * lanes : (i + 1) * lanes]
            logits[at, s : s + lanes] = jnp.where(here[at] < masked_below, masked_fill, row)
            rows.append(row.astype(bf16))
        mixed = jnp.dot(w_coord1[...], jnp.concatenate(rows, axis=1), preferred_element_type=f32)
        mixed = gelu(mixed)
        for i in range(own):
            strength = jnp.sum(
                mixed[:, i * lanes : (i + 1) * lanes] * w_coord2[...], axis=0, keepdims=True
            )
            masked = here[i * heads : i * heads + 1] < masked_below
            strengths[i : i + 1, s : s + lanes] = jnp.where(masked, 0.0, strength)

    masked = logits[...]
    weights = jnp.exp(masked - jnp.max(masked, axis=1, keepdims=True))
    share = 1.0 / jnp.sum(weights, axis=1, keepdims=True)
    taken = jnp.dot(weights.astype(bf16), values[...], preferred_element_type=f32) * share
    head_mask = iota((heads, width), 1) // (width // heads) == iota((heads, width), 0)
    attended[...] = jnp.concatenate(
        [
            jnp.sum(
                jnp.where(head_mask, taken[i * heads : (i + 1) * heads], 0.0), axis=0, keepdims=True
            )
            for i in range(own)
        ],
        axis=0,
    ).astype(bf16)
    here = coords[...]
    shift = jnp.zeros((3, own), f32)
    for i in range(own):
        pulls = (here[:, i : i + 1] - places[0:3, :]) * strengths[i : i + 1, :]
        shift = jnp.where(iota((3, own), 1) == i, jnp.sum(pulls, axis=1, keepdims=True), shift)
    moved[...] = here + shift * (1.0 / atoms)


def exchange(x, steps, distances):
    rows, cols = lax.axis_size("row"), lax.axis_size("col")
    pairs = [
        (r * cols + c, (r ^ steps[r % 2]) * cols + (c + distances[r % 2]) % cols)
        for r in range(rows)
        for c in range(cols)
    ]
    return lax.ppermute(x, ("row", "col"), pairs)


def shards(
    nodes,
    coords,
    atom_types,
    segment_ids,
    pair_mask,
    pair_bias,
    ln_gain,
    w_qkv,
    gauss_mul,
    gauss_add,
    gauss_mean,
    gauss_width,
    w_gauss,
    w_heads,
    w_coord1,
    w_coord2,
):
    cols, rows = lax.axis_size("col"), lax.axis_size("row")
    own, width = nodes.shape
    heads, queries, keys = pair_bias.shape
    kinds, gauss = gauss_mul.shape[0], gauss_mean.shape[0]
    atoms = own * rows * cols
    dims = (own, cols, width, heads, keys, kinds)
    bias_rows, mask_rows, first_rows, wide_table, second_rows = sizes(dims)
    near_step, still = (1, 1), (0, 0)
    along_col = paired(list(range(1, cols)))
    along_row = [(even, odd) for odd, even in paired(list(range(3, rows, 2)))]
    column_parts, row_parts = sources(along_col), sources(along_row)
    row_parts = [(even ^ (1 - other), odd ^ (1 - other), other) if n else (0, 0, 0) for n, (even, odd, other) in enumerate(row_parts)]
    shape = jax.ShapeDtypeStruct
    params = pltpu.CompilerParams(vmem_limit_bytes=(16 if atoms <= 128 else 56) * 2**20)
    vmem, anywhere = pl.BlockSpec(memory_space=pltpu.VMEM), pl.BlockSpec(memory_space=pl.ANY)

    def call(kernel, name, out_shape, inputs, remote=(), scratch=()):
        single = not isinstance(out_shape, list)
        return pl.pallas_call(
            kernel,
            out_shape=out_shape,
            in_specs=[vmem] * len(inputs) + [anywhere] * len(remote),
            out_specs=vmem if single else [vmem] * len(out_shape),
            scratch_shapes=list(scratch),
            compiler_params=params,
            name=name,
        )(*inputs, *map(in_hbm, remote))

    own_arrays = (
        nodes,
        coords,
        atom_types[None, :],
        segment_ids[None, :],
        ln_gain[None, :],
        pair_mask,
        pair_bias.transpose(1, 2, 0),
    )
    mine, kept = call(
        functools.partial(pack_kernel, dims),
        "pack",
        [
            shape((first_rows, lanes), bf16),
            shape((-(-(bias_rows + mask_rows) // 16) * 16, lanes), bf16),
        ],
        (),
        own_arrays,
        [pltpu.VMEM(x.shape, x.dtype) for x in own_arrays]
        + [pltpu.VMEM((cols, mask_rows, lanes), f32), pltpu.SemaphoreType.DMA((7,))],
    )
    other = exchange(mine, near_step, still)
    grouped = call(
        functools.partial(regroup_kernel, dims, along_col),
        "regroup",
        [shape((second_rows, lanes), bf16)] * len(along_col),
        (mine, other),
    )
    received = [exchange(x, near_step, shift) for x, shift in zip(grouped, along_col, strict=True)]
    small = (w_heads.T, coords)
    tables = (gauss_mul, gauss_add, gauss_mean[None, :], gauss_width[None, :], w_gauss, w_coord1)
    tables += (w_coord2[None, :],)
    prepared = call(
        functools.partial(prepare_kernel, dims),
        "prepare",
        [shape(x.shape, x.dtype) for x in small]
        + [
            shape((gauss, gauss), bf16),
            shape(w_coord1.shape, bf16),
            shape((heads, lanes), f32),
            shape((2 * own, lanes), f32),
            shape((24, lanes), f32),
            shape((3, gauss, lanes), f32),
        ],
        (lax.optimization_barrier((mine, grouped[0]))[0],),
        small + tables,
        [pltpu.VMEM(x.shape, x.dtype) for x in tables] + [pltpu.SemaphoreType.DMA((9,))],
    )
    received[0], prepared = lax.optimization_barrier((received[0], prepared))
    received += [exchange(x, near_step, still) for x in received[:-1]]
    w_heads, coords, w_gauss, w_coord1, w_coord2, lookup, own_columns, kernels = prepared
    near = call(
        functools.partial(gather_kernel, dims),
        "gather",
        shape((table_rows + 2 * node_rows(width, own) * cols, lanes), bf16),
        (mine, other, *received),
    )
    pieces = [near] + [exchange(near, step, still) for step in along_row]
    pieces += [exchange(x, near_step, still) for x in pieces[1 : len(along_row)]]
    bias, spread_queries, w_qkv = call(
        functools.partial(arrange_kernel, dims, column_parts, row_parts),
        "arrange",
        [
            shape((own * heads, atoms), bf16),
            shape((own * heads, width), bf16),
            shape(w_qkv.shape, bf16),
        ],
        (lax.optimization_barrier((mine, pieces[1]))[0], kept, *received),
        (w_qkv,),
        [pltpu.SemaphoreType.DMA((1,))],
    )
    attended, moved = call(
        functools.partial(attend_kernel, dims, len(pieces)),
        "attend",
        [shape((own, width), bf16), shape((3, own), f32)],
        (*pieces, bias, spread_queries, w_qkv, w_heads, coords)
        + (w_gauss, w_coord1, w_coord2, lookup, own_columns, kernels),
        (),
        [
            pltpu.VMEM((own * heads, atoms), f32),
            pltpu.VMEM((atoms, width), bf16),
            pltpu.VMEM((8, atoms), f32),
            pltpu.VMEM((8, atoms), f32),
        ],
    )
    return attended, moved


def solution(mesh):
    own, tile, whole = P(("row", "col")), P("row", "col"), P()
    in_specs = (
        P(("row", "col"), None),
        P(None, ("row", "col")),
        own,
        own,
        tile,
        P(None, "row", "col"),
    ) + (whole,) * 10
    out_specs = (P(("row", "col"), None), P(None, ("row", "col")))
    return jax.shard_map(shards, mesh=mesh, in_specs=in_specs, out_specs=out_specs, check_vma=False)
```

```python
import functools
import math

import jax
import jax.numpy as jnp
from jax import lax
from jax.experimental import pallas as pl
from jax.experimental.pallas import tpu as pltpu
from jax.sharding import PartitionSpec as P

ln_epsilon = 1e-05
masked_fill = -1000000000.0
masked_below = -100000000.0
root_shift = 0.01
lanes = 128
f32 = jnp.float32
bf16 = jnp.bfloat16
nt = (((1,), (1,)), ((), ()))
tn = (((0,), (0,)), ((), ()))


def split3(x):
    hi = x.astype(bf16).astype(f32)
    mid = (x - hi).astype(bf16).astype(f32)
    return hi, mid, x - hi - mid


def iota(shape, axis):
    return lax.broadcasted_iota(jnp.int32, shape, axis)


def column(row):
    n = row.shape[1]
    square = jnp.where(iota((n, n), 0) == iota((n, n), 1), jnp.broadcast_to(row, (n, n)), 0.0)
    return jnp.sum(square, axis=1, keepdims=True)


def gelu(x):
    inner = x * (0.7978845608028654 + 0.035677408136300125 * (x * x))
    return (0.5 * x) * (1.0 + jnp.tanh(inner))


table_rows, table_used = 16, 11


def node_rows(width, own):
    return width // lanes * own


def sizes(dims):
    own, cols, width, heads, keys, kinds = dims
    bias_rows, mask_rows = own * keys * heads // lanes, own * keys // lanes
    first = table_rows + node_rows(width, own) + (cols - 1) * (bias_rows + mask_rows)
    wide_table = -(-(table_used + 2 * mask_rows) // 16) * 16
    second = 2 * bias_rows + wide_table + 2 * node_rows(width, own)
    return bias_rows, mask_rows, -(-first // 16) * 16, wide_table, second


def paired(steps):
    return [(steps[n + 1], steps[n]) for n in range(0, len(steps) - 1, 2)] + [(steps[-1], steps[-1])]


def sources(transfers):
    direct = [(odd, even, 1) for even, odd in transfers]
    return [(0, 0, 0)] + direct + [(even, odd, 0) for even, odd in transfers[:-1]]


def in_hbm(x):
    return pltpu.with_memory_space_constraint(x, pltpu.HBM)


def fetch(sources, targets, semaphores):
    copies = [
        pltpu.make_async_copy(source, target, semaphores.at[n])
        for n, (source, target) in enumerate(zip(sources, targets, strict=True))
    ]
    for copy in copies:
        copy.start()
    return copies


def filled(blocks, rows):
    rest = rows - sum(block.shape[0] for block in blocks)
    return jnp.concatenate(blocks + ([jnp.zeros((rest, lanes), f32)] if rest else []), axis=0)


def normed(x, gain):
    features = x.astype(f32)
    centred = features - jnp.mean(features, axis=1, keepdims=True)
    spread = jnp.mean(centred * centred, axis=1, keepdims=True)
    return (centred * lax.rsqrt(spread + ln_epsilon) * gain).astype(bf16)


def pack_kernel(dims, *refs):
    own, cols, width, heads, keys, kinds = dims
    bias_rows, mask_rows, first_rows, wide_table, second_rows = sizes(dims)
    first, kept, held, masks, semaphores = refs[7], refs[8], refs[9:16], refs[16], refs[17]
    copies = fetch(refs[:7], held, semaphores)
    nodes, coords, types, segments, ln_gain, mask, bias = held
    me = lax.axis_index("col")
    pairs, fold = own * keys, lanes // heads
    for copy in copies[:5]:
        copy.wait()
    high, middle, low = split3(coords[...])
    kind = (types[...] + kinds // 2 * segments[...]).astype(f32)
    blank = jnp.zeros((1, own), f32)
    table = jnp.concatenate([high, kind, low, blank, middle] + [blank] * 5, axis=0)
    table = jnp.concatenate([table, jnp.zeros((table_rows, lanes - own), f32)], axis=1)
    full = normed(nodes[...], ln_gain[...]).astype(f32)
    blocks = [table] + [full[:, b * lanes : (b + 1) * lanes] for b in range(width // lanes)]
    copies[5].wait()
    wide_mask = mask[...].astype(f32)
    for d in range(cols):
        row = jnp.concatenate([wide_mask[d * own + i : d * own + i + 1] for i in range(own)], axis=1)
        for n in range(mask_rows):
            masks[d, n : n + 1, :] = row[:, n * lanes : (n + 1) * lanes]
    start = (cols - 1) * bias_rows
    tail = filled(blocks + [masks[(me + k) % cols] for k in range(1, cols)], first_rows - start)
    first[start:, :] = tail.astype(bf16)
    kept[bias_rows:, :] = filled([masks[me]], kept.shape[0] - bias_rows).astype(bf16)
    copies[6].wait()
    for k in range(cols):
        tile = bias[pl.ds((me + k) % cols * own, own)].astype(f32).reshape(pairs, heads)
        wide = [tile[n * bias_rows : (n + 1) * bias_rows] for n in range(fold)]
        block = jnp.concatenate(wide, axis=1).astype(bf16)
        if k:
            first[(k - 1) * bias_rows : k * bias_rows, :] = block
        else:
            kept[:bias_rows, :] = block


def regroup_kernel(dims, transfers, mine, other, *outs):
    own, cols, width, heads, keys, kinds = dims
    bias_rows, mask_rows, first_rows, wide_table, second_rows = sizes(dims)
    odd = lax.axis_index("row") % 2 == 1
    start, rows = (cols - 1) * bias_rows, table_rows + node_rows(width, own)
    here, there = mine[start:, :].astype(f32), other[start:, :].astype(f32)
    table = (here[:table_rows] + pltpu.roll(there[:table_rows], own, 1))[:table_used]
    nodes = [here[table_rows:rows], there[table_rows:rows]]
    for out, (for_even, for_odd) in zip(outs, transfers, strict=True):

        def chosen(x, first, count):
            even_block = x[first + (for_even - 1) * count : first + for_even * count]
            if for_even == for_odd:
                return even_block
            return jnp.where(odd, x[first + (for_odd - 1) * count : first + for_odd * count], even_block)

        for n, ref in enumerate((mine, other)):
            out[n * bias_rows : (n + 1) * bias_rows, :] = chosen(ref, 0, bias_rows)
        masks = [chosen(x, rows, mask_rows) for x in (here, there)]
        tail = filled([table] + masks, wide_table)
        out[2 * bias_rows :, :] = jnp.concatenate([tail] + nodes, axis=0).astype(bf16)


def gather_kernel(dims, mine, other, *refs):
    own, cols, width, heads, keys, kinds = dims
    bias_rows, mask_rows, first_rows, wide_table, second_rows = sizes(dims)
    start, rows = (cols - 1) * bias_rows, node_rows(width, own)
    out = refs[cols - 1]
    here, there = mine[start:, :].astype(f32), other[start:, :].astype(f32)
    tails = [ref[2 * bias_rows :, :].astype(f32) for ref in refs[: cols - 1]]
    table = here[:table_rows] + pltpu.roll(there[:table_rows], own, 1)
    for k, tail in enumerate(tails, 1):
        part = jnp.where(iota((table_rows, lanes), 0) < table_used, tail[:table_rows], 0.0)
        table = table + pltpu.roll(part, 2 * own * k, 1)
    out[:table_rows, :] = table.astype(bf16)
    blocks = [here[table_rows:], there[table_rows:]]
    for tail in tails:
        blocks += [tail[wide_table : wide_table + rows], tail[wide_table + rows :]]
    each = 2 * own * cols
    for b in range(width // lanes):
        taken = jnp.concatenate([block[b * own : (b + 1) * own] for block in blocks], axis=0)
        out[table_rows + b * each : table_rows + (b + 1) * each, :] = taken.astype(bf16)


def arrange_kernel(dims, column_parts, row_parts, mine, kept, *refs):
    own, cols, width, heads, keys, kinds = dims
    bias_rows, mask_rows, first_rows, wide_table, second_rows = sizes(dims)
    received = refs[: cols - 1]
    w_qkv, out, spread_queries = refs[cols - 1 :]
    atoms = out.shape[1]
    fold = lanes // heads
    each = own // fold
    per_row = 2 * own * cols
    r, c = lax.axis_index("row"), lax.axis_index("col")

    def by_core(odd, part):
        return jnp.where(odd, part[1], part[0])

    blocks, masks = [], []
    for b in range(each):
        rows = [kept[b * keys : (b + 1) * keys, :]]
        for ref, part in zip(received, column_parts[1:], strict=True):
            first = part[2] * bias_rows + b * keys
            rows.append(ref[first : first + keys, :])
        blocks.append(jnp.concatenate(rows, axis=0))
    tails = [kept[bias_rows:, :].astype(f32)[:mask_rows]]
    for ref, part in zip(received, column_parts[1:], strict=True):
        first = table_used + part[2] * mask_rows
        tails.append(ref[2 * bias_rows : 2 * bias_rows + wide_table, :].astype(f32)[first : first + mask_rows])
    for i in range(own):
        n, lane = i * keys // lanes, i * keys % lanes
        masks.append(jnp.concatenate([tail[n : n + 1, lane : lane + keys] for tail in tails], axis=1))
    masks = jnp.concatenate(masks + [jnp.zeros((16 - own, atoms), f32)], axis=0).astype(bf16)
    place = iota((atoms, 1), 0)
    step = jnp.zeros((atoms, 1), jnp.int32)
    for n, part in enumerate(column_parts):
        step = jnp.where(place // keys == n, by_core(r % 2 == 1, part), step)
    atom = (c + cols - step) % cols * keys + place % keys
    for s in range(0, atoms, lanes):
        slot = s + iota((1, lanes), 1)
        piece, inner = slot // per_row, slot % per_row
        row = jnp.zeros((1, lanes), jnp.int32) + r
        for n, part in enumerate(row_parts):
            row = jnp.where(piece == n, r ^ by_core(r % 2 == 1, part), row)
        step, flip = jnp.zeros((1, lanes), jnp.int32), jnp.zeros((1, lanes), jnp.int32)
        for n, part in enumerate(column_parts):
            here = inner // (2 * own) == n
            step = jnp.where(here, by_core(row % 2 == 1, part), step)
            flip = jnp.where(here, part[2], flip)
        row = row ^ flip ^ (inner // own % 2)
        source = (row * cols + (c + cols - step) % cols) * own + inner % own
        chosen = (atom == source).astype(f32).astype(bf16)
        valid = jnp.dot(masks, chosen, preferred_element_type=f32)
        for b in range(each):
            moved = lax.dot_general(blocks[b], chosen, tn, preferred_element_type=f32)
            for a in range(fold):
                i = a * each + b
                taken = jnp.where(valid[i : i + 1] > 0.5, moved[a * heads : (a + 1) * heads], masked_fill)
                out[i * heads : (i + 1) * heads, s : s + lanes] = taken.astype(bf16)
    rows = mine[(cols - 1) * bias_rows :, :].astype(f32)[table_rows : table_rows + node_rows(width, own)]
    x = jnp.concatenate([rows[b * own : (b + 1) * own] for b in range(width // lanes)], axis=1)
    x = jnp.concatenate([x, jnp.zeros((16 - own, width), f32)], axis=0).astype(bf16)
    queries = jnp.dot(x, w_qkv[:, :width], preferred_element_type=f32)
    head_mask = iota((heads, width), 1) // (width // heads) == iota((heads, width), 0)
    for i in range(own):
        spread = jnp.where(head_mask, jnp.broadcast_to(queries[i : i + 1], (heads, width)), 0.0)
        spread_queries[i * heads : (i + 1) * heads, :] = spread.astype(bf16)


def prepare_kernel(dims, mine, *refs):
    own, cols, width, heads, keys, kinds = dims
    bias_rows, mask_rows, first_rows, wide_table, second_rows = sizes(dims)
    w_qkv, w_heads, coords, w_gauss, w_coord1, w_coord2 = refs[10:16]
    lookup, own_columns, kernels = refs[16:19]
    mul_held, add_held, mean_held, width_held, gauss_held, coord1_held, coord2_held = refs[19:26]
    copies = fetch(
        refs[:10],
        (w_qkv, w_heads, coords, mul_held, add_held, mean_held, width_held)
        + (gauss_held, coord1_held, coord2_held),
        refs[26],
    )
    table = mine[(cols - 1) * bias_rows :, :].astype(f32)[:table_rows]
    places = (table[0:3] + table[8:11]) + table[4:7]
    for c in range(3):
        own_columns[c * 8 : c * 8 + own, :] = jnp.broadcast_to(
            column(places[c : c + 1, :own]), (own, lanes)
        )
    own_kind = column(table[3:4, :own]).astype(jnp.int32)
    own_kind = jnp.concatenate([own_kind, jnp.zeros((16 - own, 1), jnp.int32)], axis=0)
    query_onehot = (own_kind == iota((16, kinds), 1)).astype(f32).astype(bf16)
    for copy in copies:
        copy.wait()
    inverse = 1.0 / column(width_held[...])
    gauss = inverse.shape[0]
    kernels[0] = jnp.broadcast_to(column(mean_held[...]), (gauss, lanes))
    kernels[1] = jnp.broadcast_to(inverse * math.sqrt(0.5 * math.log2(math.e)), (gauss, lanes))
    kernels[2] = jnp.broadcast_to(jnp.log2(inverse * (1.0 / math.sqrt(2.0 * math.pi))), (gauss, lanes))
    found = []
    for table in (mul_held, add_held):
        parts = [
            jnp.dot(query_onehot, part.astype(bf16), preferred_element_type=f32)
            for part in split3(table[...])
        ]
        found.append((parts[0] + parts[1] + parts[2])[:own])
    found = jnp.concatenate(found, axis=0)
    lookup[...] = jnp.concatenate([found, jnp.zeros((2 * own, lanes - kinds), f32)], axis=1)
    w_gauss[...] = gauss_held[...].astype(f32).T.astype(bf16)
    w_coord1[...] = coord1_held[...].astype(f32).T.astype(bf16)
    w_coord2[...] = jnp.broadcast_to(column(coord2_held[...].astype(f32)), (heads, lanes))


def attend_kernel(dims, count, *refs):
    own, cols, width, heads, keys, kinds = dims
    pieces = refs[:count]
    bias, spread_queries, w_qkv, w_heads, coords = refs[count : count + 5]
    w_gauss, w_coord1, w_coord2, lookup, own_columns, kernels = refs[count + 5 : count + 11]
    attended, moved, logits, values, places, strengths = refs[count + 11 :]
    atoms = bias.shape[1]
    each = 2 * own * cols
    centre, sharp, norming = kernels[0], kernels[1], kernels[2]
    found = lookup[...]

    for s in range(0, atoms, lanes):
        taken = pieces[s // each : (s + lanes) // each]
        x = [
            jnp.concatenate(
                [
                    ref[table_rows + b * each : table_rows + (b + 1) * each, :]
                    for b in range(width // lanes)
                ],
                axis=1,
            )
            for ref in taken
        ]
        block = jnp.concatenate(x, axis=0)
        table = jnp.concatenate([ref[:table_rows, :].astype(f32)[:, :each] for ref in taken], axis=1)
        place = (table[0:3] + table[8:11]) + table[4:7]
        places[0:3, s : s + lanes] = place
        offsets = [own_columns[c * 8 : c * 8 + own, :] - place[c : c + 1] for c in range(3)]
        squares = offsets[0] * offsets[0] + offsets[1] * offsets[1] + offsets[2] * offsets[2]
        distance = jnp.sqrt(squares + root_shift)
        kind = jnp.broadcast_to(table[3:4].astype(jnp.int32), (2 * own, lanes))
        pair = jnp.take_along_axis(found, kind, axis=1)
        expanded = pair[:own] * distance + pair[own:]
        features = []
        for i in range(own):
            scaled = (expanded[i : i + 1] - centre) * sharp
            features.append(jnp.exp2(norming - scaled * scaled).astype(bf16))
        keys_here = jnp.dot(block, w_qkv[:, width : 2 * width], preferred_element_type=f32)
        values[s : s + lanes, :] = jnp.dot(
            block, w_qkv[:, 2 * width :], preferred_element_type=f32
        ).astype(bf16)
        affinity = lax.dot_general(
            spread_queries[...], keys_here.astype(bf16), nt, preferred_element_type=f32
        )
        hidden = jnp.dot(w_gauss[...], jnp.concatenate(features, axis=1), preferred_element_type=f32)
        geometry = jnp.dot(w_heads[...], gelu(hidden).astype(bf16), preferred_element_type=f32)
        here = bias[:, s : s + lanes].astype(f32)
        rows = []
        for i in range(own):
            at = slice(i * heads, (i + 1) * heads)
            row = here[at] + affinity[at] * (1.0 / math.sqrt(width // heads))
            row = row + geometry[:, i * lanes : (i + 1) * lanes]
            logits[at, s : s + lanes] = jnp.where(here[at] < masked_below, masked_fill, row)
            rows.append(row.astype(bf16))
        mixed = jnp.dot(w_coord1[...], jnp.concatenate(rows, axis=1), preferred_element_type=f32)
        mixed = gelu(mixed)
        for i in range(own):
            strength = jnp.sum(
                mixed[:, i * lanes : (i + 1) * lanes] * w_coord2[...], axis=0, keepdims=True
            )
            masked = here[i * heads : i * heads + 1] < masked_below
            strengths[i : i + 1, s : s + lanes] = jnp.where(masked, 0.0, strength)

    masked = logits[...]
    weights = jnp.exp(masked - jnp.max(masked, axis=1, keepdims=True))
    share = 1.0 / jnp.sum(weights, axis=1, keepdims=True)
    taken = jnp.dot(weights.astype(bf16), values[...], preferred_element_type=f32) * share
    head_mask = iota((heads, width), 1) // (width // heads) == iota((heads, width), 0)
    attended[...] = jnp.concatenate(
        [
            jnp.sum(
                jnp.where(head_mask, taken[i * heads : (i + 1) * heads], 0.0), axis=0, keepdims=True
            )
            for i in range(own)
        ],
        axis=0,
    ).astype(bf16)
    here = coords[...]
    shift = jnp.zeros((3, own), f32)
    for i in range(own):
        pulls = (here[:, i : i + 1] - places[0:3, :]) * strengths[i : i + 1, :]
        shift = jnp.where(iota((3, own), 1) == i, jnp.sum(pulls, axis=1, keepdims=True), shift)
    moved[...] = here + shift * (1.0 / atoms)


def exchange(x, steps, distances):
    rows, cols = lax.axis_size("row"), lax.axis_size("col")
    pairs = [
        (r * cols + c, (r ^ steps[r % 2]) * cols + (c + distances[r % 2]) % cols)
        for r in range(rows)
        for c in range(cols)
    ]
    return lax.ppermute(x, ("row", "col"), pairs)


def shards(
    nodes,
    coords,
    atom_types,
    segment_ids,
    pair_mask,
    pair_bias,
    ln_gain,
    w_qkv,
    gauss_mul,
    gauss_add,
    gauss_mean,
    gauss_width,
    w_gauss,
    w_heads,
    w_coord1,
    w_coord2,
):
    cols, rows = lax.axis_size("col"), lax.axis_size("row")
    own, width = nodes.shape
    heads, queries, keys = pair_bias.shape
    kinds, gauss = gauss_mul.shape[0], gauss_mean.shape[0]
    atoms = own * rows * cols
    dims = (own, cols, width, heads, keys, kinds)
    bias_rows, mask_rows, first_rows, wide_table, second_rows = sizes(dims)
    near_step, still = (1, 1), (0, 0)
    along_col = paired(list(range(1, cols)))
    along_row = [(even, odd) for odd, even in paired(list(range(3, rows, 2)))]
    column_parts, row_parts = sources(along_col), sources(along_row)
    row_parts = [(even ^ (1 - other), odd ^ (1 - other), other) if n else (0, 0, 0) for n, (even, odd, other) in enumerate(row_parts)]
    shape = jax.ShapeDtypeStruct
    params = pltpu.CompilerParams(vmem_limit_bytes=(16 if atoms <= 128 else 56) * 2**20)
    vmem, anywhere = pl.BlockSpec(memory_space=pltpu.VMEM), pl.BlockSpec(memory_space=pl.ANY)

    def call(kernel, name, out_shape, inputs, remote=(), scratch=()):
        single = not isinstance(out_shape, list)
        return pl.pallas_call(
            kernel,
            out_shape=out_shape,
            in_specs=[vmem] * len(inputs) + [anywhere] * len(remote),
            out_specs=vmem if single else [vmem] * len(out_shape),
            scratch_shapes=list(scratch),
            compiler_params=params,
            name=name,
        )(*inputs, *map(in_hbm, remote))

    own_arrays = (
        nodes,
        coords,
        atom_types[None, :],
        segment_ids[None, :],
        ln_gain[None, :],
        pair_mask,
        pair_bias.transpose(1, 2, 0),
    )
    mine, kept = call(
        functools.partial(pack_kernel, dims),
        "pack",
        [
            shape((first_rows, lanes), bf16),
            shape((-(-(bias_rows + mask_rows) // 16) * 16, lanes), bf16),
        ],
        (),
        own_arrays,
        [pltpu.VMEM(x.shape, x.dtype) for x in own_arrays]
        + [pltpu.VMEM((cols, mask_rows, lanes), f32), pltpu.SemaphoreType.DMA((7,))],
    )
    other = exchange(mine, near_step, still)
    grouped = call(
        functools.partial(regroup_kernel, dims, along_col),
        "regroup",
        [shape((second_rows, lanes), bf16)] * len(along_col),
        (mine, other),
    )
    received = [exchange(x, near_step, shift) for x, shift in zip(grouped, along_col, strict=True)]
    small = (w_qkv, w_heads.T, coords)
    tables = (gauss_mul, gauss_add, gauss_mean[None, :], gauss_width[None, :], w_gauss, w_coord1)
    tables += (w_coord2[None, :],)
    prepared = call(
        functools.partial(prepare_kernel, dims),
        "prepare",
        [shape(x.shape, x.dtype) for x in small]
        + [
            shape((gauss, gauss), bf16),
            shape(w_coord1.shape, bf16),
            shape((heads, lanes), f32),
            shape((2 * own, lanes), f32),
            shape((24, lanes), f32),
            shape((3, gauss, lanes), f32),
        ],
        (lax.optimization_barrier((mine, grouped[0]))[0],),
        small + tables,
        [pltpu.VMEM(x.shape, x.dtype) for x in tables] + [pltpu.SemaphoreType.DMA((10,))],
    )
    received[0], prepared = lax.optimization_barrier((received[0], prepared))
    received += [exchange(x, near_step, still) for x in received[:-1]]
    w_qkv, w_heads, coords, w_gauss, w_coord1, w_coord2, lookup, own_columns, kernels = prepared
    near = call(
        functools.partial(gather_kernel, dims),
        "gather",
        shape((table_rows + 2 * node_rows(width, own) * cols, lanes), bf16),
        (mine, other, *received),
    )
    pieces = [near] + [exchange(near, step, still) for step in along_row]
    pieces += [exchange(x, near_step, still) for x in pieces[1 : len(along_row)]]
    bias, spread_queries = call(
        functools.partial(arrange_kernel, dims, column_parts, row_parts),
        "arrange",
        [
            shape((own * heads, atoms), bf16),
            shape((own * heads, width), bf16),
        ],
        (lax.optimization_barrier((mine, pieces[1]))[0], kept, *received, w_qkv),
    )
    attended, moved = call(
        functools.partial(attend_kernel, dims, len(pieces)),
        "attend",
        [shape((own, width), bf16), shape((3, own), f32)],
        (*pieces, bias, spread_queries, w_qkv, w_heads, coords)
        + (w_gauss, w_coord1, w_coord2, lookup, own_columns, kernels),
        (),
        [
            pltpu.VMEM((own * heads, atoms), f32),
            pltpu.VMEM((atoms, width), bf16),
            pltpu.VMEM((8, atoms), f32),
            pltpu.VMEM((8, atoms), f32),
        ],
    )
    return attended, moved


def solution(mesh):
    own, tile, whole = P(("row", "col")), P("row", "col"), P()
    in_specs = (
        P(("row", "col"), None),
        P(None, ("row", "col")),
        own,
        own,
        tile,
        P(None, "row", "col"),
    ) + (whole,) * 10
    out_specs = (P(("row", "col"), None), P(None, ("row", "col")))
    return jax.shard_map(shards, mesh=mesh, in_specs=in_specs, out_specs=out_specs, check_vma=False)
```

```python
import functools
import math

import jax
import jax.numpy as jnp
from jax import lax
from jax.experimental import pallas as pl
from jax.experimental.pallas import tpu as pltpu
from jax.sharding import PartitionSpec as P

ln_epsilon = 1e-05
masked_fill = -1000000000.0
masked_below = -100000000.0
root_shift = 0.01
lanes = 128
f32 = jnp.float32
bf16 = jnp.bfloat16
nt = (((1,), (1,)), ((), ()))
tn = (((0,), (0,)), ((), ()))


def split3(x):
    hi = x.astype(bf16).astype(f32)
    mid = (x - hi).astype(bf16).astype(f32)
    return hi, mid, x - hi - mid


def iota(shape, axis):
    return lax.broadcasted_iota(jnp.int32, shape, axis)


def column(row):
    n = row.shape[1]
    square = jnp.where(iota((n, n), 0) == iota((n, n), 1), jnp.broadcast_to(row, (n, n)), 0.0)
    return jnp.sum(square, axis=1, keepdims=True)


def gelu(x):
    inner = x * (0.7978845608028654 + 0.035677408136300125 * (x * x))
    return (0.5 * x) * (1.0 + jnp.tanh(inner))


table_rows, table_used = 16, 11


def node_rows(width, own):
    return width // lanes * own


def sizes(dims):
    own, cols, width, heads, keys, kinds = dims
    bias_rows, mask_rows = own * keys * heads // lanes, own * keys // lanes
    first = table_rows + node_rows(width, own) + (cols - 1) * (bias_rows + mask_rows)
    wide_table = -(-(table_used + 2 * mask_rows) // 16) * 16
    second = 2 * bias_rows + wide_table + 2 * node_rows(width, own)
    return bias_rows, mask_rows, -(-first // 16) * 16, wide_table, second


def paired(steps):
    return [(steps[n + 1], steps[n]) for n in range(0, len(steps) - 1, 2)] + [(steps[-1], steps[-1])]


def sources(transfers):
    direct = [(odd, even, 1) for even, odd in transfers]
    return [(0, 0, 0)] + direct + [(even, odd, 0) for even, odd in transfers[:-1]]


def in_hbm(x):
    return pltpu.with_memory_space_constraint(x, pltpu.HBM)


def fetch(sources, targets, semaphores):
    copies = [
        pltpu.make_async_copy(source, target, semaphores.at[n])
        for n, (source, target) in enumerate(zip(sources, targets, strict=True))
    ]
    for copy in copies:
        copy.start()
    return copies


def filled(blocks, rows):
    rest = rows - sum(block.shape[0] for block in blocks)
    return jnp.concatenate(blocks + ([jnp.zeros((rest, lanes), f32)] if rest else []), axis=0)


def normed(x, gain):
    features = x.astype(f32)
    centred = features - jnp.mean(features, axis=1, keepdims=True)
    spread = jnp.mean(centred * centred, axis=1, keepdims=True)
    return (centred * lax.rsqrt(spread + ln_epsilon) * gain).astype(bf16)


def pack_kernel(dims, *refs):
    own, cols, width, heads, keys, kinds = dims
    bias_rows, mask_rows, first_rows, wide_table, second_rows = sizes(dims)
    first, kept, held, masks, semaphores = refs[7], refs[8], refs[9:16], refs[16], refs[17]
    copies = fetch(refs[:7], held, semaphores)
    nodes, coords, types, segments, ln_gain, mask, bias = held
    me = lax.axis_index("col")
    pairs, fold = own * keys, lanes // heads
    for copy in copies[:5]:
        copy.wait()
    high, middle, low = split3(coords[...])
    kind = (types[...] + kinds // 2 * segments[...]).astype(f32)
    blank = jnp.zeros((1, own), f32)
    table = jnp.concatenate([high, kind, low, blank, middle] + [blank] * 5, axis=0)
    table = jnp.concatenate([table, jnp.zeros((table_rows, lanes - own), f32)], axis=1)
    full = normed(nodes[...], ln_gain[...]).astype(f32)
    blocks = [table] + [full[:, b * lanes : (b + 1) * lanes] for b in range(width // lanes)]
    copies[5].wait()
    wide_mask = mask[...].astype(f32)
    for d in range(cols):
        row = jnp.concatenate([wide_mask[d * own + i : d * own + i + 1] for i in range(own)], axis=1)
        for n in range(mask_rows):
            masks[d, n : n + 1, :] = row[:, n * lanes : (n + 1) * lanes]
    start = (cols - 1) * bias_rows
    tail = filled(blocks + [masks[(me + k) % cols] for k in range(1, cols)], first_rows - start)
    first[start:, :] = tail.astype(bf16)
    kept[bias_rows:, :] = filled([masks[me]], kept.shape[0] - bias_rows).astype(bf16)
    copies[6].wait()
    for k in range(cols):
        tile = bias[pl.ds((me + k) % cols * own, own)].astype(f32).reshape(pairs, heads)
        wide = [tile[n * bias_rows : (n + 1) * bias_rows] for n in range(fold)]
        block = jnp.concatenate(wide, axis=1).astype(bf16)
        if k:
            first[(k - 1) * bias_rows : k * bias_rows, :] = block
        else:
            kept[:bias_rows, :] = block


def regroup_kernel(dims, transfers, mine, other, *outs):
    own, cols, width, heads, keys, kinds = dims
    bias_rows, mask_rows, first_rows, wide_table, second_rows = sizes(dims)
    odd = lax.axis_index("row") % 2 == 1
    start, rows = (cols - 1) * bias_rows, table_rows + node_rows(width, own)
    here, there = mine[start:, :].astype(f32), other[start:, :].astype(f32)
    table = (here[:table_rows] + pltpu.roll(there[:table_rows], own, 1))[:table_used]
    nodes = [here[table_rows:rows], there[table_rows:rows]]
    for out, (for_even, for_odd) in zip(outs, transfers, strict=True):

        def chosen(x, first, count):
            even_block = x[first + (for_even - 1) * count : first + for_even * count]
            if for_even == for_odd:
                return even_block
            return jnp.where(odd, x[first + (for_odd - 1) * count : first + for_odd * count], even_block)

        for n, ref in enumerate((mine, other)):
            out[n * bias_rows : (n + 1) * bias_rows, :] = chosen(ref, 0, bias_rows)
        masks = [chosen(x, rows, mask_rows) for x in (here, there)]
        tail = filled([table] + masks, wide_table)
        out[2 * bias_rows :, :] = jnp.concatenate([tail] + nodes, axis=0).astype(bf16)


def gather_kernel(dims, mine, other, *refs):
    own, cols, width, heads, keys, kinds = dims
    bias_rows, mask_rows, first_rows, wide_table, second_rows = sizes(dims)
    start, rows = (cols - 1) * bias_rows, node_rows(width, own)
    out = refs[cols - 1]
    here, there = mine[start:, :].astype(f32), other[start:, :].astype(f32)
    tails = [ref[2 * bias_rows :, :].astype(f32) for ref in refs[: cols - 1]]
    table = here[:table_rows] + pltpu.roll(there[:table_rows], own, 1)
    for k, tail in enumerate(tails, 1):
        part = jnp.where(iota((table_rows, lanes), 0) < table_used, tail[:table_rows], 0.0)
        table = table + pltpu.roll(part, 2 * own * k, 1)
    out[:table_rows, :] = table.astype(bf16)
    blocks = [here[table_rows:], there[table_rows:]]
    for tail in tails:
        blocks += [tail[wide_table : wide_table + rows], tail[wide_table + rows :]]
    each = 2 * own * cols
    for b in range(width // lanes):
        taken = jnp.concatenate([block[b * own : (b + 1) * own] for block in blocks], axis=0)
        out[table_rows + b * each : table_rows + (b + 1) * each, :] = taken.astype(bf16)


def arrange_kernel(dims, column_parts, row_parts, mine, kept, *refs):
    own, cols, width, heads, keys, kinds = dims
    bias_rows, mask_rows, first_rows, wide_table, second_rows = sizes(dims)
    received = refs[: cols - 1]
    w_qkv, out, spread_queries = refs[cols - 1 :]
    atoms = out.shape[1]
    fold = lanes // heads
    each = own // fold
    per_row = 2 * own * cols
    r, c = lax.axis_index("row"), lax.axis_index("col")

    def by_core(odd, part):
        return jnp.where(odd, part[1], part[0])

    blocks, masks = [], []
    for b in range(each):
        rows = [kept[b * keys : (b + 1) * keys, :]]
        for ref, part in zip(received, column_parts[1:], strict=True):
            first = part[2] * bias_rows + b * keys
            rows.append(ref[first : first + keys, :])
        blocks.append(jnp.concatenate(rows, axis=0))
    tails = [kept[bias_rows:, :].astype(f32)[:mask_rows]]
    for ref, part in zip(received, column_parts[1:], strict=True):
        first = table_used + part[2] * mask_rows
        tails.append(ref[2 * bias_rows : 2 * bias_rows + wide_table, :].astype(f32)[first : first + mask_rows])
    for i in range(own):
        n, lane = i * keys // lanes, i * keys % lanes
        masks.append(jnp.concatenate([tail[n : n + 1, lane : lane + keys] for tail in tails], axis=1))
    masks = jnp.concatenate(masks + [jnp.zeros((16 - own, atoms), f32)], axis=0).astype(bf16)
    place = iota((atoms, 1), 0)
    step = jnp.zeros((atoms, 1), jnp.int32)
    for n, part in enumerate(column_parts):
        step = jnp.where(place // keys == n, by_core(r % 2 == 1, part), step)
    atom = (c + cols - step) % cols * keys + place % keys
    for s in range(0, atoms, lanes):
        slot = s + iota((1, lanes), 1)
        piece, inner = slot // per_row, slot % per_row
        row = jnp.zeros((1, lanes), jnp.int32) + r
        for n, part in enumerate(row_parts):
            row = jnp.where(piece == n, r ^ by_core(r % 2 == 1, part), row)
        step, flip = jnp.zeros((1, lanes), jnp.int32), jnp.zeros((1, lanes), jnp.int32)
        for n, part in enumerate(column_parts):
            here = inner // (2 * own) == n
            step = jnp.where(here, by_core(row % 2 == 1, part), step)
            flip = jnp.where(here, part[2], flip)
        row = row ^ flip ^ (inner // own % 2)
        source = (row * cols + (c + cols - step) % cols) * own + inner % own
        chosen = (atom == source).astype(f32).astype(bf16)
        valid = jnp.dot(masks, chosen, preferred_element_type=f32)
        for b in range(each):
            moved = lax.dot_general(blocks[b], chosen, tn, preferred_element_type=f32)
            for a in range(fold):
                i = a * each + b
                taken = jnp.where(valid[i : i + 1] > 0.5, moved[a * heads : (a + 1) * heads], masked_fill)
                out[i * heads : (i + 1) * heads, s : s + lanes] = taken.astype(bf16)
    rows = mine[(cols - 1) * bias_rows :, :].astype(f32)[table_rows : table_rows + node_rows(width, own)]
    x = jnp.concatenate([rows[b * own : (b + 1) * own] for b in range(width // lanes)], axis=1)
    x = jnp.concatenate([x, jnp.zeros((16 - own, width), f32)], axis=0).astype(bf16)
    queries = jnp.dot(x, w_qkv[:, :width], preferred_element_type=f32)
    head_mask = iota((heads, width), 1) // (width // heads) == iota((heads, width), 0)
    for i in range(own):
        spread = jnp.where(head_mask, jnp.broadcast_to(queries[i : i + 1], (heads, width)), 0.0)
        spread_queries[i * heads : (i + 1) * heads, :] = spread.astype(bf16)


def prepare_kernel(dims, mine, *refs):
    own, cols, width, heads, keys, kinds = dims
    bias_rows, mask_rows, first_rows, wide_table, second_rows = sizes(dims)
    w_qkv, w_heads, coords, w_gauss, w_coord1, w_coord2 = refs[10:16]
    lookup, own_columns, kernels = refs[16:19]
    mul_held, add_held, mean_held, width_held, gauss_held, coord1_held, coord2_held = refs[19:26]
    copies = fetch(
        refs[:10],
        (w_qkv, w_heads, coords, mul_held, add_held, mean_held, width_held)
        + (gauss_held, coord1_held, coord2_held),
        refs[26],
    )
    table = mine[(cols - 1) * bias_rows :, :].astype(f32)[:table_rows]
    places = (table[0:3] + table[8:11]) + table[4:7]
    for c in range(3):
        own_columns[c * 8 : c * 8 + own, :] = jnp.broadcast_to(
            column(places[c : c + 1, :own]), (own, lanes)
        )
    own_kind = column(table[3:4, :own]).astype(jnp.int32)
    own_kind = jnp.concatenate([own_kind, jnp.zeros((16 - own, 1), jnp.int32)], axis=0)
    query_onehot = (own_kind == iota((16, kinds), 1)).astype(f32).astype(bf16)
    for copy in copies:
        copy.wait()
    inverse = 1.0 / column(width_held[...])
    gauss = inverse.shape[0]
    kernels[0] = jnp.broadcast_to(column(mean_held[...]), (gauss, lanes))
    kernels[1] = jnp.broadcast_to(inverse * math.sqrt(0.5 * math.log2(math.e)), (gauss, lanes))
    kernels[2] = jnp.broadcast_to(jnp.log2(inverse * (1.0 / math.sqrt(2.0 * math.pi))), (gauss, lanes))
    found = []
    for table in (mul_held, add_held):
        parts = [
            jnp.dot(query_onehot, part.astype(bf16), preferred_element_type=f32)
            for part in split3(table[...])
        ]
        found.append((parts[0] + parts[1] + parts[2])[:own])
    found = jnp.concatenate(found, axis=0)
    lookup[...] = jnp.concatenate([found, jnp.zeros((2 * own, lanes - kinds), f32)], axis=1)
    w_gauss[...] = gauss_held[...].astype(f32).T.astype(bf16)
    w_coord1[...] = coord1_held[...].astype(f32).T.astype(bf16)
    w_coord2[...] = jnp.broadcast_to(column(coord2_held[...].astype(f32)), (heads, lanes))


def attend_kernel(dims, count, *refs):
    own, cols, width, heads, keys, kinds = dims
    pieces = refs[:count]
    bias, spread_queries, w_qkv, w_heads, coords = refs[count : count + 5]
    w_gauss, w_coord1, w_coord2, lookup, own_columns, kernels = refs[count + 5 : count + 11]
    attended, moved, logits, values, places, strengths = refs[count + 11 :]
    atoms = bias.shape[1]
    each = 2 * own * cols
    centre, sharp, norming = kernels[0], kernels[1], kernels[2]
    found = lookup[...]

    for s in range(0, atoms, lanes):
        taken = pieces[s // each : (s + lanes) // each]
        x = [
            jnp.concatenate(
                [
                    ref[table_rows + b * each : table_rows + (b + 1) * each, :]
                    for b in range(width // lanes)
                ],
                axis=1,
            )
            for ref in taken
        ]
        block = jnp.concatenate(x, axis=0)
        table = jnp.concatenate([ref[:table_rows, :].astype(f32)[:, :each] for ref in taken], axis=1)
        place = (table[0:3] + table[8:11]) + table[4:7]
        places[0:3, s : s + lanes] = place
        offsets = [own_columns[c * 8 : c * 8 + own, :] - place[c : c + 1] for c in range(3)]
        squares = offsets[0] * offsets[0] + offsets[1] * offsets[1] + offsets[2] * offsets[2]
        distance = jnp.sqrt(squares + root_shift)
        kind = jnp.broadcast_to(table[3:4].astype(jnp.int32), (2 * own, lanes))
        pair = jnp.take_along_axis(found, kind, axis=1)
        expanded = pair[:own] * distance + pair[own:]
        features = []
        for i in range(own):
            scaled = (expanded[i : i + 1] - centre) * sharp
            features.append(jnp.exp2(norming - scaled * scaled).astype(bf16))
        keys_here = jnp.dot(block, w_qkv[:, width : 2 * width], preferred_element_type=f32)
        values[s : s + lanes, :] = jnp.dot(
            block, w_qkv[:, 2 * width :], preferred_element_type=f32
        ).astype(bf16)
        affinity = lax.dot_general(
            spread_queries[...], keys_here.astype(bf16), nt, preferred_element_type=f32
        )
        hidden = jnp.dot(w_gauss[...], jnp.concatenate(features, axis=1), preferred_element_type=f32)
        geometry = jnp.dot(w_heads[...], gelu(hidden).astype(bf16), preferred_element_type=f32)
        here = bias[:, s : s + lanes].astype(f32)
        rows = []
        for i in range(own):
            at = slice(i * heads, (i + 1) * heads)
            row = here[at] + affinity[at] * (1.0 / math.sqrt(width // heads))
            row = row + geometry[:, i * lanes : (i + 1) * lanes]
            logits[at, s : s + lanes] = jnp.where(here[at] < masked_below, masked_fill, row)
            rows.append(row.astype(bf16))
        mixed = jnp.dot(w_coord1[...], jnp.concatenate(rows, axis=1), preferred_element_type=f32)
        mixed = gelu(mixed)
        for i in range(own):
            strength = jnp.sum(
                mixed[:, i * lanes : (i + 1) * lanes] * w_coord2[...], axis=0, keepdims=True
            )
            masked = here[i * heads : i * heads + 1] < masked_below
            strengths[i : i + 1, s : s + lanes] = jnp.where(masked, 0.0, strength)

    masked = logits[...]
    weights = jnp.exp(masked - jnp.max(masked, axis=1, keepdims=True))
    share = 1.0 / jnp.sum(weights, axis=1, keepdims=True)
    taken = jnp.dot(weights.astype(bf16), values[...], preferred_element_type=f32) * share
    head_mask = iota((heads, width), 1) // (width // heads) == iota((heads, width), 0)
    attended[...] = jnp.concatenate(
        [
            jnp.sum(
                jnp.where(head_mask, taken[i * heads : (i + 1) * heads], 0.0), axis=0, keepdims=True
            )
            for i in range(own)
        ],
        axis=0,
    ).astype(bf16)
    here = coords[...]
    shift = jnp.zeros((3, own), f32)
    for i in range(own):
        pulls = (here[:, i : i + 1] - places[0:3, :]) * strengths[i : i + 1, :]
        shift = jnp.where(iota((3, own), 1) == i, jnp.sum(pulls, axis=1, keepdims=True), shift)
    moved[...] = here + shift * (1.0 / atoms)


def exchange(x, steps, distances):
    rows, cols = lax.axis_size("row"), lax.axis_size("col")
    pairs = [
        (r * cols + c, (r ^ steps[r % 2]) * cols + (c + distances[r % 2]) % cols)
        for r in range(rows)
        for c in range(cols)
    ]
    return lax.ppermute(x, ("row", "col"), pairs)


def shards(
    nodes,
    coords,
    atom_types,
    segment_ids,
    pair_mask,
    pair_bias,
    ln_gain,
    w_qkv,
    gauss_mul,
    gauss_add,
    gauss_mean,
    gauss_width,
    w_gauss,
    w_heads,
    w_coord1,
    w_coord2,
):
    cols, rows = lax.axis_size("col"), lax.axis_size("row")
    own, width = nodes.shape
    heads, queries, keys = pair_bias.shape
    kinds, gauss = gauss_mul.shape[0], gauss_mean.shape[0]
    atoms = own * rows * cols
    dims = (own, cols, width, heads, keys, kinds)
    bias_rows, mask_rows, first_rows, wide_table, second_rows = sizes(dims)
    near_step, still = (1, 1), (0, 0)
    along_col = paired(list(range(1, cols)))
    along_row = [(even, odd) for odd, even in paired(list(range(3, rows, 2)))]
    column_parts, row_parts = sources(along_col), sources(along_row)
    row_parts = [(even ^ (1 - other), odd ^ (1 - other), other) if n else (0, 0, 0) for n, (even, odd, other) in enumerate(row_parts)]
    shape = jax.ShapeDtypeStruct
    params = pltpu.CompilerParams(vmem_limit_bytes=(16 if atoms <= 128 else 56) * 2**20)
    vmem, anywhere = pl.BlockSpec(memory_space=pltpu.VMEM), pl.BlockSpec(memory_space=pl.ANY)

    def call(kernel, name, out_shape, inputs, remote=(), scratch=()):
        single = not isinstance(out_shape, list)
        return pl.pallas_call(
            kernel,
            out_shape=out_shape,
            in_specs=[vmem] * len(inputs) + [anywhere] * len(remote),
            out_specs=vmem if single else [vmem] * len(out_shape),
            scratch_shapes=list(scratch),
            compiler_params=params,
            name=name,
        )(*inputs, *map(in_hbm, remote))

    own_arrays = (
        nodes,
        coords,
        atom_types[None, :],
        segment_ids[None, :],
        ln_gain[None, :],
        pair_mask,
        pair_bias.transpose(1, 2, 0),
    )
    mine, kept = call(
        functools.partial(pack_kernel, dims),
        "pack",
        [
            shape((first_rows, lanes), bf16),
            shape((-(-(bias_rows + mask_rows) // 16) * 16, lanes), bf16),
        ],
        (),
        own_arrays,
        [pltpu.VMEM(x.shape, x.dtype) for x in own_arrays]
        + [pltpu.VMEM((cols, mask_rows, lanes), f32), pltpu.SemaphoreType.DMA((7,))],
    )
    other = exchange(mine, near_step, still)
    grouped = call(
        functools.partial(regroup_kernel, dims, along_col),
        "regroup",
        [shape((second_rows, lanes), bf16)] * len(along_col),
        (mine, other),
    )
    received = [exchange(x, near_step, shift) for x, shift in zip(grouped, along_col, strict=True)]
    received += [exchange(x, near_step, still) for x in received[:-1]]
    near = call(
        functools.partial(gather_kernel, dims),
        "gather",
        shape((table_rows + 2 * node_rows(width, own) * cols, lanes), bf16),
        (mine, other, *received),
    )
    pieces = [near] + [exchange(near, step, still) for step in along_row]
    pieces += [exchange(x, near_step, still) for x in pieces[1 : len(along_row)]]
    small = (w_qkv, w_heads.T, coords)
    tables = (gauss_mul, gauss_add, gauss_mean[None, :], gauss_width[None, :], w_gauss, w_coord1)
    tables += (w_coord2[None, :],)
    prepared = call(
        functools.partial(prepare_kernel, dims),
        "prepare",
        [shape(x.shape, x.dtype) for x in small]
        + [
            shape((gauss, gauss), bf16),
            shape(w_coord1.shape, bf16),
            shape((heads, lanes), f32),
            shape((2 * own, lanes), f32),
            shape((24, lanes), f32),
            shape((3, gauss, lanes), f32),
        ],
        (lax.optimization_barrier((mine, pieces[1]))[0],),
        small + tables,
        [pltpu.VMEM(x.shape, x.dtype) for x in tables] + [pltpu.SemaphoreType.DMA((10,))],
    )
    w_qkv, w_heads, coords, w_gauss, w_coord1, w_coord2, lookup, own_columns, kernels = prepared
    bias, spread_queries = call(
        functools.partial(arrange_kernel, dims, column_parts, row_parts),
        "arrange",
        [
            shape((own * heads, atoms), bf16),
            shape((own * heads, width), bf16),
        ],
        (lax.optimization_barrier((mine, pieces[1]))[0], kept, *received, w_qkv),
    )
    attended, moved = call(
        functools.partial(attend_kernel, dims, len(pieces)),
        "attend",
        [shape((own, width), bf16), shape((3, own), f32)],
        (*pieces, bias, spread_queries, w_qkv, w_heads, coords)
        + (w_gauss, w_coord1, w_coord2, lookup, own_columns, kernels),
        (),
        [
            pltpu.VMEM((own * heads, atoms), f32),
            pltpu.VMEM((atoms, width), bf16),
            pltpu.VMEM((8, atoms), f32),
            pltpu.VMEM((8, atoms), f32),
        ],
    )
    return attended, moved


def solution(mesh):
    own, tile, whole = P(("row", "col")), P("row", "col"), P()
    in_specs = (
        P(("row", "col"), None),
        P(None, ("row", "col")),
        own,
        own,
        tile,
        P(None, "row", "col"),
    ) + (whole,) * 10
    out_specs = (P(("row", "col"), None), P(None, ("row", "col")))
    return jax.shard_map(shards, mesh=mesh, in_specs=in_specs, out_specs=out_specs, check_vma=False)
```
